512 devices in a mesh: ctx: 64 (over z, x_hi, core), tp: 8 (over y, x_lo).
Axes of the slice: x: 4 (x_hi: 2, x_lo: 2; x = x_hi * 2 + x_lo), y: 4, z: 16, core: 2. Of those that a mesh axis runs over, the one named last changes fastest.
Arguments:
- qkv_in: bfloat16 [8192, 3, 4096], P('ctx', None, 'tp'), may hold values from -6 to 6
- short_taps: float32 [3, 3, 4096], P(None, None, 'tp'), may hold values from -3.5 to 3.5
- long_filter: float32 [8192, 4096], P('ctx', 'tp'), may hold values from -1.7 to 1.7
- skip_gain: float32 [4096], P('tp'), may hold values from 0.2 to 1.5
- out_weight: bfloat16 [4096, 4096], P('tp', 'ctx'), may hold values from -0.25 to 0.25
Outputs:
- mixed_out: bfloat16 [8192, 4096], P('ctx', 'tp')
The draws below stay inside these ranges and needn't reach their ends.
All inputs are finite; a program needn't handle non-finite values.
Results may differ from the reference program's by a relative error of at most 0.0049.
Values may be sent and summed in bfloat16 or wider, within the bound.
A program may use at most 64 MiB of HBM per device.

```python
import math
import jax
import jax.numpy as jnp
from jax import lax

D = 4096
SHORT_TAPS = 3
TOKENS = 8192


def draw_long_filter(key, part):
    key = jax.random.fold_in(key, 7)
    rate_key, tap_key = jax.random.split(key)
    positions = lax.iota(jnp.float32, TOKENS)[:, None]
    tap_noise = jnp.clip(jax.random.normal(tap_key, (TOKENS, D), jnp.float32), -6.0, 6.0)
    log_decay = jax.random.uniform(rate_key, (1, D), jnp.float32, math.log(30.0), math.log(2.0 * TOKENS))
    decay_len = jnp.exp(log_decay)
    return jnp.sqrt(2.0 / decay_len) * tap_noise * jnp.exp(-positions / decay_len)


def spiked(values, rng, source, target, parts, factor):
    owner, partner = [(jnp.arange(values.shape[axis_at]) // (values.shape[axis_at] // parts)).reshape([-1 if axis == axis_at else 1 for axis in range(values.ndim)]) for axis_at in (source, target)]
    chosen = jax.random.permutation(rng, parts)[partner]
    strong = (owner == chosen) | (owner == (partner + parts // 2) % parts)
    return jnp.where(strong, factor * values, values)


def level_of(rng, dims, cuts, smallest, largest):
    loudness, own = 1.0, jax.random.fold_in(rng, 6)
    for position, parts in cuts:
        draws = jnp.exp(jax.random.uniform(jax.random.fold_in(own, position), (parts,), jnp.float32, smallest / len(cuts), largest / len(cuts)))
        loudness = loudness * jnp.repeat(draws, dims[position] // parts).reshape([-1 if axis == position else 1 for axis in range(len(dims))])
    return loudness


def noise(rng, dims, scale, limit, cuts=(), held_as=jnp.bfloat16):
    array = jax.random.normal(rng, dims, jnp.float32) * scale
    if len(cuts) > 0:
        array = level_of(rng, dims, cuts, -0.22, 0.18) * array
    return jnp.clip(array, min=-limit, max=limit).astype(held_as)


def gaussian_with(key, extent, spread, bound, shards, heavy, dtype=jnp.bfloat16):
    values = spread * jax.random.normal(key, extent, jnp.float32)
    if shards:
        values = values * level_of(key, extent, shards, -0.22, 0.18)
    return jnp.clip(spiked(values, jax.random.fold_in(key, 3), *heavy), -bound, bound).astype(dtype)


def setup_inputs(seed: int = 0) -> dict:
    arg_keys = jax.random.split(jax.random.key(seed), 6)
    return {
        "qkv_in": noise(arg_keys[0], (TOKENS, 3, D), 1.0, 6.0, ((0, 64), (2, 8))),
        "short_taps": noise(arg_keys[1], (3, SHORT_TAPS, D), SHORT_TAPS ** -0.5, 3.5, ((2, 8),), jnp.float32),
        "long_filter": draw_long_filter(jax.random.fold_in(arg_keys[5], 71), 0),
        "skip_gain": jnp.clip(0.2 + 1.3 * jax.random.uniform(arg_keys[3], (D,), jnp.float32) ** level_of(arg_keys[3], (D,), ((0, 8),), -0.2, 0.2), 0.2, 1.5),
        "out_weight": gaussian_with(arg_keys[4], (D, D), D ** -0.5, 0.25, ((0, 8), (1, 64)), (0, 1, 64, 4.0)),
    }


def featurize(inputs, taps_one):
    tap_count = taps_one.shape[0]
    length = inputs.shape[0]
    padded = jnp.pad(inputs, ((tap_count - 1, 0), (0, 0)))
    result = jnp.zeros_like(inputs)
    for index_tap in range(tap_count):
        begin = tap_count - 1 - index_tap
        result = result + taps_one[index_tap][None, :] * padded[begin:begin + length]
    return result


def reference(qkv_in, short_taps, long_filter, skip_gain, out_weight):
    queries = featurize(qkv_in[:, 0, :].astype(jnp.float32), short_taps[0])
    keys_feat = featurize(qkv_in[:, 1, :].astype(jnp.float32), short_taps[1])
    values_feat = featurize(qkv_in[:, 2, :].astype(jnp.float32), short_taps[2])
    mixed_in = keys_feat * values_feat
    total_len = 2 * TOKENS
    spectrum = jnp.fft.rfft(mixed_in, n=total_len, axis=0) * jnp.fft.rfft(long_filter, n=total_len, axis=0)
    convolved = jnp.fft.irfft(spectrum, n=total_len, axis=0)[:TOKENS]
    gated_rows = (queries * (convolved + skip_gain[None, :] * mixed_in)).astype(jnp.bfloat16)
    return jnp.dot(gated_rows, out_weight, preferred_element_type=jnp.float32).astype(jnp.bfloat16)
```

```python
import functools

import jax
import jax.numpy as jnp
import numpy as np
from jax import lax
from jax.experimental import pallas as pl
from jax.experimental.pallas import tpu as pltpu
from jax.sharding import Mesh, PartitionSpec as P

F32 = jnp.float32
BF16 = jnp.bfloat16
CH = 8
VMEM = pl.BlockSpec(memory_space=pltpu.VMEM)


def split_hi_lo(table):
    high = table.astype(np.float32).astype(jnp.bfloat16)
    low = (table - high.astype(np.float64)).astype(np.float32).astype(jnp.bfloat16)
    return high, low


def tables(blocks, width):
    length = blocks * width
    f1 = np.arange(blocks)[:, None]
    a = np.exp(-2j * np.pi * ((np.arange(blocks)[None, :] * (4 * f1 + 1)) % (4 * blocks)) / (4 * blocks))
    t = np.exp(-2j * np.pi * (np.arange(width)[None, :] * (4 * f1 + 1)) / (4 * length))
    i = np.arange(width)
    b = np.exp(-2j * np.pi * ((i[:, None] * i[None, :]) % width) / width)
    a_high, a_low = split_hi_lo(np.concatenate([a.real, a.imag], 0))
    b_high, b_low = split_hi_lo(np.block([[b.real, b.imag], [-b.imag, b.real]]))
    c_high, c_low = split_hi_lo(np.block([[b.real, -b.imag], [b.imag, b.real]]))
    d_high, d_low = split_hi_lo(np.concatenate([a.real.T, a.imag.T], 1) / length)
    return (
        np.concatenate([a_high, a_low], 1),
        t.real.astype(np.float32),
        t.imag.astype(np.float32),
        np.concatenate([b_high, b_high, b_low], 0),
        np.concatenate([c_high, c_high, c_low], 0),
        np.concatenate([d_high, d_high, d_low], 1),
    )


def dot(left, right):
    return jnp.dot(left, right, preferred_element_type=F32)


def high_low(value):
    high = value.astype(BF16)
    return high, (value - high.astype(F32)).astype(BF16)


def send_all(chips, me, source, target, send_sem, recv_sem):
    def step(k, carry):
        peer = lax.rem(me + k, chips)
        pltpu.make_async_remote_copy(
            src_ref=source.at[peer],
            dst_ref=target.at[me],
            send_sem=send_sem,
            recv_sem=recv_sem,
            device_id={"z": peer // 2, "xh": lax.rem(peer, 2)},
        ).start()
        return carry

    lax.fori_loop(1, chips, step, 0)
    target[pl.ds(me, 1)] = source[pl.ds(me, 1)]


def wait_all(chips, ref, sem):
    part = ref.at[pl.ds(0, chips - 1)]
    pltpu.make_async_copy(part, part, sem).wait()


def spectrum(received, scratch, a_fwd, t_re, t_im, b_fwd):
    rows = scratch.shape[0]
    blocks = rows // CH
    scratch[...] = received[...].astype(F32).reshape(rows, -1)
    columns = [scratch[pl.ds(c, blocks, stride=CH), :].astype(BF16) for c in range(CH)]
    signal = jnp.concatenate(columns, axis=1)
    mixed = dot(a_fwd[...], jnp.concatenate([signal, signal], axis=0))
    width = t_re.shape[1]
    parts = []
    for c in range(CH):
        re = mixed[:blocks, c * width : (c + 1) * width]
        im = mixed[blocks:, c * width : (c + 1) * width]
        parts.append(
            jnp.concatenate(
                [re * t_re[...] - im * t_im[...], re * t_im[...] + im * t_re[...]], axis=1
            )
        )
    high, low = high_low(jnp.concatenate(parts, axis=0))
    return dot(jnp.concatenate([high, low, high], axis=1), b_fwd[...])


def inverse(product, scratch, t_re, t_im, b_inv, a_inv):
    blocks, width = t_re.shape
    high, low = high_low(product)
    back = dot(jnp.concatenate([high, low, high], axis=1), b_inv[...])
    parts = []
    for c in range(CH):
        re = back[c * blocks : (c + 1) * blocks, :width]
        im = back[c * blocks : (c + 1) * blocks, width:]
        parts.append(
            jnp.concatenate(
                [re * t_re[...] + im * t_im[...], im * t_re[...] - re * t_im[...]], axis=0
            )
        )
    high, low = high_low(jnp.concatenate(parts, axis=1))
    result = dot(a_inv[...], jnp.concatenate([high, low, high], axis=0))
    for c in range(CH):
        scratch[pl.ds(c, blocks, stride=CH), :] = result[:, c * width : (c + 1) * width]


def conv_kernel(
    chips,
    qkv, taps, filt, skip, a_fwd, t_re, t_im, b_fwd, b_inv, a_inv,
    gated,
    h_own, h_pair, h_send, h_recv, x_all, u_send, u_recv, y_send, y_recv, scratch,
    near_send, near_recv, far_send, far_recv, local_sem,
):
    core = lax.axis_index("core")
    me = lax.axis_index("z") * 2 + lax.axis_index("xh")
    other = 1 - core
    rows = qkv.shape[1]
    half = chips * CH
    halo = 16

    barrier = pltpu.get_barrier_semaphore()
    pl.semaphore_signal(barrier, inc=1, device_id={"core": other})
    step_to = lax.rem(me + jnp.where(core == 1, 1, chips - 1), chips)
    pl.semaphore_signal(
        barrier, inc=1, device_id={"z": step_to // 2, "xh": lax.rem(step_to, 2), "core": other}
    )

    def greet(k, carry):
        peer = lax.rem(me + k, chips)
        pl.semaphore_signal(
            barrier, inc=1, device_id={"z": peer // 2, "xh": lax.rem(peer, 2)}
        )
        return carry

    lax.fori_loop(1, chips, greet, 0)

    turned = filt[...].T.reshape(2, chips, CH, rows)
    h_own[...] = turned
    pl.semaphore_wait(barrier, chips + 1)

    my_rows = pl.ds(pl.multiple_of(core * CH, CH), CH)
    h_copy = pltpu.make_async_remote_copy(
        src_ref=h_own.at[other],
        dst_ref=h_pair.at[:, my_rows, :],
        send_sem=near_send.at[0],
        recv_sem=near_recv.at[0],
        device_id={"core": other},
    )
    h_copy.start()
    mine = pl.ds(pl.multiple_of(core * half, half), half)
    theirs = pl.ds(pl.multiple_of(other * half, half), half)
    place = pl.ds(pl.multiple_of(halo + core * rows, 16), rows)
    x_copy = pltpu.make_async_remote_copy(
        src_ref=qkv.at[:, :, theirs],
        dst_ref=x_all.at[:, place, :],
        send_sem=near_send.at[1],
        recv_sem=near_recv.at[1],
        device_id={"core": other},
    )
    x_copy.start()

    after = lax.rem(me + 1, chips)

    def halo_copy(target):
        return pltpu.make_async_remote_copy(
            src_ref=qkv.at[:, pl.ds(rows - halo, halo), pl.ds(target * half, half)],
            dst_ref=x_all.at[:, pl.ds(0, halo), :],
            send_sem=near_send.at[2 + target],
            recv_sem=near_recv.at[2],
            device_id={"z": after // 2, "xh": lax.rem(after, 2), "core": target},
        )

    @pl.when(core == 1)
    def _():
        halo_copy(0).start()
        halo_copy(1).start()

    x_local = pltpu.make_async_copy(qkv.at[:, :, mine], x_all.at[:, place, :], local_sem)
    x_local.start()
    h_pair[:, my_rows, :] = h_own[pl.ds(core, 1)].reshape(chips, CH, rows)
    h_copy.wait_recv()
    h_send[...] = h_pair[...].astype(BF16)
    send_all(chips, me, h_send, h_recv, far_send.at[0], far_recv.at[0])

    x_local.wait()
    x_copy.wait_recv()
    halo_copy(0).wait_recv()

    @pl.when(core == 1)
    def _():
        halo_copy(0).wait_send()
        halo_copy(1).wait_send()

    features = []
    for s in range(3):
        x = x_all[s].astype(F32)
        first = jnp.where(me == 0, 0.0, x[:halo])
        x = jnp.concatenate([first, x[halo:]], axis=0)
        total = taps[s, 0:1, mine] * x[halo:]
        for back in range(1, taps.shape[1]):
            total = total + taps[s, back : back + 1, mine] * x[halo - back : halo - back + 2 * rows]
        features.append(total)
    query, mixed_in = features[0], features[1] * features[2]
    flipped = mixed_in.T.reshape(chips, CH, 2 * rows)
    u_send[...] = jnp.concatenate([flipped[:, :, :rows], flipped[:, :, rows:]], axis=1).astype(BF16)
    send_all(chips, me, u_send, u_recv, far_send.at[1], far_recv.at[1])

    wait_all(chips, h_recv, far_recv.at[0])
    h_freq = spectrum(h_recv, scratch, a_fwd, t_re, t_im, b_fwd)
    wait_all(chips, u_recv, far_recv.at[1])
    u_freq = spectrum(u_recv, scratch, a_fwd, t_re, t_im, b_fwd)
    width = t_re.shape[1]
    h_re, h_im = h_freq[:, :width], h_freq[:, width:]
    u_re, u_im = u_freq[:, :width], u_freq[:, width:]
    product = jnp.concatenate([h_re * u_re - h_im * u_im, h_re * u_im + h_im * u_re], axis=1)
    inverse(product, scratch, t_re, t_im, b_inv, a_inv)
    y_send[...] = scratch[...].reshape(y_send.shape).astype(BF16)
    send_all(chips, me, y_send, y_recv, far_send.at[2], far_recv.at[2])
    wait_all(chips, y_recv, far_recv.at[2])
    back = y_recv[...].astype(F32)
    convolved = jnp.concatenate(
        [back[:, CH * b : CH * (b + 1), :].reshape(half, rows).T for b in range(2)], axis=0
    )
    gated[...] = (query * (convolved + skip[:, mine] * mixed_in)).astype(BF16)

    h_copy.wait_send()
    x_copy.wait_send()
    wait_all(chips, h_send, far_send.at[0])
    wait_all(chips, u_send, far_send.at[1])
    wait_all(chips, y_send, far_send.at[2])


def project_kernel(
    groups, gated, weight, out, g_all, parts, landed, near_send, near_recv, far_send, far_recv
):
    core, xh = lax.axis_index("core"), lax.axis_index("xh")
    xls = lax.axis_size("xl")
    me = lax.axis_index("y") * xls + lax.axis_index("xl")
    tokens, half = gated.shape
    rows = tokens // 2
    slot = xh * 2 + core

    barrier = pltpu.get_barrier_semaphore()

    def place(index):
        which, owner = index // groups, lax.rem(index, groups)
        return {
            "xh": which // 2,
            "core": lax.rem(which, 2),
            "y": owner // xls,
            "xl": lax.rem(owner, xls),
        }

    everyone = 4 * groups
    my_index = slot * groups + me

    def greet(k, carry):
        pl.semaphore_signal(barrier, inc=1, device_id=place(lax.rem(my_index + k, everyone)))
        return carry

    lax.fori_loop(1, everyone, greet, 0)
    mine = pl.ds(pl.multiple_of(core * half, half), half)
    g_all[pl.ds(xh, 1), :, mine] = gated[...].reshape(1, tokens, half)
    pl.semaphore_wait(barrier, everyone - 1)

    copies = []
    for far in range(2):
        for cross in range(2):
            if far == 0 and cross == 0:
                continue
            index = far * 2 + cross - 1
            copies.append(
                pltpu.make_async_remote_copy(
                    src_ref=gated,
                    dst_ref=g_all.at[xh, :, mine],
                    send_sem=near_send.at[index],
                    recv_sem=near_recv.at[index],
                    device_id={
                        "xh": 1 - xh if far else xh,
                        "core": 1 - core if cross else core,
                    },
                )
            )
    for copy in copies:
        copy.start()

    wide = landed.shape[-1]

    def send(which_x, b, owner):
        pltpu.make_async_remote_copy(
            src_ref=parts.at[which_x, b, owner],
            dst_ref=landed.at[slot, me],
            send_sem=far_send,
            recv_sem=far_recv.at[slot, me],
            device_id={"xh": which_x, "core": b, "y": owner // xls, "xl": lax.rem(owner, xls)},
        ).start()

    def compute(which_x, owner):
        block = weight[pl.ds(pl.multiple_of(owner * wide, wide), wide), :]
        left = g_all[pl.ds(which_x, 1)].reshape(tokens, 2 * half)
        product = lax.dot_general(
            left, block, (((1,), (1,)), ((), ())), preferred_element_type=F32
        ).astype(BF16)
        for b in range(2):
            parts[pl.ds(which_x, 1), b, pl.ds(owner, 1)] = product[
                b * rows : (b + 1) * rows
            ].reshape(1, 1, rows, wide)

    copies[0].wait_recv()

    def own_step(k, carry):
        owner = lax.rem(me + k, groups)
        compute(xh, owner)
        for b in range(2):
            send(xh, b, owner)
        return carry

    lax.fori_loop(1, groups, own_step, 0)
    compute(xh, me)
    send(xh, 1 - core, me)
    landed[pl.ds(slot, 1), pl.ds(me, 1)] = parts[
        pl.ds(xh, 1), pl.ds(core, 1), pl.ds(me, 1)
    ].reshape(1, 1, rows, wide)
    copies[1].wait_recv()
    copies[2].wait_recv()

    def far_step(k, carry):
        owner = lax.rem(me + k, groups)
        compute(1 - xh, owner)
        for b in range(2):
            send(1 - xh, b, owner)
        return carry

    lax.fori_loop(0, groups, far_step, 0)

    def arrived(k, carry):
        index = lax.rem(my_index + k, everyone)
        which, owner = index // groups, lax.rem(index, groups)
        block = landed.at[which, owner]
        pltpu.make_async_copy(block, block, far_recv.at[which, owner]).wait()
        return carry

    lax.fori_loop(1, everyone, arrived, 0)
    sums = []
    for s in range(4):
        total = landed[s, 0].astype(F32)
        for owner in range(1, groups):
            total = total + landed[s, owner].astype(F32)
        sums.append(total)
    width = weight.shape[0] // lax.axis_size("z")
    for part in range(wide // width):
        columns = [total[:, part * width : (part + 1) * width] for total in sums]
        out[:, part * 4 * width : (part + 1) * 4 * width] = jnp.concatenate(
            columns, axis=1
        ).astype(out.dtype)

    for copy in copies:
        copy.wait_send()
    sent = parts.at[0, 0, pl.ds(0, groups - 1)]
    pltpu.make_async_copy(sent, sent, far_send).wait()
    rest = parts.at[0, 1]
    pltpu.make_async_copy(rest, rest, far_send).wait()
    rest = parts.at[1]
    pltpu.make_async_copy(rest, rest, far_send).wait()


def body(qkv_in, short_taps, long_filter, skip_gain, out_weight):
    rows, _, channels = qkv_in.shape
    half = channels // 2
    chips = lax.axis_size("z") * lax.axis_size("xh")
    groups = lax.axis_size("y") * lax.axis_size("xl")
    blocks = 2 * chips
    weight = lax.all_gather(out_weight.T, "z", axis=0, tiled=True)
    lookup = tables(blocks, rows)
    exchange = (chips, 2 * CH, rows)
    gated = pl.pallas_call(
        functools.partial(conv_kernel, chips),
        out_shape=jax.ShapeDtypeStruct((2 * rows, half), BF16),
        in_specs=[VMEM] * 10,
        out_specs=VMEM,
        scratch_shapes=[
            pltpu.VMEM((2, chips, CH, rows), F32),
            pltpu.VMEM(exchange, F32),
            pltpu.VMEM(exchange, BF16),
            pltpu.VMEM(exchange, BF16),
            pltpu.VMEM((3, 16 + 2 * rows, half), BF16),
            pltpu.VMEM(exchange, BF16),
            pltpu.VMEM(exchange, BF16),
            pltpu.VMEM(exchange, BF16),
            pltpu.VMEM(exchange, BF16),
            pltpu.VMEM((blocks * CH, rows), F32),
            pltpu.SemaphoreType.DMA((4,)),
            pltpu.SemaphoreType.DMA((3,)),
            pltpu.SemaphoreType.DMA((3,)),
            pltpu.SemaphoreType.DMA((3,)),
            pltpu.SemaphoreType.DMA,
        ],
        compiler_params=pltpu.CompilerParams(
            collective_id=0, has_side_effects=True, vmem_limit_bytes=32 * 2**20
        ),
        name="conv",
    )(
        qkv_in.transpose(1, 0, 2),
        short_taps,
        long_filter,
        skip_gain[None, :],
        *[jnp.asarray(table) for table in lookup],
    )
    wide = weight.shape[0] // groups
    return pl.pallas_call(
        functools.partial(project_kernel, groups),
        out_shape=jax.ShapeDtypeStruct((rows, channels), BF16),
        in_specs=[VMEM] * 2,
        out_specs=VMEM,
        scratch_shapes=[
            pltpu.VMEM((2, 2 * rows, channels), BF16),
            pltpu.VMEM((2, 2, groups, rows, wide), BF16),
            pltpu.VMEM((4, groups, rows, wide), BF16),
            pltpu.SemaphoreType.DMA((3,)),
            pltpu.SemaphoreType.DMA((3,)),
            pltpu.SemaphoreType.DMA,
            pltpu.SemaphoreType.DMA((4, groups)),
        ],
        compiler_params=pltpu.CompilerParams(
            collective_id=1, has_side_effects=True, vmem_limit_bytes=32 * 2**20
        ),
        name="project",
    )(gated, weight)


def solution(mesh):
    sizes = dict(mesh.shape)
    split = Mesh(
        mesh.devices.reshape(sizes["ctx"] // 4, 2, 2, sizes["tp"] // 2, 2),
        ("z", "xh", "core", "y", "xl"),
    )
    ctx, tp = ("z", "xh", "core"), ("y", "xl")
    return jax.shard_map(
        body,
        mesh=split,
        in_specs=(P(ctx, None, tp), P(None, None, tp), P(ctx, tp), P(tp), P(tp, ctx)),
        out_specs=P(ctx, tp),
        check_vma=False,
    )
```

```python
import jax
import jax.numpy as jnp
import numpy as np
from jax import lax
from jax.experimental import pallas as pl
from jax.experimental.pallas import tpu as pltpu
from jax.sharding import Mesh, PartitionSpec as P

F32 = jnp.float32
BF16 = jnp.bfloat16
CH = 8
VMEM = pl.BlockSpec(memory_space=pltpu.VMEM)


def split_hi_lo(table):
    high = table.astype(np.float32).astype(jnp.bfloat16)
    low = (table - high.astype(np.float64)).astype(np.float32).astype(jnp.bfloat16)
    return high, low


def tables(blocks, width):
    length = blocks * width
    f1 = np.arange(blocks)[:, None]
    a = np.exp(-2j * np.pi * ((np.arange(blocks)[None, :] * (4 * f1 + 1)) % (4 * blocks)) / (4 * blocks))
    t = np.exp(-2j * np.pi * (np.arange(width)[None, :] * (4 * f1 + 1)) / (4 * length))
    i = np.arange(width)
    b = np.exp(-2j * np.pi * ((i[:, None] * i[None, :]) % width) / width)
    a_high, a_low = split_hi_lo(np.concatenate([a.real, a.imag], 0))
    b_high, b_low = split_hi_lo(np.block([[b.real, b.imag], [-b.imag, b.real]]))
    c_high, c_low = split_hi_lo(np.block([[b.real, -b.imag], [b.imag, b.real]]))
    d_high, d_low = split_hi_lo(np.concatenate([a.real.T, a.imag.T], 1) / length)
    return (
        np.concatenate([a_high, a_low], 1),
        t.real.astype(np.float32),
        t.imag.astype(np.float32),
        np.concatenate([b_high, b_high, b_low], 0),
        np.concatenate([c_high, c_high, c_low], 0),
        np.concatenate([d_high, d_high, d_low], 1),
    )


def dot(left, right):
    return jnp.dot(left, right, preferred_element_type=F32)


def high_low(value):
    high = value.astype(BF16)
    return high, (value - high.astype(F32)).astype(BF16)


def send_all(chips, me, source, target, send_sem, recv_sem):
    def step(k, carry):
        peer = lax.rem(me + k, chips)
        pltpu.make_async_remote_copy(
            src_ref=source.at[peer],
            dst_ref=target.at[me],
            send_sem=send_sem,
            recv_sem=recv_sem,
            device_id={"z": peer // 2, "xh": lax.rem(peer, 2)},
        ).start()
        return carry

    lax.fori_loop(1, chips, step, 0)
    target[pl.ds(me, 1)] = source[pl.ds(me, 1)]


def wait_all(chips, ref, sem):
    part = ref.at[pl.ds(0, chips - 1)]
    pltpu.make_async_copy(part, part, sem).wait()


def spectrum(received, scratch, a_fwd, t_re, t_im, b_fwd):
    rows = scratch.shape[0]
    blocks = rows // CH
    scratch[...] = received[...].astype(F32).reshape(rows, -1)
    columns = [scratch[pl.ds(c, blocks, stride=CH), :].astype(BF16) for c in range(CH)]
    signal = jnp.concatenate(columns, axis=1)
    mixed = dot(a_fwd[...], jnp.concatenate([signal, signal], axis=0))
    width = t_re.shape[1]
    parts = []
    for c in range(CH):
        re = mixed[:blocks, c * width : (c + 1) * width]
        im = mixed[blocks:, c * width : (c + 1) * width]
        parts.append(
            jnp.concatenate(
                [re * t_re - im * t_im, re * t_im + im * t_re], axis=1
            )
        )
    high, low = high_low(jnp.concatenate(parts, axis=0))
    return dot(jnp.concatenate([high, low, high], axis=1), b_fwd[...])


def inverse(product, scratch, t_re, t_im, b_inv, a_inv):
    blocks, width = t_re.shape
    high, low = high_low(product)
    back = dot(jnp.concatenate([high, low, high], axis=1), b_inv[...])
    parts = []
    for c in range(CH):
        re = back[c * blocks : (c + 1) * blocks, :width]
        im = back[c * blocks : (c + 1) * blocks, width:]
        parts.append(
            jnp.concatenate(
                [re * t_re + im * t_im, im * t_re - re * t_im], axis=0
            )
        )
    high, low = high_low(jnp.concatenate(parts, axis=1))
    result = dot(a_inv[...], jnp.concatenate([high, low, high], axis=0))
    for c in range(CH):
        scratch[pl.ds(c, blocks, stride=CH), :] = result[:, c * width : (c + 1) * width]


def local_copy(source, target, sem):
    copy = pltpu.make_async_copy(source, target, sem)
    copy.start()
    return copy


def mixer_kernel(
    qkv_hbm, taps_hbm, filt_hbm, skip_hbm, weight_hbm,
    a_fwd_hbm, t_hbm, b_fwd_hbm, b_inv_hbm, a_inv_hbm,
    out,
    taps, filt, skip, a_fwd, t_both, b_fwd, b_inv, a_inv,
    h_own, h_pair, h_send, h_recv, x_all, u_send, u_recv, y_send, y_recv, scratch,
    weight, gated, g_all, parts, landed,
    load_sem, near_send, near_recv, far_send, far_recv,
    right_send, right_recv, left_send, left_recv, g_send, g_recv, part_send, part_recv,
):
    z, xh, core = lax.axis_index("z"), lax.axis_index("xh"), lax.axis_index("core")
    zs, xls = lax.axis_size("z"), lax.axis_size("xl")
    chips, groups = zs * 2, lax.axis_size("y") * xls
    me = z * 2 + xh
    owner_me = lax.axis_index("y") * xls + lax.axis_index("xl")
    slot = xh * 2 + core
    other = 1 - core
    rows = qkv_hbm.shape[1]
    half = chips * CH
    halo = 16
    mine = pl.ds(pl.multiple_of(core * half, half), half)
    theirs = pl.ds(pl.multiple_of(other * half, half), half)
    place = pl.ds(pl.multiple_of(halo + core * rows, 16), rows)
    everyone = 4 * groups
    my_index = slot * groups + owner_me

    filt_load = local_copy(filt_hbm, filt, load_sem.at[0])
    x_load = local_copy(qkv_hbm.at[:, :, mine], x_all.at[:, place, :], load_sem.at[1])
    weight_load = local_copy(weight_hbm, weight.at[z], load_sem.at[2])
    small = [
        local_copy(source, target, load_sem.at[3 + k])
        for k, (source, target) in enumerate(
            [
                (taps_hbm, taps),
                (skip_hbm, skip),
                (a_fwd_hbm, a_fwd),
                (t_hbm, t_both),
                (b_fwd_hbm, b_fwd),
                (b_inv_hbm, b_inv),
                (a_inv_hbm, a_inv),
            ]
        )
    ]

    barrier = pltpu.get_barrier_semaphore()
    step_to = lax.rem(me + jnp.where(core == 1, 1, chips - 1), chips)
    pl.semaphore_signal(
        barrier, inc=1, device_id={"z": step_to // 2, "xh": lax.rem(step_to, 2), "core": other}
    )

    def place_of(index):
        which, owner = index // groups, lax.rem(index, groups)
        return {
            "xh": which // 2,
            "core": lax.rem(which, 2),
            "y": owner // xls,
            "xl": lax.rem(owner, xls),
        }

    def greet_ctx(k, carry):
        peer = lax.rem(me + k, chips)
        pl.semaphore_signal(
            barrier, inc=1, device_id={"z": peer // 2, "xh": lax.rem(peer, 2)}
        )
        return carry

    def greet_plane(k, carry):
        pl.semaphore_signal(barrier, inc=1, device_id=place_of(lax.rem(my_index + k, everyone)))
        return carry

    lax.fori_loop(1, chips, greet_ctx, 0)
    lax.fori_loop(1, everyone, greet_plane, 0)

    filt_load.wait()
    h_own[...] = filt[...].T.reshape(2, chips, CH, rows)
    pl.semaphore_wait(barrier, 1 + chips - 1 + everyone - 1)

    my_rows = pl.ds(pl.multiple_of(core * CH, CH), CH)
    h_copy = pltpu.make_async_remote_copy(
        src_ref=h_own.at[other],
        dst_ref=h_pair.at[:, my_rows, :],
        send_sem=near_send.at[0],
        recv_sem=near_recv.at[0],
        device_id={"core": other},
    )
    h_copy.start()
    x_copy = pltpu.make_async_remote_copy(
        src_ref=qkv_hbm.at[:, :, theirs],
        dst_ref=x_all.at[:, place, :],
        send_sem=near_send.at[1],
        recv_sem=near_recv.at[1],
        device_id={"core": other},
    )
    x_copy.start()

    after = lax.rem(me + 1, chips)

    def halo_copy(target):
        return pltpu.make_async_remote_copy(
            src_ref=qkv_hbm.at[:, pl.ds(rows - halo, halo), pl.ds(target * half, half)],
            dst_ref=x_all.at[:, pl.ds(0, halo), :],
            send_sem=near_send.at[2 + target],
            recv_sem=near_recv.at[2],
            device_id={"z": after // 2, "xh": lax.rem(after, 2), "core": target},
        )

    @pl.when(core == 1)
    def _():
        halo_copy(0).start()
        halo_copy(1).start()

    right_steps = zs // 2
    left_steps = zs - 1 - right_steps

    def right_copy(step):
        block = lax.rem(z + zs - step, zs)
        return pltpu.make_async_remote_copy(
            src_ref=weight.at[block],
            dst_ref=weight.at[block],
            send_sem=right_send.at[step],
            recv_sem=right_recv.at[step],
            device_id={"z": lax.rem(z + 1, zs)},
        )

    def left_copy(step):
        block = lax.rem(z + step, zs)
        return pltpu.make_async_remote_copy(
            src_ref=weight.at[block],
            dst_ref=weight.at[block],
            send_sem=left_send.at[step],
            recv_sem=left_recv.at[step],
            device_id={"z": lax.rem(z + zs - 1, zs)},
        )

    def landing(step, shift, sem):
        block = weight.at[lax.rem(z + shift, zs)]
        pltpu.make_async_copy(block, block, sem.at[step]).wait()

    def ring(step):
        if step == 0:
            weight_load.wait()
        if 0 < step <= right_steps:
            landing(step - 1, zs - step, right_recv)
        if 0 < step <= left_steps:
            landing(step - 1, step, left_recv)
        if step < right_steps:
            right_copy(step).start()
        if step < left_steps:
            left_copy(step).start()

    ring(0)
    h_pair[:, my_rows, :] = h_own[pl.ds(core, 1)].reshape(chips, CH, rows)
    h_copy.wait_recv()
    h_send[...] = h_pair[...].astype(BF16)
    send_all(chips, me, h_send, h_recv, far_send.at[0], far_recv.at[0])

    x_load.wait()
    small[0].wait()
    x_copy.wait_recv()
    halo_copy(0).wait_recv()
    features = []
    for s in range(3):
        x = x_all[s].astype(F32)
        first = jnp.where(me == 0, 0.0, x[:halo])
        x = jnp.concatenate([first, x[halo:]], axis=0)
        total = taps[s, 0:1, mine] * x[halo:]
        for back in range(1, taps.shape[1]):
            total = total + taps[s, back : back + 1, mine] * x[halo - back : halo - back + 2 * rows]
        features.append(total)
    query, mixed_in = features[0], features[1] * features[2]
    flipped = mixed_in.T.reshape(chips, CH, 2 * rows)
    u_send[...] = jnp.concatenate([flipped[:, :, :rows], flipped[:, :, rows:]], axis=1).astype(BF16)
    send_all(chips, me, u_send, u_recv, far_send.at[1], far_recv.at[1])
    ring(1)

    for load in small[1:]:
        load.wait()
    wait_all(chips, h_recv, far_recv.at[0])
    ring(2)
    t_re, t_im = t_both[0], t_both[1]
    h_freq = spectrum(h_recv, scratch, a_fwd, t_re, t_im, b_fwd)
    ring(3)
    wait_all(chips, u_recv, far_recv.at[1])
    ring(4)
    u_freq = spectrum(u_recv, scratch, a_fwd, t_re, t_im, b_fwd)
    ring(5)
    width = t_re.shape[1]
    h_re, h_im = h_freq[:, :width], h_freq[:, width:]
    u_re, u_im = u_freq[:, :width], u_freq[:, width:]
    product = jnp.concatenate([h_re * u_re - h_im * u_im, h_re * u_im + h_im * u_re], axis=1)
    inverse(product, scratch, t_re, t_im, b_inv, a_inv)
    y_send[...] = scratch[...].reshape(y_send.shape).astype(BF16)
    send_all(chips, me, y_send, y_recv, far_send.at[2], far_recv.at[2])
    ring(6)
    ring(7)
    wait_all(chips, y_recv, far_recv.at[2])
    for step in range(8, right_steps + 1):
        ring(step)
    back = y_recv[...].astype(F32)
    convolved = jnp.concatenate(
        [back[:, CH * b : CH * (b + 1), :].reshape(half, rows).T for b in range(2)], axis=0
    )
    gated[...] = (query * (convolved + skip[:, mine] * mixed_in)).astype(BF16)

    copies = []
    for far in range(2):
        for cross in range(2):
            if far == 0 and cross == 0:
                continue
            index = far * 2 + cross - 1
            copies.append(
                pltpu.make_async_remote_copy(
                    src_ref=gated,
                    dst_ref=g_all.at[xh, :, mine],
                    send_sem=g_send.at[index],
                    recv_sem=g_recv.at[index],
                    device_id={"xh": 1 - xh if far else xh, "core": other if cross else core},
                )
            )
    for copy in copies:
        copy.start()
    tokens = 2 * rows
    g_all[pl.ds(xh, 1), :, mine] = gated[...].reshape(1, tokens, half)
    per_owner = zs // groups
    columns = weight.shape[1]
    wide = per_owner * columns

    def send(which_x, b, owner):
        pltpu.make_async_remote_copy(
            src_ref=parts.at[which_x, b, owner],
            dst_ref=landed.at[slot, owner_me],
            send_sem=part_send,
            recv_sem=part_recv.at[slot, owner_me],
            device_id={"xh": which_x, "core": b, "y": owner // xls, "xl": lax.rem(owner, xls)},
        ).start()

    def compute(which_x, owner):
        block = weight[pl.ds(owner * per_owner, per_owner)].reshape(wide, 2 * half)
        left = g_all[pl.ds(which_x, 1)].reshape(tokens, 2 * half)
        product = lax.dot_general(
            left, block, (((1,), (1,)), ((), ())), preferred_element_type=F32
        ).astype(BF16)
        for b in range(2):
            parts[pl.ds(which_x, 1), b, pl.ds(owner, 1)] = product[
                b * rows : (b + 1) * rows
            ].reshape(1, 1, rows, wide)

    copies[0].wait_recv()

    def own_step(k, carry):
        owner = lax.rem(owner_me + k, groups)
        compute(xh, owner)
        for b in range(2):
            send(xh, b, owner)
        return carry

    lax.fori_loop(1, groups, own_step, 0)
    compute(xh, owner_me)
    send(xh, other, owner_me)
    landed[pl.ds(slot, 1), pl.ds(owner_me, 1)] = parts[
        pl.ds(xh, 1), pl.ds(core, 1), pl.ds(owner_me, 1)
    ].reshape(1, 1, rows, wide)
    copies[1].wait_recv()
    copies[2].wait_recv()

    def far_step(k, carry):
        owner = lax.rem(owner_me + k, groups)
        compute(1 - xh, owner)
        for b in range(2):
            send(1 - xh, b, owner)
        return carry

    lax.fori_loop(0, groups, far_step, 0)

    def arrived(k, carry):
        index = lax.rem(my_index + k, everyone)
        which, owner = index // groups, lax.rem(index, groups)
        block = landed.at[which, owner]
        pltpu.make_async_copy(block, block, part_recv.at[which, owner]).wait()
        return carry

    lax.fori_loop(1, everyone, arrived, 0)
    sums = []
    for s in range(4):
        total = landed[s, 0].astype(F32)
        for owner in range(1, groups):
            total = total + landed[s, owner].astype(F32)
        sums.append(total)
    for part in range(per_owner):
        pieces = [total[:, part * columns : (part + 1) * columns] for total in sums]
        out[:, part * 4 * columns : (part + 1) * 4 * columns] = jnp.concatenate(
            pieces, axis=1
        ).astype(out.dtype)

    h_copy.wait_send()
    x_copy.wait_send()

    @pl.when(core == 1)
    def _():
        halo_copy(0).wait_send()
        halo_copy(1).wait_send()

    for step in range(right_steps):
        right_copy(step).wait_send()
    for step in range(left_steps):
        left_copy(step).wait_send()
    wait_all(chips, h_send, far_send.at[0])
    wait_all(chips, u_send, far_send.at[1])
    wait_all(chips, y_send, far_send.at[2])
    for copy in copies:
        copy.wait_send()
    for sent in (parts.at[0, 0, pl.ds(0, groups - 1)], parts.at[0, 1], parts.at[1]):
        pltpu.make_async_copy(sent, sent, part_send).wait()


def body(qkv_in, short_taps, long_filter, skip_gain, out_weight):
    rows, _, channels = qkv_in.shape
    half = channels // 2
    zs = lax.axis_size("z")
    chips = zs * 2
    groups = lax.axis_size("y") * lax.axis_size("xl")
    blocks = 2 * chips
    columns = out_weight.shape[1]
    wide = zs // groups * columns
    a_fwd, t_re, t_im, b_fwd, b_inv, a_inv = tables(blocks, rows)
    lookup = [jnp.asarray(table) for table in (a_fwd, np.stack([t_re, t_im]), b_fwd, b_inv, a_inv)]
    exchange = (chips, 2 * CH, rows)
    dma = pltpu.SemaphoreType.DMA
    return pl.pallas_call(
        mixer_kernel,
        out_shape=jax.ShapeDtypeStruct((rows, channels), BF16),
        in_specs=[pl.BlockSpec(memory_space=pl.ANY)] * 10,
        out_specs=VMEM,
        scratch_shapes=[
            pltpu.VMEM(short_taps.shape, F32),
            pltpu.VMEM((rows, channels), F32),
            pltpu.VMEM((1, channels), F32),
            *[pltpu.VMEM(table.shape, table.dtype) for table in lookup],
            pltpu.VMEM((2, chips, CH, rows), F32),
            pltpu.VMEM(exchange, F32),
            pltpu.VMEM(exchange, BF16),
            pltpu.VMEM(exchange, BF16),
            pltpu.VMEM((3, 16 + 2 * rows, half), BF16),
            pltpu.VMEM(exchange, BF16),
            pltpu.VMEM(exchange, BF16),
            pltpu.VMEM(exchange, BF16),
            pltpu.VMEM(exchange, BF16),
            pltpu.VMEM((blocks * CH, rows), F32),
            pltpu.VMEM((zs, columns, channels), BF16),
            pltpu.VMEM((2 * rows, half), BF16),
            pltpu.VMEM((2, 2 * rows, channels), BF16),
            pltpu.VMEM((2, 2, groups, rows, wide), BF16),
            pltpu.VMEM((4, groups, rows, wide), BF16),
            dma((10,)),
            dma((4,)),
            dma((3,)),
            dma((3,)),
            dma((3,)),
            dma((zs,)),
            dma((zs,)),
            dma((zs,)),
            dma((zs,)),
            dma((3,)),
            dma((3,)),
            dma,
            dma((4, groups)),
        ],
        compiler_params=pltpu.CompilerParams(
            collective_id=0, has_side_effects=True, vmem_limit_bytes=48 * 2**20
        ),
        name="mixer",
    )(
        qkv_in.transpose(1, 0, 2),
        short_taps,
        long_filter,
        skip_gain[None, :],
        out_weight.T,
        *lookup,
    )


def solution(mesh):
    sizes = dict(mesh.shape)
    split = Mesh(
        mesh.devices.reshape(sizes["ctx"] // 4, 2, 2, sizes["tp"] // 2, 2),
        ("z", "xh", "core", "y", "xl"),
    )
    ctx, tp = ("z", "xh", "core"), ("y", "xl")
    return jax.shard_map(
        body,
        mesh=split,
        in_specs=(P(ctx, None, tp), P(None, None, tp), P(ctx, tp), P(tp), P(tp, ctx)),
        out_specs=P(ctx, tp),
        check_vma=False,
    )
```

```python
import jax
import jax.numpy as jnp
import numpy as np
from jax import lax
from jax.experimental import pallas as pl
from jax.experimental.pallas import tpu as pltpu
from jax.sharding import Mesh, PartitionSpec as P

F32 = jnp.float32
BF16 = jnp.bfloat16
CH = 8
VMEM = pl.BlockSpec(memory_space=pltpu.VMEM)


def tables(blocks, width):
    length = blocks * width
    f1 = np.arange(blocks)[:, None]
    a = np.exp(-2j * np.pi * ((np.arange(blocks)[None, :] * (4 * f1 + 1)) % (4 * blocks)) / (4 * blocks))
    t = np.exp(-2j * np.pi * (np.arange(width)[None, :] * (4 * f1 + 1)) / (4 * length))
    i = np.arange(width)
    b = np.exp(-2j * np.pi * ((i[:, None] * i[None, :]) % width) / width)
    found = (
        np.concatenate([a.real, a.imag], 0),
        np.stack([t.real, t.imag]),
        np.block([[b.real, b.imag], [-b.imag, b.real]]),
        np.concatenate([a.real.T, a.imag.T], 1) / length,
    )
    return [jnp.asarray(table.astype(np.float32)) for table in found]


def dot(left, right):
    return jnp.dot(left, right, preferred_element_type=F32)


def high_low(value):
    high = value.astype(BF16)
    return high, (value - high.astype(F32)).astype(BF16)


def send_all(chips, me, source, target, send_sem, recv_sem):
    def step(k, carry):
        peer = lax.rem(me + k, chips)
        pltpu.make_async_remote_copy(
            src_ref=source.at[peer],
            dst_ref=target.at[me],
            send_sem=send_sem,
            recv_sem=recv_sem,
            device_id={"z": peer // 2, "xh": lax.rem(peer, 2)},
        ).start()
        return carry

    lax.fori_loop(1, chips, step, 0)
    target[pl.ds(me, 1)] = source[pl.ds(me, 1)]


def wait_all(chips, ref, sem):
    part = ref.at[pl.ds(0, chips - 1)]
    pltpu.make_async_copy(part, part, sem).wait()


def spectrum(received, scratch, a_fwd, t_re, t_im, b_dft):
    rows = scratch.shape[0]
    blocks = rows // CH
    scratch[...] = received[...].astype(F32).reshape(rows, -1)
    columns = [scratch[pl.ds(c, blocks, stride=CH), :].astype(BF16) for c in range(CH)]
    signal = jnp.concatenate(columns, axis=1)
    mixed = dot(a_fwd[...], jnp.concatenate([signal, signal], axis=0))
    width = t_re.shape[1]
    parts = []
    for c in range(CH):
        re = mixed[:blocks, c * width : (c + 1) * width]
        im = mixed[blocks:, c * width : (c + 1) * width]
        parts.append(
            jnp.concatenate(
                [re * t_re - im * t_im, re * t_im + im * t_re], axis=1
            )
        )
    high, low = high_low(jnp.concatenate(parts, axis=0))
    return dot(jnp.concatenate([high, low, high], axis=1), b_dft[...])


def inverse(product, scratch, t_re, t_im, b_dft, a_inv):
    blocks, width = t_re.shape
    high, low = high_low(product)
    back = dot(jnp.concatenate([high, low, high], axis=1), b_dft[...])
    parts = []
    for c in range(CH):
        im = back[c * blocks : (c + 1) * blocks, :width]
        re = back[c * blocks : (c + 1) * blocks, width:]
        parts.append(
            jnp.concatenate(
                [re * t_re + im * t_im, im * t_re - re * t_im], axis=0
            )
        )
    high, low = high_low(jnp.concatenate(parts, axis=1))
    result = dot(a_inv[...], jnp.concatenate([high, low, high], axis=0))
    for c in range(CH):
        scratch[pl.ds(c, blocks, stride=CH), :] = result[:, c * width : (c + 1) * width]


def local_copy(source, target, sem):
    copy = pltpu.make_async_copy(source, target, sem)
    copy.start()
    return copy


def mixer_kernel(
    qkv_hbm, taps_hbm, filt_hbm, skip_hbm, weight_hbm,
    a_fwd_hbm, t_hbm, b_dft_hbm, a_inv_hbm,
    out,
    taps, filt, skip, a_table, t_both, b_table, a_back, a_fwd, b_dft, a_inv,
    h_own, h_pair, h_send, h_recv, x_all, u_send, u_recv, y_send, y_recv, scratch,
    weight, gated, g_all, parts, landed,
    load_sem, near_send, near_recv, far_send, far_recv,
    right_send, right_recv, left_send, left_recv, g_send, g_recv, part_send, part_recv,
):
    z, xh, core = lax.axis_index("z"), lax.axis_index("xh"), lax.axis_index("core")
    zs, xls = lax.axis_size("z"), lax.axis_size("xl")
    chips, groups = zs * 2, lax.axis_size("y") * xls
    me = z * 2 + xh
    owner_me = lax.axis_index("y") * xls + lax.axis_index("xl")
    slot = xh * 2 + core
    other = 1 - core
    rows = qkv_hbm.shape[1]
    half = chips * CH
    halo = 16
    mine = pl.ds(pl.multiple_of(core * half, half), half)
    theirs = pl.ds(pl.multiple_of(other * half, half), half)
    place = pl.ds(pl.multiple_of(halo + core * rows, 16), rows)
    everyone = 4 * groups
    my_index = slot * groups + owner_me

    filt_load = local_copy(filt_hbm, filt, load_sem.at[0])
    x_load = local_copy(qkv_hbm.at[:, :, mine], x_all.at[:, place, :], load_sem.at[1])
    weight_load = local_copy(weight_hbm, weight.at[z], load_sem.at[2])
    small = [
        local_copy(source, target, load_sem.at[3 + k])
        for k, (source, target) in enumerate(
            [
                (taps_hbm, taps),
                (skip_hbm, skip),
                (a_fwd_hbm, a_table),
                (t_hbm, t_both),
                (b_dft_hbm, b_table),
                (a_inv_hbm, a_back),
            ]
        )
    ]

    barrier = pltpu.get_barrier_semaphore()
    step_to = lax.rem(me + jnp.where(core == 1, 1, chips - 1), chips)
    pl.semaphore_signal(
        barrier, inc=1, device_id={"z": step_to // 2, "xh": lax.rem(step_to, 2), "core": other}
    )

    def place_of(index):
        which, owner = index // groups, lax.rem(index, groups)
        return {
            "xh": which // 2,
            "core": lax.rem(which, 2),
            "y": owner // xls,
            "xl": lax.rem(owner, xls),
        }

    def greet_ctx(k, carry):
        peer = lax.rem(me + k, chips)
        pl.semaphore_signal(
            barrier, inc=1, device_id={"z": peer // 2, "xh": lax.rem(peer, 2)}
        )
        return carry

    def greet_plane(k, carry):
        pl.semaphore_signal(barrier, inc=1, device_id=place_of(lax.rem(my_index + k, everyone)))
        return carry

    lax.fori_loop(1, chips, greet_ctx, 0)
    lax.fori_loop(1, everyone, greet_plane, 0)

    filt_load.wait()
    h_own[...] = filt[...].T.reshape(2, chips, CH, rows)
    pl.semaphore_wait(barrier, 1 + chips - 1 + everyone - 1)

    my_rows = pl.ds(pl.multiple_of(core * CH, CH), CH)
    h_copy = pltpu.make_async_remote_copy(
        src_ref=h_own.at[other],
        dst_ref=h_pair.at[:, my_rows, :],
        send_sem=near_send.at[0],
        recv_sem=near_recv.at[0],
        device_id={"core": other},
    )
    h_copy.start()
    x_copy = pltpu.make_async_remote_copy(
        src_ref=qkv_hbm.at[:, :, theirs],
        dst_ref=x_all.at[:, place, :],
        send_sem=near_send.at[1],
        recv_sem=near_recv.at[1],
        device_id={"core": other},
    )
    x_copy.start()

    after = lax.rem(me + 1, chips)

    def halo_copy(target):
        return pltpu.make_async_remote_copy(
            src_ref=qkv_hbm.at[:, pl.ds(rows - halo, halo), pl.ds(target * half, half)],
            dst_ref=x_all.at[:, pl.ds(0, halo), :],
            send_sem=near_send.at[2 + target],
            recv_sem=near_recv.at[2],
            device_id={"z": after // 2, "xh": lax.rem(after, 2), "core": target},
        )

    @pl.when(core == 1)
    def _():
        halo_copy(0).start()
        halo_copy(1).start()

    right_steps = zs // 2
    left_steps = zs - 1 - right_steps

    def right_copy(step):
        block = lax.rem(z + zs - step, zs)
        return pltpu.make_async_remote_copy(
            src_ref=weight.at[block],
            dst_ref=weight.at[block],
            send_sem=right_send.at[step],
            recv_sem=right_recv.at[step],
            device_id={"z": lax.rem(z + 1, zs)},
        )

    def left_copy(step):
        block = lax.rem(z + step, zs)
        return pltpu.make_async_remote_copy(
            src_ref=weight.at[block],
            dst_ref=weight.at[block],
            send_sem=left_send.at[step],
            recv_sem=left_recv.at[step],
            device_id={"z": lax.rem(z + zs - 1, zs)},
        )

    def landing(step, shift, sem):
        block = weight.at[lax.rem(z + shift, zs)]
        pltpu.make_async_copy(block, block, sem.at[step]).wait()

    def ring(step):
        if step == 0:
            weight_load.wait()
        if 0 < step <= right_steps:
            landing(step - 1, zs - step, right_recv)
        if 0 < step <= left_steps:
            landing(step - 1, step, left_recv)
        if step < right_steps:
            right_copy(step).start()
        if step < left_steps:
            left_copy(step).start()

    ring(0)
    h_pair[:, my_rows, :] = h_own[pl.ds(core, 1)].reshape(chips, CH, rows)
    h_copy.wait_recv()
    h_send[...] = h_pair[...].astype(BF16)
    send_all(chips, me, h_send, h_recv, far_send.at[0], far_recv.at[0])

    x_load.wait()
    small[0].wait()
    x_copy.wait_recv()
    halo_copy(0).wait_recv()
    features = []
    for s in range(3):
        x = x_all[s].astype(F32)
        first = jnp.where(me == 0, 0.0, x[:halo])
        x = jnp.concatenate([first, x[halo:]], axis=0)
        total = taps[s, 0:1, mine] * x[halo:]
        for back in range(1, taps.shape[1]):
            total = total + taps[s, back : back + 1, mine] * x[halo - back : halo - back + 2 * rows]
        features.append(total)
    query, mixed_in = features[0], features[1] * features[2]
    flipped = mixed_in.T.reshape(chips, CH, 2 * rows)
    u_send[...] = jnp.concatenate([flipped[:, :, :rows], flipped[:, :, rows:]], axis=1).astype(BF16)
    send_all(chips, me, u_send, u_recv, far_send.at[1], far_recv.at[1])
    ring(1)

    for load in small[1:]:
        load.wait()
    a_fwd[...] = jnp.concatenate(high_low(a_table[...]), axis=1)
    high, low = high_low(b_table[...])
    b_dft[...] = jnp.concatenate([high, high, low], axis=0)
    high, low = high_low(a_back[...])
    a_inv[...] = jnp.concatenate([high, high, low], axis=1)
    wait_all(chips, h_recv, far_recv.at[0])
    ring(2)
    t_re, t_im = t_both[0], t_both[1]
    h_freq = spectrum(h_recv, scratch, a_fwd, t_re, t_im, b_dft)
    ring(3)
    wait_all(chips, u_recv, far_recv.at[1])
    ring(4)
    u_freq = spectrum(u_recv, scratch, a_fwd, t_re, t_im, b_dft)
    ring(5)
    width = t_re.shape[1]
    h_re, h_im = h_freq[:, :width], h_freq[:, width:]
    u_re, u_im = u_freq[:, :width], u_freq[:, width:]
    product = jnp.concatenate([h_re * u_im + h_im * u_re, h_re * u_re - h_im * u_im], axis=1)
    inverse(product, scratch, t_re, t_im, b_dft, a_inv)
    y_send[...] = scratch[...].reshape(y_send.shape).astype(BF16)
    send_all(chips, me, y_send, y_recv, far_send.at[2], far_recv.at[2])
    ring(6)
    ring(7)
    wait_all(chips, y_recv, far_recv.at[2])
    for step in range(8, right_steps + 1):
        ring(step)
    back = y_recv[...].astype(F32)
    convolved = jnp.concatenate(
        [back[:, CH * b : CH * (b + 1), :].reshape(half, rows).T for b in range(2)], axis=0
    )
    gated[...] = (query * (convolved + skip[:, mine] * mixed_in)).astype(BF16)

    copies = []
    for far in range(2):
        for cross in range(2):
            if far == 0 and cross == 0:
                continue
            index = far * 2 + cross - 1
            copies.append(
                pltpu.make_async_remote_copy(
                    src_ref=gated,
                    dst_ref=g_all.at[xh, :, mine],
                    send_sem=g_send.at[index],
                    recv_sem=g_recv.at[index],
                    device_id={"xh": 1 - xh if far else xh, "core": other if cross else core},
                )
            )
    for copy in copies:
        copy.start()
    tokens = 2 * rows
    g_all[pl.ds(xh, 1), :, mine] = gated[...].reshape(1, tokens, half)
    per_owner = zs // groups
    columns = weight.shape[1]
    wide = per_owner * columns

    def send(which_x, b, owner):
        pltpu.make_async_remote_copy(
            src_ref=parts.at[which_x, b, owner],
            dst_ref=landed.at[slot, owner_me],
            send_sem=part_send,
            recv_sem=part_recv.at[slot, owner_me],
            device_id={"xh": which_x, "core": b, "y": owner // xls, "xl": lax.rem(owner, xls)},
        ).start()

    def compute(which_x, owner):
        block = weight[pl.ds(owner * per_owner, per_owner)].reshape(wide, 2 * half)
        left = g_all[pl.ds(which_x, 1)].reshape(tokens, 2 * half)
        product = lax.dot_general(
            left, block, (((1,), (1,)), ((), ())), preferred_element_type=F32
        ).astype(BF16)
        for b in range(2):
            parts[pl.ds(which_x, 1), b, pl.ds(owner, 1)] = product[
                b * rows : (b + 1) * rows
            ].reshape(1, 1, rows, wide)

    copies[0].wait_recv()

    def own_step(k, carry):
        owner = lax.rem(owner_me + k, groups)
        compute(xh, owner)
        for b in range(2):
            send(xh, b, owner)
        return carry

    lax.fori_loop(1, groups, own_step, 0)
    compute(xh, owner_me)
    send(xh, other, owner_me)
    landed[pl.ds(slot, 1), pl.ds(owner_me, 1)] = parts[
        pl.ds(xh, 1), pl.ds(core, 1), pl.ds(owner_me, 1)
    ].reshape(1, 1, rows, wide)
    copies[1].wait_recv()
    copies[2].wait_recv()

    def far_step(k, carry):
        owner = lax.rem(owner_me + k, groups)
        compute(1 - xh, owner)
        for b in range(2):
            send(1 - xh, b, owner)
        return carry

    lax.fori_loop(0, groups, far_step, 0)

    def arrived(k, carry):
        index = lax.rem(my_index + k, everyone)
        which, owner = index // groups, lax.rem(index, groups)
        block = landed.at[which, owner]
        pltpu.make_async_copy(block, block, part_recv.at[which, owner]).wait()
        return carry

    lax.fori_loop(1, everyone, arrived, 0)
    sums = []
    for s in range(4):
        total = landed[s, 0].astype(F32)
        for owner in range(1, groups):
            total = total + landed[s, owner].astype(F32)
        sums.append(total)
    for part in range(per_owner):
        pieces = [total[:, part * columns : (part + 1) * columns] for total in sums]
        out[:, part * 4 * columns : (part + 1) * 4 * columns] = jnp.concatenate(
            pieces, axis=1
        ).astype(out.dtype)

    h_copy.wait_send()
    x_copy.wait_send()

    @pl.when(core == 1)
    def _():
        halo_copy(0).wait_send()
        halo_copy(1).wait_send()

    for step in range(right_steps):
        right_copy(step).wait_send()
    for step in range(left_steps):
        left_copy(step).wait_send()
    wait_all(chips, h_send, far_send.at[0])
    wait_all(chips, u_send, far_send.at[1])
    wait_all(chips, y_send, far_send.at[2])
    for copy in copies:
        copy.wait_send()
    for sent in (parts.at[0, 0, pl.ds(0, groups - 1)], parts.at[0, 1], parts.at[1]):
        pltpu.make_async_copy(sent, sent, part_send).wait()


def body(qkv_in, short_taps, long_filter, skip_gain, out_weight):
    rows, _, channels = qkv_in.shape
    half = channels // 2
    zs = lax.axis_size("z")
    chips = zs * 2
    groups = lax.axis_size("y") * lax.axis_size("xl")
    blocks = 2 * chips
    columns = out_weight.shape[1]
    wide = zs // groups * columns
    lookup = tables(blocks, rows)
    exchange = (chips, 2 * CH, rows)
    dma = pltpu.SemaphoreType.DMA
    return pl.pallas_call(
        mixer_kernel,
        out_shape=jax.ShapeDtypeStruct((rows, channels), BF16),
        in_specs=[pl.BlockSpec(memory_space=pl.ANY)] * 9,
        out_specs=VMEM,
        scratch_shapes=[
            pltpu.VMEM(short_taps.shape, F32),
            pltpu.VMEM((rows, channels), F32),
            pltpu.VMEM((1, channels), F32),
            *[pltpu.VMEM(table.shape, table.dtype) for table in lookup],
            pltpu.VMEM((2 * blocks, 2 * blocks), BF16),
            pltpu.VMEM((6 * rows, 2 * rows), BF16),
            pltpu.VMEM((blocks, 6 * blocks), BF16),
            pltpu.VMEM((2, chips, CH, rows), F32),
            pltpu.VMEM(exchange, F32),
            pltpu.VMEM(exchange, BF16),
            pltpu.VMEM(exchange, BF16),
            pltpu.VMEM((3, 16 + 2 * rows, half), BF16),
            pltpu.VMEM(exchange, BF16),
            pltpu.VMEM(exchange, BF16),
            pltpu.VMEM(exchange, BF16),
            pltpu.VMEM(exchange, BF16),
            pltpu.VMEM((blocks * CH, rows), F32),
            pltpu.VMEM((zs, columns, channels), BF16),
            pltpu.VMEM((2 * rows, half), BF16),
            pltpu.VMEM((2, 2 * rows, channels), BF16),
            pltpu.VMEM((2, 2, groups, rows, wide), BF16),
            pltpu.VMEM((4, groups, rows, wide), BF16),
            dma((9,)),
            dma((4,)),
            dma((3,)),
            dma((3,)),
            dma((3,)),
            dma((zs,)),
            dma((zs,)),
            dma((zs,)),
            dma((zs,)),
            dma((3,)),
            dma((3,)),
            dma,
            dma((4, groups)),
        ],
        compiler_params=pltpu.CompilerParams(
            collective_id=0, has_side_effects=True, vmem_limit_bytes=60 * 2**20
        ),
        name="mixer",
    )(
        qkv_in.transpose(1, 0, 2),
        short_taps,
        long_filter,
        skip_gain[None, :],
        out_weight.T,
        *lookup,
    )


def solution(mesh):
    sizes = dict(mesh.shape)
    split = Mesh(
        mesh.devices.reshape(sizes["ctx"] // 4, 2, 2, sizes["tp"] // 2, 2),
        ("z", "xh", "core", "y", "xl"),
    )
    ctx, tp = ("z", "xh", "core"), ("y", "xl")
    return jax.shard_map(
        body,
        mesh=split,
        in_specs=(P(ctx, None, tp), P(None, None, tp), P(ctx, tp), P(tp), P(tp, ctx)),
        out_specs=P(ctx, tp),
        check_vma=False,
    )
```

```python
import jax
import jax.numpy as jnp
import numpy as np
from jax import lax
from jax.experimental import pallas as pl
from jax.experimental.pallas import tpu as pltpu
from jax.sharding import Mesh, PartitionSpec as P

F32 = jnp.float32
BF16 = jnp.bfloat16
CH = 8
VMEM = pl.BlockSpec(memory_space=pltpu.VMEM)


def tables(blocks, width):
    length = blocks * width
    f1 = np.arange(blocks)[:, None]
    a = np.exp(-2j * np.pi * ((np.arange(blocks)[None, :] * (4 * f1 + 1)) % (4 * blocks)) / (4 * blocks))
    t = np.exp(-2j * np.pi * (np.arange(width)[None, :] * (4 * f1 + 1)) / (4 * length))
    i = np.arange(width)
    b = np.exp(-2j * np.pi * ((i[:, None] * i[None, :]) % width) / width)
    found = (
        np.concatenate([a.real, a.imag], 0),
        np.stack([t.real, t.imag]),
        np.block([[b.real, b.imag], [-b.imag, b.real]]),
        np.concatenate([a.real.T, a.imag.T], 1) / length,
    )
    return [jnp.asarray(table.astype(np.float32)) for table in found]


def dot(left, right):
    return jnp.dot(left, right, preferred_element_type=F32)


def high_low(value):
    high = value.astype(BF16)
    return high, (value - high.astype(F32)).astype(BF16)


def send_all(z, xh, source, target, send_sem, recv_sem):
    zs = lax.axis_size("z")
    me = z * 2 + xh

    def step(k, carry):
        turn = k // 2
        ahead = zs // 2 + jnp.where(lax.rem(turn, 2) == 1, -((turn + 1) // 2), turn // 2)
        to_z = lax.rem(z + ahead, zs)
        to_x = jnp.where(lax.rem(k, 2) == 0, 1 - xh, xh)
        pltpu.make_async_remote_copy(
            src_ref=source.at[to_z * 2 + to_x],
            dst_ref=target.at[me],
            send_sem=send_sem,
            recv_sem=recv_sem,
            device_id={"z": to_z, "xh": to_x},
        ).start()
        return carry

    lax.fori_loop(0, 2 * zs - 1, step, 0)
    target[pl.ds(me, 1)] = source[pl.ds(me, 1)]


def wait_all(chips, ref, sem):
    part = ref.at[pl.ds(0, chips - 1)]
    pltpu.make_async_copy(part, part, sem).wait()


def spectrum(received, scratch, a_fwd, t_re, t_im, b_dft):
    rows = scratch.shape[0]
    blocks = rows // CH
    scratch[...] = received[...].astype(F32).reshape(rows, -1)
    columns = [scratch[pl.ds(c, blocks, stride=CH), :].astype(BF16) for c in range(CH)]
    signal = jnp.concatenate(columns, axis=1)
    mixed = dot(a_fwd[...], jnp.concatenate([signal, signal], axis=0))
    width = t_re.shape[1]
    parts = []
    for c in range(CH):
        re = mixed[:blocks, c * width : (c + 1) * width]
        im = mixed[blocks:, c * width : (c + 1) * width]
        parts.append(
            jnp.concatenate(
                [re * t_re - im * t_im, re * t_im + im * t_re], axis=1
            )
        )
    high, low = high_low(jnp.concatenate(parts, axis=0))
    return dot(jnp.concatenate([high, low, high], axis=1), b_dft[...])


def inverse(product, scratch, t_re, t_im, b_dft, a_inv):
    blocks, width = t_re.shape
    high, low = high_low(product)
    back = dot(jnp.concatenate([high, low, high], axis=1), b_dft[...])
    parts = []
    for c in range(CH):
        im = back[c * blocks : (c + 1) * blocks, :width]
        re = back[c * blocks : (c + 1) * blocks, width:]
        parts.append(
            jnp.concatenate(
                [re * t_re + im * t_im, im * t_re - re * t_im], axis=0
            )
        )
    high, low = high_low(jnp.concatenate(parts, axis=1))
    result = dot(a_inv[...], jnp.concatenate([high, low, high], axis=0))
    for c in range(CH):
        scratch[pl.ds(c, blocks, stride=CH), :] = result[:, c * width : (c + 1) * width]


def local_copy(source, target, sem):
    copy = pltpu.make_async_copy(source, target, sem)
    copy.start()
    return copy


def mixer_kernel(
    qkv_hbm, taps_hbm, filt_hbm, skip_hbm, weight_hbm,
    a_fwd_hbm, t_hbm, b_dft_hbm, a_inv_hbm,
    out,
    taps, filt, skip, a_table, t_both, b_table, a_back, a_fwd, b_dft, a_inv,
    h_own, h_pair, h_send, h_recv, x_all, u_send, u_recv, y_send, y_recv, scratch,
    weight, gated, g_all, parts, landed,
    load_sem, near_send, near_recv, far_send, far_recv,
    right_send, right_recv, left_send, left_recv, g_send, g_recv, part_send, part_recv,
):
    z, xh, core = lax.axis_index("z"), lax.axis_index("xh"), lax.axis_index("core")
    y, xl = lax.axis_index("y"), lax.axis_index("xl")
    zs, ys = lax.axis_size("z"), lax.axis_size("y")
    chips = zs * 2
    per_owner = zs // (2 * ys)
    me = z * 2 + xh
    slot = xh * 2 + core
    other = 1 - core
    rows = qkv_hbm.shape[1]
    half = chips * CH
    halo = 16
    mine = pl.ds(pl.multiple_of(core * half, half), half)
    theirs = pl.ds(pl.multiple_of(other * half, half), half)
    place = pl.ds(pl.multiple_of(halo + core * rows, 16), rows)
    everyone = 4 * ys
    my_index = slot * ys + y
    x = xh * 2 + xl
    up, down = lax.rem(x + 1, 4), lax.rem(x + 3, 4)
    up_x = {"xh": up // 2, "xl": lax.rem(up, 2)}
    down_x = {"xh": down // 2, "xl": lax.rem(down, 2)}

    def on(block):
        return lax.rem(block // per_owner, 2) == xl

    def spot(block):
        return block // (2 * per_owner) * per_owner + lax.rem(block, per_owner)

    filt_load = local_copy(filt_hbm, filt, load_sem.at[0])
    x_load = local_copy(qkv_hbm.at[:, :, mine], x_all.at[:, place, :], load_sem.at[1])
    weight_load = pltpu.make_async_copy(weight_hbm, weight.at[spot(z), xl], load_sem.at[2])

    @pl.when(on(z))
    def _():
        weight_load.start()

    small = [
        local_copy(source, target, load_sem.at[3 + k])
        for k, (source, target) in enumerate(
            [
                (taps_hbm, taps),
                (skip_hbm, skip),
                (a_fwd_hbm, a_table),
                (t_hbm, t_both),
                (b_dft_hbm, b_table),
                (a_inv_hbm, a_back),
            ]
        )
    ]

    barrier = pltpu.get_barrier_semaphore()
    step_to = lax.rem(me + jnp.where(core == 1, 1, chips - 1), chips)
    pl.semaphore_signal(
        barrier, inc=1, device_id={"z": step_to // 2, "xh": lax.rem(step_to, 2), "core": other}
    )

    pl.semaphore_signal(barrier, inc=1, device_id=up_x)
    pl.semaphore_signal(barrier, inc=1, device_id=down_x)

    def place_of(index):
        which = index // ys
        return {"xh": which // 2, "core": lax.rem(which, 2), "y": lax.rem(index, ys)}

    def greet_ctx(k, carry):
        peer = lax.rem(me + k, chips)
        pl.semaphore_signal(
            barrier, inc=1, device_id={"z": peer // 2, "xh": lax.rem(peer, 2)}
        )
        return carry

    def greet_plane(k, carry):
        pl.semaphore_signal(barrier, inc=1, device_id=place_of(lax.rem(my_index + k, everyone)))
        return carry

    lax.fori_loop(1, chips, greet_ctx, 0)
    lax.fori_loop(1, everyone, greet_plane, 0)

    filt_load.wait()
    h_own[...] = filt[...].T.reshape(2, chips, CH, rows)
    pl.semaphore_wait(barrier, 3 + chips - 1 + everyone - 1)

    my_rows = pl.ds(pl.multiple_of(core * CH, CH), CH)
    h_copy = pltpu.make_async_remote_copy(
        src_ref=h_own.at[other],
        dst_ref=h_pair.at[:, my_rows, :],
        send_sem=near_send.at[0],
        recv_sem=near_recv.at[0],
        device_id={"core": other},
    )
    h_copy.start()
    x_copy = pltpu.make_async_remote_copy(
        src_ref=qkv_hbm.at[:, :, theirs],
        dst_ref=x_all.at[:, place, :],
        send_sem=near_send.at[1],
        recv_sem=near_recv.at[1],
        device_id={"core": other},
    )
    x_copy.start()

    after = lax.rem(me + 1, chips)

    def halo_copy(target):
        return pltpu.make_async_remote_copy(
            src_ref=qkv_hbm.at[:, pl.ds(rows - halo, halo), pl.ds(target * half, half)],
            dst_ref=x_all.at[:, pl.ds(0, halo), :],
            send_sem=near_send.at[2 + target],
            recv_sem=near_recv.at[2],
            device_id={"z": after // 2, "xh": lax.rem(after, 2), "core": target},
        )

    @pl.when(core == 1)
    def _():
        halo_copy(0).start()
        halo_copy(1).start()

    swap = pltpu.make_async_remote_copy(
        src_ref=weight_hbm,
        dst_ref=weight.at[spot(z), xl],
        send_sem=near_send.at[4],
        recv_sem=near_recv.at[3],
        device_id={"xl": 1 - xl},
    )

    @pl.when(jnp.logical_not(on(z)))
    def _():
        swap.start()

    right_steps = zs // 2
    left_steps = zs - 1 - right_steps

    def pass_on(block, step, send_sem, recv_sem, ahead):
        return pltpu.make_async_remote_copy(
            src_ref=weight.at[spot(block)],
            dst_ref=weight.at[spot(block)],
            send_sem=send_sem.at[step],
            recv_sem=recv_sem.at[step],
            device_id={"z": lax.rem(z + ahead, zs)},
        )

    def right_copy(step):
        return pass_on(lax.rem(z + zs - step, zs), step, right_send, right_recv, 1)

    def left_copy(step):
        return pass_on(lax.rem(z + step, zs), step, left_send, left_recv, zs - 1)

    def landing(step, shift, sem):
        block = lax.rem(z + shift, zs)

        @pl.when(on(block))
        def _():
            landed_at = weight.at[spot(block)]
            pltpu.make_async_copy(landed_at, landed_at, sem.at[step]).wait()

    def ring(step):
        if step > right_steps:
            return
        if step == 0:

            @pl.when(on(z))
            def _():
                weight_load.wait()
                swap.wait_recv()

        if 0 < step <= right_steps:
            landing(step - 1, zs - step, right_recv)
        if 0 < step <= left_steps:
            landing(step - 1, step, left_recv)
        if step < right_steps:

            @pl.when(on(lax.rem(z + zs - step, zs)))
            def _():
                right_copy(step).start()

        if step < left_steps:

            @pl.when(on(lax.rem(z + step, zs)))
            def _():
                left_copy(step).start()

    ring(0)
    h_pair[:, my_rows, :] = h_own[pl.ds(core, 1)].reshape(chips, CH, rows)
    h_copy.wait_recv()
    h_send[...] = h_pair[...].astype(BF16)
    send_all(z, xh, h_send, h_recv, far_send.at[0], far_recv.at[0])

    x_load.wait()
    small[0].wait()
    x_copy.wait_recv()
    halo_copy(0).wait_recv()
    features = []
    for s in range(3):
        raw = x_all[s].astype(F32)
        first = jnp.where(me == 0, 0.0, raw[:halo])
        raw = jnp.concatenate([first, raw[halo:]], axis=0)
        total = taps[s, 0:1, mine] * raw[halo:]
        for back in range(1, taps.shape[1]):
            total = total + taps[s, back : back + 1, mine] * raw[halo - back : halo - back + 2 * rows]
        features.append(total)
    query, mixed_in = features[0], features[1] * features[2]
    flipped = mixed_in.T.reshape(chips, CH, 2 * rows)
    u_send[...] = jnp.concatenate([flipped[:, :, :rows], flipped[:, :, rows:]], axis=1).astype(BF16)
    send_all(z, xh, u_send, u_recv, far_send.at[1], far_recv.at[1])
    ring(1)

    for load in small[1:]:
        load.wait()
    a_fwd[...] = jnp.concatenate(high_low(a_table[...]), axis=1)
    high, low = high_low(b_table[...])
    b_dft[...] = jnp.concatenate([high, high, low], axis=0)
    high, low = high_low(a_back[...])
    a_inv[...] = jnp.concatenate([high, high, low], axis=1)
    wait_all(chips, h_recv, far_recv.at[0])
    ring(2)
    t_re, t_im = t_both[0], t_both[1]
    h_freq = spectrum(h_recv, scratch, a_fwd, t_re, t_im, b_dft)
    ring(3)
    wait_all(chips, u_recv, far_recv.at[1])
    ring(4)
    u_freq = spectrum(u_recv, scratch, a_fwd, t_re, t_im, b_dft)
    ring(5)
    width = t_re.shape[1]
    h_re, h_im = h_freq[:, :width], h_freq[:, width:]
    u_re, u_im = u_freq[:, :width], u_freq[:, width:]
    product = jnp.concatenate([h_re * u_im + h_im * u_re, h_re * u_re - h_im * u_im], axis=1)
    inverse(product, scratch, t_re, t_im, b_dft, a_inv)
    y_send[...] = scratch[...].reshape(y_send.shape).astype(BF16)
    send_all(z, xh, y_send, y_recv, far_send.at[2], far_recv.at[2])
    wait_all(chips, y_recv, far_recv.at[2])
    back = y_recv[...].astype(F32)
    convolved = jnp.concatenate(
        [back[:, CH * b : CH * (b + 1), :].reshape(half, rows).T for b in range(2)], axis=0
    )
    gated[...] = (query * (convolved + skip[:, mine] * mixed_in)).astype(BF16)

    tokens = 2 * rows

    def g_at(ref, which):
        return ref.at[which // 2, lax.rem(which, 2), :, mine]

    def g_copy(index, source, which, device_id):
        return pltpu.make_async_remote_copy(
            src_ref=source,
            dst_ref=g_at(g_all, which),
            send_sem=g_send.at[index],
            recv_sem=g_recv.at[index],
            device_id=device_id,
        )

    across = lax.rem(x + 2, 4)
    to_up = g_copy(0, gated, x, up_x)
    to_down = g_copy(1, gated, x, down_x)
    to_other = [
        g_copy(3, gated, x, {"core": other}),
        g_copy(4, g_at(g_all, down), down, {"core": other}),
        g_copy(5, g_at(g_all, up), up, {"core": other}),
        g_copy(6, g_at(g_all, across), across, {"core": other}),
    ]
    pass_up = g_copy(2, g_at(g_all, down), down, up_x)
    pass_down = g_copy(2, g_at(g_all, up), up, down_x)
    to_up.start()
    to_down.start()
    to_other[0].start()
    g_all[pl.ds(xh, 1), pl.ds(xl, 1), :, mine] = gated[...].reshape(1, 1, tokens, half)
    for step in range(6, right_steps + 1):
        ring(step)
    to_up.wait_recv()
    to_other[1].start()

    @pl.when(core == 0)
    def _():
        pass_up.start()

    to_down.wait_recv()
    to_other[2].start()

    @pl.when(core == 1)
    def _():
        pass_down.start()

    columns = weight.shape[2]
    wide = per_owner * columns

    def send(which_x, b, owner):
        pltpu.make_async_remote_copy(
            src_ref=parts.at[which_x, b, owner],
            dst_ref=landed.at[slot, y],
            send_sem=part_send,
            recv_sem=part_recv.at[slot, y],
            device_id={"xh": which_x, "core": b, "y": owner},
        ).start()

    def compute(which_x, owner):
        product = jnp.zeros((tokens, wide), F32)
        for part in range(2):
            block = weight[pl.ds(owner * per_owner, per_owner), part].reshape(wide, 2 * half)
            left = g_all[pl.ds(which_x, 1), part].reshape(tokens, 2 * half)
            product = product + lax.dot_general(
                left, block, (((1,), (1,)), ((), ())), preferred_element_type=F32
            )
        for b in range(2):
            parts[pl.ds(which_x, 1), b, pl.ds(owner, 1)] = (
                product[b * rows : (b + 1) * rows].astype(BF16).reshape(1, 1, rows, wide)
            )

    for copy in to_other[:3]:
        copy.wait_recv()

    def own_step(k, carry):
        owner = lax.rem(y + k, ys)
        compute(xh, owner)
        for b in range(2):
            send(xh, b, owner)
        return carry

    lax.fori_loop(1, ys, own_step, 0)
    compute(xh, y)
    send(xh, other, y)
    landed[pl.ds(slot, 1), pl.ds(y, 1)] = parts[
        pl.ds(xh, 1), pl.ds(core, 1), pl.ds(y, 1)
    ].reshape(1, 1, rows, wide)
    pass_up.wait_recv()
    to_other[3].start()
    to_other[3].wait_recv()

    def far_step(k, carry):
        owner = lax.rem(y + k, ys)
        compute(1 - xh, owner)
        for b in range(2):
            send(1 - xh, b, owner)
        return carry

    lax.fori_loop(0, ys, far_step, 0)

    def arrived(k, carry):
        index = lax.rem(my_index + k, everyone)
        which, owner = index // ys, lax.rem(index, ys)
        block = landed.at[which, owner]
        pltpu.make_async_copy(block, block, part_recv.at[which, owner]).wait()
        return carry

    lax.fori_loop(1, everyone, arrived, 0)
    sums = []
    for s in range(4):
        total = landed[s, 0].astype(F32)
        for owner in range(1, ys):
            total = total + landed[s, owner].astype(F32)
        sums.append(total)
    for part in range(per_owner):
        pieces = [total[:, part * columns : (part + 1) * columns] for total in sums]
        out[:, part * 4 * columns : (part + 1) * 4 * columns] = jnp.concatenate(
            pieces, axis=1
        ).astype(out.dtype)

    h_copy.wait_send()
    x_copy.wait_send()

    @pl.when(core == 1)
    def _():
        halo_copy(0).wait_send()
        halo_copy(1).wait_send()

    @pl.when(jnp.logical_not(on(z)))
    def _():
        swap.wait_send()

    for step in range(right_steps):

        @pl.when(on(lax.rem(z + zs - step, zs)))
        def _():
            right_copy(step).wait_send()

    for step in range(left_steps):

        @pl.when(on(lax.rem(z + step, zs)))
        def _():
            left_copy(step).wait_send()

    wait_all(chips, h_send, far_send.at[0])
    wait_all(chips, u_send, far_send.at[1])
    wait_all(chips, y_send, far_send.at[2])
    for copy in (to_up, to_down, pass_up, *to_other):
        copy.wait_send()
    for sent in (parts.at[0, 0, pl.ds(0, ys - 1)], parts.at[0, 1], parts.at[1]):
        pltpu.make_async_copy(sent, sent, part_send).wait()


def body(qkv_in, short_taps, long_filter, skip_gain, out_weight):
    rows, _, channels = qkv_in.shape
    half = channels // 2
    zs = lax.axis_size("z")
    chips = zs * 2
    ys = lax.axis_size("y")
    blocks = 2 * chips
    columns = out_weight.shape[1]
    wide = zs // (2 * ys) * columns
    lookup = tables(blocks, rows)
    exchange = (chips, 2 * CH, rows)
    dma = pltpu.SemaphoreType.DMA
    return pl.pallas_call(
        mixer_kernel,
        out_shape=jax.ShapeDtypeStruct((rows, channels), BF16),
        in_specs=[pl.BlockSpec(memory_space=pl.ANY)] * 9,
        out_specs=VMEM,
        scratch_shapes=[
            pltpu.VMEM(short_taps.shape, F32),
            pltpu.VMEM((rows, channels), F32),
            pltpu.VMEM((1, channels), F32),
            *[pltpu.VMEM(table.shape, table.dtype) for table in lookup],
            pltpu.VMEM((2 * blocks, 2 * blocks), BF16),
            pltpu.VMEM((6 * rows, 2 * rows), BF16),
            pltpu.VMEM((blocks, 6 * blocks), BF16),
            pltpu.VMEM((2, chips, CH, rows), F32),
            pltpu.VMEM(exchange, F32),
            pltpu.VMEM(exchange, BF16),
            pltpu.VMEM(exchange, BF16),
            pltpu.VMEM((3, 16 + 2 * rows, half), BF16),
            pltpu.VMEM(exchange, BF16),
            pltpu.VMEM(exchange, BF16),
            pltpu.VMEM(exchange, BF16),
            pltpu.VMEM(exchange, BF16),
            pltpu.VMEM((blocks * CH, rows), F32),
            pltpu.VMEM((zs // 2, 2, columns, channels), BF16),
            pltpu.VMEM((2 * rows, half), BF16),
            pltpu.VMEM((2, 2, 2 * rows, channels), BF16),
            pltpu.VMEM((2, 2, ys, rows, wide), BF16),
            pltpu.VMEM((4, ys, rows, wide), BF16),
            dma((9,)),
            dma((5,)),
            dma((4,)),
            dma((3,)),
            dma((3,)),
            dma((zs,)),
            dma((zs,)),
            dma((zs,)),
            dma((zs,)),
            dma((7,)),
            dma((7,)),
            dma,
            dma((4, ys)),
        ],
        compiler_params=pltpu.CompilerParams(
            collective_id=0, has_side_effects=True, vmem_limit_bytes=60 * 2**20
        ),
        name="mixer",
    )(
        qkv_in.transpose(1, 0, 2),
        short_taps,
        long_filter,
        skip_gain[None, :],
        out_weight.T,
        *lookup,
    )


def solution(mesh):
    sizes = dict(mesh.shape)
    split = Mesh(
        mesh.devices.reshape(sizes["ctx"] // 4, 2, 2, sizes["tp"] // 2, 2),
        ("z", "xh", "core", "y", "xl"),
    )
    ctx, tp = ("z", "xh", "core"), ("y", "xl")
    return jax.shard_map(
        body,
        mesh=split,
        in_specs=(P(ctx, None, tp), P(None, None, tp), P(ctx, tp), P(tp), P(tp, ctx)),
        out_specs=P(ctx, tp),
        check_vma=False,
    )
```

```python
import jax
import jax.numpy as jnp
import numpy as np
from jax import lax
from jax.experimental import pallas as pl
from jax.experimental.pallas import tpu as pltpu
from jax.sharding import Mesh, PartitionSpec as P

F32 = jnp.float32
BF16 = jnp.bfloat16
CH = 8
VMEM = pl.BlockSpec(memory_space=pltpu.VMEM)


def tables(blocks, width):
    length = blocks * width
    f1 = np.arange(blocks)[:, None]
    a = np.exp(-2j * np.pi * ((np.arange(blocks)[None, :] * (4 * f1 + 1)) % (4 * blocks)) / (4 * blocks))
    t = np.exp(-2j * np.pi * (np.arange(width)[None, :] * (4 * f1 + 1)) / (4 * length))
    i = np.arange(width)
    b = np.exp(-2j * np.pi * ((i[:, None] * i[None, :]) % width) / width)
    found = (
        np.concatenate([a.real, a.imag], 0),
        np.stack([t.real, t.imag]),
        np.block([[b.real, b.imag], [-b.imag, b.real]]),
        np.concatenate([a.real.T, a.imag.T], 1) / length,
    )
    return [jnp.asarray(table.astype(np.float32)) for table in found]


def dot(left, right):
    return jnp.dot(left, right, preferred_element_type=F32)


def high_low(value):
    high = value.astype(BF16)
    return high, (value - high.astype(F32)).astype(BF16)


def send_all(z, xh, source, target, send_sem, recv_sems):
    zs = lax.axis_size("z")
    me = z * 2 + xh
    size = 2 * zs // recv_sems.shape[0]

    def step(k, carry):
        turn = k // 2
        ahead = zs // 2 + jnp.where(lax.rem(turn, 2) == 1, -((turn + 1) // 2), turn // 2)
        to_z = lax.rem(z + ahead, zs)
        to_x = jnp.where(lax.rem(k, 2) == 0, 1 - xh, xh)
        pltpu.make_async_remote_copy(
            src_ref=source.at[to_z * 2 + to_x],
            dst_ref=target.at[me],
            send_sem=send_sem,
            recv_sem=recv_sems.at[k // size],
            device_id={"z": to_z, "xh": to_x},
        ).start()
        return carry

    lax.fori_loop(0, 2 * zs - 1, step, 0)
    target[pl.ds(me, 1)] = source[pl.ds(me, 1)]


def wait_blocks(count, ref, sem):
    part = ref.at[pl.ds(0, count)]
    pltpu.make_async_copy(part, part, sem).wait()


def wait_group(ref, sems, group):
    size = ref.shape[0] // sems.shape[0]
    wait_blocks(size - (group == sems.shape[0] - 1), ref, sems.at[group])


def spectrum(received, scratch, a_fwd, t_re, t_im, b_dft):
    rows = scratch.shape[0]
    blocks = rows // CH
    scratch[...] = received[...].astype(F32).reshape(rows, -1)
    columns = [scratch[pl.ds(c, blocks, stride=CH), :].astype(BF16) for c in range(CH)]
    signal = jnp.concatenate(columns, axis=1)
    mixed = dot(a_fwd[...], jnp.concatenate([signal, signal], axis=0))
    width = t_re.shape[1]
    parts = []
    for c in range(CH):
        re = mixed[:blocks, c * width : (c + 1) * width]
        im = mixed[blocks:, c * width : (c + 1) * width]
        parts.append(
            jnp.concatenate(
                [re * t_re - im * t_im, re * t_im + im * t_re], axis=1
            )
        )
    high, low = high_low(jnp.concatenate(parts, axis=0))
    return dot(jnp.concatenate([high, low, high], axis=1), b_dft[...])


def inverse(product, scratch, t_re, t_im, b_dft, a_inv):
    blocks, width = t_re.shape
    high, low = high_low(product)
    back = dot(jnp.concatenate([high, low, high], axis=1), b_dft[...])
    parts = []
    for c in range(CH):
        im = back[c * blocks : (c + 1) * blocks, :width]
        re = back[c * blocks : (c + 1) * blocks, width:]
        parts.append(
            jnp.concatenate(
                [re * t_re + im * t_im, im * t_re - re * t_im], axis=0
            )
        )
    high, low = high_low(jnp.concatenate(parts, axis=1))
    result = dot(a_inv[...], jnp.concatenate([high, low, high], axis=0))
    for c in range(CH):
        scratch[pl.ds(c, blocks, stride=CH), :] = result[:, c * width : (c + 1) * width]


def local_copy(source, target, sem):
    copy = pltpu.make_async_copy(source, target, sem)
    copy.start()
    return copy


def mixer_kernel(
    qkv_hbm, taps_hbm, filt_hbm, skip_hbm, weight_hbm,
    a_fwd_hbm, t_hbm, b_dft_hbm, a_inv_hbm,
    out,
    taps, filt, skip, a_table, t_both, b_table, a_back, a_fwd, b_dft, a_inv,
    h_own, h_pair, h_send, h_recv, x_all, u_send, u_recv, y_send, y_recv, scratch,
    weight, gated, g_all, parts, landed,
    load_sem, near_send, near_recv, far_send, far_recv,
    right_send, right_recv, left_send, left_recv, g_send, g_recv, part_send, part_recv,
):
    z, xh, core = lax.axis_index("z"), lax.axis_index("xh"), lax.axis_index("core")
    y, xl = lax.axis_index("y"), lax.axis_index("xl")
    zs, ys = lax.axis_size("z"), lax.axis_size("y")
    chips = zs * 2
    per_owner = zs // (2 * ys)
    me = z * 2 + xh
    other = 1 - core
    rows = qkv_hbm.shape[1]
    half = chips * CH
    halo = 16
    mine = pl.ds(pl.multiple_of(core * half, half), half)
    theirs = pl.ds(pl.multiple_of(other * half, half), half)
    place = pl.ds(pl.multiple_of(halo + core * rows, 16), rows)
    x = xh * 2 + xl
    everyone = 8 * ys
    my_index = (x * 2 + core) * ys + y
    up, down = lax.rem(x + 1, 4), lax.rem(x + 3, 4)
    up_x = {"xh": up // 2, "xl": lax.rem(up, 2)}
    down_x = {"xh": down // 2, "xl": lax.rem(down, 2)}
    columns = weight.shape[2]

    filt_load = local_copy(filt_hbm, filt, load_sem.at[0])
    x_load = local_copy(qkv_hbm.at[:, :, mine], x_all.at[:, place, :], load_sem.at[1])
    weight_load = local_copy(
        weight_hbm.at[pl.ds(pl.multiple_of(xl * columns, columns), columns), :],
        weight.at[z, xl],
        load_sem.at[2],
    )
    small = [
        local_copy(source, target, load_sem.at[3 + k])
        for k, (source, target) in enumerate(
            [
                (taps_hbm, taps),
                (skip_hbm, skip),
                (a_fwd_hbm, a_table),
                (t_hbm, t_both),
                (b_dft_hbm, b_table),
                (a_inv_hbm, a_back),
            ]
        )
    ]

    barrier = pltpu.get_barrier_semaphore()
    step_to = lax.rem(me + jnp.where(core == 1, 1, chips - 1), chips)
    pl.semaphore_signal(
        barrier, inc=1, device_id={"z": step_to // 2, "xh": lax.rem(step_to, 2), "core": other}
    )


    def place_of(index):
        which = index // ys
        return {
            "xh": which // 4,
            "xl": lax.rem(which // 2, 2),
            "core": lax.rem(which, 2),
            "y": lax.rem(index, ys),
        }

    def greet_ctx(k, carry):
        peer = lax.rem(me + k, chips)
        pl.semaphore_signal(
            barrier, inc=1, device_id={"z": peer // 2, "xh": lax.rem(peer, 2)}
        )
        return carry

    def greet_plane(k, carry):
        pl.semaphore_signal(barrier, inc=1, device_id=place_of(lax.rem(my_index + k, everyone)))
        return carry

    lax.fori_loop(1, chips, greet_ctx, 0)
    lax.fori_loop(1, everyone, greet_plane, 0)

    filt_load.wait()
    h_own[...] = filt[...].T.reshape(2, chips, CH, rows)
    pl.semaphore_wait(barrier, 1 + chips - 1 + everyone - 1)

    my_rows = pl.ds(pl.multiple_of(core * CH, CH), CH)
    h_copy = pltpu.make_async_remote_copy(
        src_ref=h_own.at[other],
        dst_ref=h_pair.at[:, my_rows, :],
        send_sem=near_send.at[0],
        recv_sem=near_recv.at[0],
        device_id={"core": other},
    )
    h_copy.start()
    x_copy = pltpu.make_async_remote_copy(
        src_ref=qkv_hbm.at[:, :, theirs],
        dst_ref=x_all.at[:, place, :],
        send_sem=near_send.at[1],
        recv_sem=near_recv.at[1],
        device_id={"core": other},
    )
    x_copy.start()

    after = lax.rem(me + 1, chips)

    def halo_copy(target):
        return pltpu.make_async_remote_copy(
            src_ref=qkv_hbm.at[:, pl.ds(rows - halo, halo), pl.ds(target * half, half)],
            dst_ref=x_all.at[:, pl.ds(0, halo), :],
            send_sem=near_send.at[2 + target],
            recv_sem=near_recv.at[2],
            device_id={"z": after // 2, "xh": lax.rem(after, 2), "core": target},
        )

    @pl.when(core == 1)
    def _():
        halo_copy(0).start()
        halo_copy(1).start()

    swap = pltpu.make_async_remote_copy(
        src_ref=weight_hbm.at[pl.ds(pl.multiple_of((1 - xl) * columns, columns), columns), :],
        dst_ref=weight.at[z, xl],
        send_sem=near_send.at[4],
        recv_sem=near_recv.at[3],
        device_id={"xl": 1 - xl},
    )
    swap.start()
    right_steps = zs // 2
    left_steps = zs - 1 - right_steps

    def pass_on(block, step, send_sem, recv_sem, ahead):
        return pltpu.make_async_remote_copy(
            src_ref=weight.at[block],
            dst_ref=weight.at[block],
            send_sem=send_sem.at[step],
            recv_sem=recv_sem.at[step],
            device_id={"z": lax.rem(z + ahead, zs)},
        )

    def right_copy(step):
        return pass_on(lax.rem(z + zs - step, zs), step, right_send, right_recv, 1)

    def left_copy(step):
        return pass_on(lax.rem(z + step, zs), step, left_send, left_recv, zs - 1)

    def landing(step, shift, sem):
        landed_at = weight.at[lax.rem(z + shift, zs)]
        pltpu.make_async_copy(landed_at, landed_at, sem.at[step]).wait()

    def ring(step):
        if step > right_steps:
            return
        if step == 0:
            weight_load.wait()
            swap.wait_recv()
        if 0 < step <= right_steps:
            landing(step - 1, zs - step, right_recv)
        if 0 < step <= left_steps:
            landing(step - 1, step, left_recv)
        if step < right_steps:
            right_copy(step).start()
        if step < left_steps:
            left_copy(step).start()

    h_pair[:, my_rows, :] = h_own[pl.ds(core, 1)].reshape(chips, CH, rows)
    h_copy.wait_recv()
    h_send[...] = h_pair[...].astype(BF16)
    send_all(z, xh, h_send, h_recv, far_send.at[0], far_recv.at[0])
    ring(0)

    x_load.wait()
    small[0].wait()
    x_copy.wait_recv()
    halo_copy(0).wait_recv()
    features = []
    for s in range(3):
        raw = x_all[s].astype(F32)
        first = jnp.where(me == 0, 0.0, raw[:halo])
        raw = jnp.concatenate([first, raw[halo:]], axis=0)
        total = taps[s, 0:1, mine] * raw[halo:]
        for back in range(1, taps.shape[1]):
            total = total + taps[s, back : back + 1, mine] * raw[halo - back : halo - back + 2 * rows]
        features.append(total)
    query, mixed_in = features[0], features[1] * features[2]
    flipped = mixed_in.T.reshape(chips, CH, 2 * rows)
    u_send[...] = jnp.concatenate([flipped[:, :, :rows], flipped[:, :, rows:]], axis=1).astype(BF16)
    send_all(z, xh, u_send, u_recv, far_send.at[1], far_recv.at[1])
    ring(1)

    for load in small[1:]:
        load.wait()
    a_fwd[...] = jnp.concatenate(high_low(a_table[...]), axis=1)
    high, low = high_low(b_table[...])
    b_dft[...] = jnp.concatenate([high, high, low], axis=0)
    high, low = high_low(a_back[...])
    a_inv[...] = jnp.concatenate([high, high, low], axis=1)
    for group in range(4):
        wait_group(h_recv, far_recv.at[0], group)
    ring(2)
    t_re, t_im = t_both[0], t_both[1]
    h_freq = spectrum(h_recv, scratch, a_fwd, t_re, t_im, b_dft)
    for group in range(4):
        wait_group(u_recv, far_recv.at[1], group)
        if group == 1:
            ring(3)
    u_freq = spectrum(u_recv, scratch, a_fwd, t_re, t_im, b_dft)
    width = t_re.shape[1]
    h_re, h_im = h_freq[:, :width], h_freq[:, width:]
    u_re, u_im = u_freq[:, :width], u_freq[:, width:]
    product = jnp.concatenate([h_re * u_im + h_im * u_re, h_re * u_re - h_im * u_im], axis=1)
    inverse(product, scratch, t_re, t_im, b_dft, a_inv)
    y_send[...] = scratch[...].reshape(y_send.shape).astype(BF16)
    send_all(z, xh, y_send, y_recv, far_send.at[2], far_recv.at[2])
    ring(4)
    for group in range(4):
        wait_group(y_recv, far_recv.at[2], group)
        if group == 1:
            ring(5)
    back = y_recv[...].astype(F32)
    convolved = jnp.concatenate(
        [back[:, CH * b : CH * (b + 1), :].reshape(half, rows).T for b in range(2)], axis=0
    )
    across = lax.rem(x + 2, 4)

    def g_copy(kind, b, source, which, device_id):
        def at(ref):
            return ref.at[which // 2, lax.rem(which, 2), pl.ds(b * rows, rows), mine]

        return pltpu.make_async_remote_copy(
            src_ref=gated.at[pl.ds(b * rows, rows), :] if source is gated else at(source),
            dst_ref=at(g_all),
            send_sem=g_send.at[kind, b],
            recv_sem=g_recv.at[kind, b],
            device_id=device_id,
        )

    to_up = [g_copy(0, b, gated, x, up_x) for b in range(2)]
    to_down = [g_copy(1, b, gated, x, down_x) for b in range(2)]
    pass_up = [g_copy(2, b, g_all, down, up_x) for b in range(2)]
    pass_down = [g_copy(2, b, g_all, up, down_x) for b in range(2)]
    share = [g_copy(3, b, gated, x, {"core": other}) for b in range(2)]
    share_down = [g_copy(4, b, g_all, down, {"core": other}) for b in range(2)]
    share_up = [g_copy(5, b, g_all, up, {"core": other}) for b in range(2)]
    share_across = [g_copy(6, b, g_all, across, {"core": other}) for b in range(2)]
    for b in range(2):
        part = slice(b * rows, (b + 1) * rows)
        value = (query[part] * (convolved[part] + skip[:, mine] * mixed_in[part])).astype(BF16)
        gated[part, :] = value
        g_all[pl.ds(xh, 1), pl.ds(xl, 1), part, mine] = value.reshape(1, 1, rows, half)
        to_up[b].start()
        to_down[b].start()
        share[b].start()
    ring(6)
    for b in range(2):
        to_up[b].wait_recv()
        share_down[b].start()

        @pl.when(core == 0)
        def _():
            pass_up[b].start()

        to_down[b].wait_recv()
        share_up[b].start()

        @pl.when(core == 1)
        def _():
            pass_down[b].start()

    ring(7)
    for b in range(2):
        pass_up[b].wait_recv()
        share_across[b].start()
    for step in range(8, right_steps + 1):
        ring(step)
    tokens = 2 * rows
    wide = per_owner * columns

    def send(which_x, b, to_y, to_x):
        pltpu.make_async_remote_copy(
            src_ref=parts.at[which_x, b, to_y, to_x],
            dst_ref=landed.at[x * 2 + core, y],
            send_sem=part_send,
            recv_sem=part_recv.at[x * 2 + core, y],
            device_id={"xh": which_x, "xl": to_x, "core": b, "y": to_y},
        ).start()

    def compute(which_x, to_y):
        product = jnp.zeros((2 * wide, tokens), F32)
        for part in range(2):
            block = weight[pl.ds(to_y * 2 * per_owner, 2 * per_owner), part]
            right = g_all[pl.ds(which_x, 1), part].reshape(tokens, 2 * half)
            product = product + lax.dot_general(
                block.reshape(2 * wide, 2 * half),
                right,
                (((1,), (1,)), ((), ())),
                preferred_element_type=F32,
            )
        for b in range(2):
            parts[pl.ds(which_x, 1), b, pl.ds(to_y, 1)] = (
                product[:, b * rows : (b + 1) * rows]
                .astype(BF16)
                .reshape(1, 1, 2, wide, rows)
            )

    for b in range(2):
        share[b].wait_recv()
        share_down[b].wait_recv()
        share_up[b].wait_recv()

    def own_last():
        compute(xh, y)
        send(xh, core, y, 1 - xl)
        send(xh, other, y, xl)
        send(xh, other, y, 1 - xl)
        landed[pl.ds(x * 2 + core, 1), pl.ds(y, 1)] = parts[
            pl.ds(xh, 1), pl.ds(core, 1), pl.ds(y, 1), pl.ds(xl, 1)
        ].reshape(1, 1, wide, rows)

    def own_step(k, carry):
        to_y = lax.rem(y + k, ys)
        compute(xh, to_y)
        for b in range(2):
            for to_x in range(2):
                send(xh, b, to_y, to_x)
        return carry

    lax.fori_loop(1, ys, own_step, 0)
    own_last()
    for b in range(2):
        share_across[b].wait_recv()

    def far_step(k, carry):
        to_y = lax.rem(y + k, ys)
        compute(1 - xh, to_y)
        for b in range(2):
            for to_x in range(2):
                send(1 - xh, b, to_y, to_x)
        return carry

    lax.fori_loop(0, ys, far_step, 0)

    def arrived(k, carry):
        index = lax.rem(my_index + k, everyone)
        which, owner = index // ys, lax.rem(index, ys)
        block = landed.at[which, owner]
        pltpu.make_async_copy(block, block, part_recv.at[which, owner]).wait()
        return carry

    lax.fori_loop(1, everyone, arrived, 0)
    sums = []
    for which in range(8):
        total = landed[which, 0].astype(F32)
        for source in range(1, ys):
            total = total + landed[which, source].astype(F32)
        sums.append(total)
    order = [a * 4 + c * 2 + b for a in range(2) for b in range(2) for c in range(2)]
    pieces = [
        sums[which][part * columns : (part + 1) * columns]
        for part in range(per_owner)
        for which in order
    ]
    out[...] = jnp.concatenate(pieces, axis=0).T.astype(out.dtype)

    h_copy.wait_send()
    x_copy.wait_send()

    @pl.when(core == 1)
    def _():
        halo_copy(0).wait_send()
        halo_copy(1).wait_send()

    swap.wait_send()
    for step in range(right_steps):
        right_copy(step).wait_send()
    for step in range(left_steps):
        left_copy(step).wait_send()
    wait_blocks(chips - 1, h_send, far_send.at[0])
    wait_blocks(chips - 1, u_send, far_send.at[1])
    wait_blocks(chips - 1, y_send, far_send.at[2])
    for group in (to_up, to_down, pass_up, share, share_down, share_up, share_across):
        for copy in group:
            copy.wait_send()
    pltpu.make_async_copy(parts.at[1], parts.at[1], part_send).wait()
    pltpu.make_async_copy(parts.at[0, 1], parts.at[0, 1], part_send).wait()
    pltpu.make_async_copy(parts.at[0, 0, 0, 0], parts.at[0, 0, 0, 0], part_send).wait()
    if ys > 1:
        sent = parts.at[0, 0, pl.ds(1, ys - 1)]
        pltpu.make_async_copy(sent, sent, part_send).wait()


def body(qkv_in, short_taps, long_filter, skip_gain, out_weight):
    rows, _, channels = qkv_in.shape
    half = channels // 2
    zs = lax.axis_size("z")
    chips = zs * 2
    ys = lax.axis_size("y")
    blocks = 2 * chips
    columns = out_weight.shape[1] // 2
    wide = zs // (2 * ys) * columns
    lookup = tables(blocks, rows)
    exchange = (chips, 2 * CH, rows)
    dma = pltpu.SemaphoreType.DMA
    return pl.pallas_call(
        mixer_kernel,
        out_shape=jax.ShapeDtypeStruct((rows, channels), BF16),
        in_specs=[pl.BlockSpec(memory_space=pl.ANY)] * 9,
        out_specs=VMEM,
        scratch_shapes=[
            pltpu.VMEM(short_taps.shape, F32),
            pltpu.VMEM((rows, channels), F32),
            pltpu.VMEM((1, channels), F32),
            *[pltpu.VMEM(table.shape, table.dtype) for table in lookup],
            pltpu.VMEM((2 * blocks, 2 * blocks), BF16),
            pltpu.VMEM((6 * rows, 2 * rows), BF16),
            pltpu.VMEM((blocks, 6 * blocks), BF16),
            pltpu.VMEM((2, chips, CH, rows), F32),
            pltpu.VMEM(exchange, F32),
            pltpu.VMEM(exchange, BF16),
            pltpu.VMEM(exchange, BF16),
            pltpu.VMEM((3, 16 + 2 * rows, half), BF16),
            pltpu.VMEM(exchange, BF16),
            pltpu.VMEM(exchange, BF16),
            pltpu.VMEM(exchange, BF16),
            pltpu.VMEM(exchange, BF16),
            pltpu.VMEM((blocks * CH, rows), F32),
            pltpu.VMEM((zs, 2, columns, channels), BF16),
            pltpu.VMEM((2 * rows, half), BF16),
            pltpu.VMEM((2, 2, 2 * rows, channels), BF16),
            pltpu.VMEM((2, 2, ys, 2, wide, rows), BF16),
            pltpu.VMEM((8, ys, wide, rows), BF16),
            dma((9,)),
            dma((5,)),
            dma((4,)),
            dma((3,)),
            dma((3, 4)),
            dma((zs,)),
            dma((zs,)),
            dma((zs,)),
            dma((zs,)),
            dma((7, 2)),
            dma((7, 2)),
            dma,
            dma((8, ys)),
        ],
        compiler_params=pltpu.CompilerParams(
            collective_id=0, has_side_effects=True, vmem_limit_bytes=60 * 2**20
        ),
        name="mixer",
    )(
        qkv_in.transpose(1, 0, 2),
        short_taps,
        long_filter,
        skip_gain[None, :],
        out_weight.T,
        *lookup,
    )


def solution(mesh):
    sizes = dict(mesh.shape)
    split = Mesh(
        mesh.devices.reshape(sizes["ctx"] // 4, 2, 2, sizes["tp"] // 2, 2),
        ("z", "xh", "core", "y", "xl"),
    )
    ctx, tp = ("z", "xh", "core"), ("y", "xl")
    return jax.shard_map(
        body,
        mesh=split,
        in_specs=(P(ctx, None, tp), P(None, None, tp), P(ctx, tp), P(tp), P(tp, ctx)),
        out_specs=P(ctx, tp),
        check_vma=False,
    )
```

```python
import jax
import jax.numpy as jnp
import numpy as np
from jax import lax
from jax.experimental import pallas as pl
from jax.experimental.pallas import tpu as pltpu
from jax.sharding import Mesh, PartitionSpec as P

F32 = jnp.float32
BF16 = jnp.bfloat16
CH = 8
VMEM = pl.BlockSpec(memory_space=pltpu.VMEM)


def tables(blocks, width):
    length = blocks * width
    f1 = np.arange(blocks)[:, None]
    a = np.exp(-2j * np.pi * ((np.arange(blocks)[None, :] * (4 * f1 + 1)) % (4 * blocks)) / (4 * blocks))
    t = np.exp(-2j * np.pi * (np.arange(width)[None, :] * (4 * f1 + 1)) / (4 * length))
    i = np.arange(width)
    b = np.exp(-2j * np.pi * ((i[:, None] * i[None, :]) % width) / width)
    found = (
        np.concatenate([a.real, a.imag], 0),
        np.stack([t.real, t.imag]),
        np.block([[b.real, b.imag], [-b.imag, b.real]]),
        np.concatenate([a.real.T, a.imag.T], 1) / length,
    )
    return [jnp.asarray(table.astype(np.float32)) for table in found]


def dot(left, right):
    return jnp.dot(left, right, preferred_element_type=F32)


def high_low(value):
    high = value.astype(BF16)
    return high, (value - high.astype(F32)).astype(BF16)


def send_all(z, xh, source, target, send_sem, recv_sems, by_turn=False):
    zs = lax.axis_size("z")
    me = z * 2 + xh
    size = 2 * zs // recv_sems.shape[0]

    def step(k, carry):
        turn = k // 2
        ahead = zs // 2 + jnp.where(lax.rem(turn, 2) == 1, -((turn + 1) // 2), turn // 2)
        to_z = lax.rem(z + ahead, zs)
        to_x = jnp.where(lax.rem(k, 2) == 0, 1 - xh, xh)
        pltpu.make_async_remote_copy(
            src_ref=source.at[to_z * 2 + to_x],
            dst_ref=target.at[turn * 2 + xh if by_turn else me],
            send_sem=send_sem,
            recv_sem=recv_sems.at[k // size],
            device_id={"z": to_z, "xh": to_x},
        ).start()
        return carry

    lax.fori_loop(0, 2 * zs - 1, step, 0)
    slot = (zs - 1) * 2 + xh if by_turn else me
    target[pl.ds(slot, 1)] = source[pl.ds(me, 1)]


def wait_blocks(count, ref, sem):
    part = ref.at[pl.ds(0, count)]
    pltpu.make_async_copy(part, part, sem).wait()


def wait_group(ref, sems, group):
    size = ref.shape[0] // sems.shape[0]
    wait_blocks(size - (group == sems.shape[0] - 1), ref, sems.at[group])


def spectrum(received, scratch, a_fwd, t_re, t_im, b_dft):
    rows = scratch.shape[0]
    blocks = rows // CH
    scratch[...] = received[...].astype(F32).reshape(rows, -1)
    columns = [scratch[pl.ds(c, blocks, stride=CH), :].astype(BF16) for c in range(CH)]
    signal = jnp.concatenate(columns, axis=1)
    mixed = dot(a_fwd[...], jnp.concatenate([signal, signal], axis=0))
    width = t_re.shape[1]
    parts = []
    for c in range(CH):
        re = mixed[:blocks, c * width : (c + 1) * width]
        im = mixed[blocks:, c * width : (c + 1) * width]
        parts.append(
            jnp.concatenate(
                [re * t_re - im * t_im, re * t_im + im * t_re], axis=1
            )
        )
    high, low = high_low(jnp.concatenate(parts, axis=0))
    return dot(jnp.concatenate([high, low, high], axis=1), b_dft[...])


def inverse(product, scratch, t_re, t_im, b_dft, a_inv):
    blocks, width = t_re.shape
    high, low = high_low(product)
    back = dot(jnp.concatenate([high, low, high], axis=1), b_dft[...])
    parts = []
    for c in range(CH):
        im = back[c * blocks : (c + 1) * blocks, :width]
        re = back[c * blocks : (c + 1) * blocks, width:]
        parts.append(
            jnp.concatenate(
                [re * t_re + im * t_im, im * t_re - re * t_im], axis=0
            )
        )
    high, low = high_low(jnp.concatenate(parts, axis=1))
    result = dot(a_inv[...], jnp.concatenate([high, low, high], axis=0))
    for c in range(CH):
        scratch[pl.ds(c, blocks, stride=CH), :] = result[:, c * width : (c + 1) * width]


def local_copy(source, target, sem):
    copy = pltpu.make_async_copy(source, target, sem)
    copy.start()
    return copy


def mixer_kernel(
    qkv_hbm, taps_hbm, filt_hbm, skip_hbm, weight_hbm,
    a_fwd_hbm, t_hbm, b_dft_hbm, a_inv_hbm,
    out,
    taps, filt, skip, a_table, t_both, b_table, a_back, a_fwd, b_dft, a_inv,
    h_own, h_pair, h_send, h_recv, x_all, u_send, u_recv, y_send, y_recv, scratch,
    weight, query_t, skip_t, g_all, g_ordered, parts, landed,
    load_sem, near_send, near_recv, far_send, far_recv,
    right_send, right_recv, left_send, left_recv, g_send, g_recv, part_send, part_recv,
):
    z, xh, core = lax.axis_index("z"), lax.axis_index("xh"), lax.axis_index("core")
    y, xl = lax.axis_index("y"), lax.axis_index("xl")
    zs, ys = lax.axis_size("z"), lax.axis_size("y")
    chips = zs * 2
    per_owner = zs // (2 * ys)
    me = z * 2 + xh
    other = 1 - core
    rows = qkv_hbm.shape[1]
    half = chips * CH
    halo = 16
    mine = pl.ds(pl.multiple_of(core * half, half), half)
    theirs = pl.ds(pl.multiple_of(other * half, half), half)
    place = pl.ds(pl.multiple_of(halo + core * rows, 16), rows)
    x = xh * 2 + xl
    everyone = 8 * ys
    my_index = (x * 2 + core) * ys + y
    up, down = lax.rem(x + 1, 4), lax.rem(x + 3, 4)
    up_x = {"xh": up // 2, "xl": lax.rem(up, 2)}
    down_x = {"xh": down // 2, "xl": lax.rem(down, 2)}
    columns = weight.shape[2]

    filt_load = local_copy(filt_hbm, filt, load_sem.at[0])
    x_load = local_copy(qkv_hbm.at[:, :, mine], x_all.at[:, place, :], load_sem.at[1])
    weight_load = local_copy(
        weight_hbm.at[pl.ds(pl.multiple_of(xl * columns, columns), columns), :],
        weight.at[z, xl],
        load_sem.at[2],
    )
    small = [
        local_copy(source, target, load_sem.at[3 + k])
        for k, (source, target) in enumerate(
            [
                (taps_hbm, taps),
                (skip_hbm, skip),
                (a_fwd_hbm, a_table),
                (t_hbm, t_both),
                (b_dft_hbm, b_table),
                (a_inv_hbm, a_back),
            ]
        )
    ]

    barrier = pltpu.get_barrier_semaphore()
    step_to = lax.rem(me + jnp.where(core == 1, 1, chips - 1), chips)
    pl.semaphore_signal(
        barrier, inc=1, device_id={"z": step_to // 2, "xh": lax.rem(step_to, 2), "core": other}
    )


    def place_of(index):
        which = index // ys
        return {
            "xh": which // 4,
            "xl": lax.rem(which // 2, 2),
            "core": lax.rem(which, 2),
            "y": lax.rem(index, ys),
        }

    def greet_ctx(k, carry):
        peer = lax.rem(me + k, chips)
        pl.semaphore_signal(
            barrier, inc=1, device_id={"z": peer // 2, "xh": lax.rem(peer, 2)}
        )
        return carry

    def greet_plane(k, carry):
        pl.semaphore_signal(barrier, inc=1, device_id=place_of(lax.rem(my_index + k, everyone)))
        return carry

    lax.fori_loop(1, chips, greet_ctx, 0)
    lax.fori_loop(1, everyone, greet_plane, 0)

    filt_load.wait()
    h_own[...] = filt[...].T.reshape(2, chips, CH, rows)
    pl.semaphore_wait(barrier, 1 + chips - 1 + everyone - 1)

    my_rows = pl.ds(pl.multiple_of(core * CH, CH), CH)
    h_copy = pltpu.make_async_remote_copy(
        src_ref=h_own.at[other],
        dst_ref=h_pair.at[:, my_rows, :],
        send_sem=near_send.at[0],
        recv_sem=near_recv.at[0],
        device_id={"core": other},
    )
    h_copy.start()
    x_copy = pltpu.make_async_remote_copy(
        src_ref=qkv_hbm.at[:, :, theirs],
        dst_ref=x_all.at[:, place, :],
        send_sem=near_send.at[1],
        recv_sem=near_recv.at[1],
        device_id={"core": other},
    )
    x_copy.start()

    after = lax.rem(me + 1, chips)

    def halo_copy(target):
        return pltpu.make_async_remote_copy(
            src_ref=qkv_hbm.at[:, pl.ds(rows - halo, halo), pl.ds(target * half, half)],
            dst_ref=x_all.at[:, pl.ds(0, halo), :],
            send_sem=near_send.at[2 + target],
            recv_sem=near_recv.at[2],
            device_id={"z": after // 2, "xh": lax.rem(after, 2), "core": target},
        )

    @pl.when(core == 1)
    def _():
        halo_copy(0).start()
        halo_copy(1).start()

    swap = pltpu.make_async_remote_copy(
        src_ref=weight_hbm.at[pl.ds(pl.multiple_of((1 - xl) * columns, columns), columns), :],
        dst_ref=weight.at[z, xl],
        send_sem=near_send.at[4],
        recv_sem=near_recv.at[3],
        device_id={"xl": 1 - xl},
    )
    swap.start()
    right_steps = zs // 2
    left_steps = zs - 1 - right_steps

    def pass_on(block, step, send_sem, recv_sem, ahead):
        return pltpu.make_async_remote_copy(
            src_ref=weight.at[block],
            dst_ref=weight.at[block],
            send_sem=send_sem.at[step],
            recv_sem=recv_sem.at[step],
            device_id={"z": lax.rem(z + ahead, zs)},
        )

    def right_copy(step):
        return pass_on(lax.rem(z + zs - step, zs), step, right_send, right_recv, 1)

    def left_copy(step):
        return pass_on(lax.rem(z + step, zs), step, left_send, left_recv, zs - 1)

    def landing(step, shift, sem):
        landed_at = weight.at[lax.rem(z + shift, zs)]
        pltpu.make_async_copy(landed_at, landed_at, sem.at[step]).wait()

    def ring(step):
        if step > right_steps:
            return
        if step == 0:
            weight_load.wait()
            swap.wait_recv()
        if 0 < step <= right_steps:
            landing(step - 1, zs - step, right_recv)
        if 0 < step <= left_steps:
            landing(step - 1, step, left_recv)
        if step < right_steps:
            right_copy(step).start()
        if step < left_steps:
            left_copy(step).start()

    h_pair[:, my_rows, :] = h_own[pl.ds(core, 1)].reshape(chips, CH, rows)
    h_copy.wait_recv()
    h_send[...] = h_pair[...].astype(BF16)
    send_all(z, xh, h_send, h_recv, far_send.at[0], far_recv.at[0])
    ring(0)

    x_load.wait()
    small[0].wait()
    small[1].wait()
    x_copy.wait_recv()
    halo_copy(0).wait_recv()
    features = []
    for s in range(3):
        raw = x_all[s].astype(F32)
        first = jnp.where(me == 0, 0.0, raw[:halo])
        raw = jnp.concatenate([first, raw[halo:]], axis=0)
        total = taps[s, 0:1, mine] * raw[halo:]
        for back in range(1, taps.shape[1]):
            total = total + taps[s, back : back + 1, mine] * raw[halo - back : halo - back + 2 * rows]
        features.append(total)
    query, mixed_in = features[0], features[1] * features[2]
    flipped = mixed_in.T.reshape(chips, CH, 2 * rows)
    u_send[...] = jnp.concatenate([flipped[:, :, :rows], flipped[:, :, rows:]], axis=1).astype(BF16)
    send_all(z, xh, u_send, u_recv, far_send.at[1], far_recv.at[1])
    ring(1)
    query_t[...] = query.T
    skip_t[...] = (skip[:, mine] * mixed_in).T

    for load in small[2:]:
        load.wait()
    a_fwd[...] = jnp.concatenate(high_low(a_table[...]), axis=1)
    high, low = high_low(b_table[...])
    b_dft[...] = jnp.concatenate([high, high, low], axis=0)
    high, low = high_low(a_back[...])
    a_inv[...] = jnp.concatenate([high, high, low], axis=1)
    for group in range(4):
        wait_group(h_recv, far_recv.at[0], group)
    ring(2)
    t_re, t_im = t_both[0], t_both[1]
    h_freq = spectrum(h_recv, scratch, a_fwd, t_re, t_im, b_dft)
    for group in range(4):
        wait_group(u_recv, far_recv.at[1], group)
        if group == 1:
            ring(3)
    u_freq = spectrum(u_recv, scratch, a_fwd, t_re, t_im, b_dft)
    width = t_re.shape[1]
    h_re, h_im = h_freq[:, :width], h_freq[:, width:]
    u_re, u_im = u_freq[:, :width], u_freq[:, width:]
    product = jnp.concatenate([h_re * u_im + h_im * u_re, h_re * u_re - h_im * u_im], axis=1)
    inverse(product, scratch, t_re, t_im, b_dft, a_inv)
    y_send[...] = scratch[...].reshape(y_send.shape).astype(BF16)
    send_all(z, xh, y_send, y_recv, far_send.at[2], far_recv.at[2], by_turn=True)
    ring(4)

    tokens = 2 * rows
    turns = zs // 4
    pairs = 2 * CH
    across = lax.rem(x + 2, 4)

    def g_copy(kind, group, which, device_id):
        part = g_all.at[which // 2, lax.rem(which, 2), core, pl.ds(group * turns, turns)]
        return pltpu.make_async_remote_copy(
            src_ref=part,
            dst_ref=part,
            send_sem=g_send.at[kind, group],
            recv_sem=g_recv.at[kind, group],
            device_id=device_id,
        )

    def g_copies(kind, which, device_id):
        return [g_copy(kind, group, which, device_id) for group in range(4)]

    to_across = g_copies(0, x, {"xh": 1 - xh})
    to_up = g_copies(1, x, up_x)
    to_down = g_copies(2, x, down_x)
    share = g_copies(3, x, {"core": other})
    share_across = g_copies(4, across, {"core": other})
    share_down = g_copies(5, down, {"core": other})
    share_up = g_copies(6, up, {"core": other})
    for group in range(4):
        wait_group(y_recv, far_recv.at[2], group)
        for turn in range(group * turns, (group + 1) * turns):
            ahead = zs // 2 + (-((turn + 1) // 2) if turn % 2 else turn // 2)
            source = pl.ds(pl.multiple_of(lax.rem(z + zs - ahead, zs) * pairs, pairs), pairs)
            back = y_recv[pl.ds(2 * turn, 2)].astype(F32)
            convolved = jnp.concatenate(
                [back[:, CH * b : CH * (b + 1), :].reshape(pairs, rows) for b in range(2)], axis=1
            )
            value = query_t[source, :] * (convolved + skip_t[source, :])
            g_all[pl.ds(xh, 1), pl.ds(xl, 1), pl.ds(core, 1), turn] = value.astype(BF16).reshape(
                1, 1, 1, pairs, tokens
            )
        to_across[group].start()
        to_up[group].start()
        to_down[group].start()
        share[group].start()
        if group == 1:
            ring(5)
    ring(6)
    for group in range(4):
        to_up[group].wait_recv()
        share_down[group].start()
        to_down[group].wait_recv()
        share_up[group].start()
        to_across[group].wait_recv()
        share_across[group].start()

    owners = 2 * ys
    owner_me = y * 2 + xl
    wide = per_owner * columns

    def order(which_x):
        for part in range(2):
            for c in range(2):
                for block in range(zs):
                    shift = lax.rem(z + zs - block, zs) - zs // 2
                    turn = jnp.where(shift < 0, -2 * shift - 1, 2 * shift)
                    start = c * half + block * pairs
                    g_ordered[which_x, part, start : start + pairs, :] = g_all[
                        which_x, part, c, pl.ds(turn, 1)
                    ].reshape(pairs, tokens)

    def compute(which_x, to):
        product = jnp.zeros((wide, tokens), F32)
        for part in range(2):
            block = weight[pl.ds(to * per_owner, per_owner), part].reshape(wide, 2 * half)
            right = g_ordered[pl.ds(which_x, 1), part].reshape(2 * half, tokens)
            product = product + dot(block, right)
        for b in range(2):
            parts[pl.ds(which_x, 1), b, pl.ds(to, 1)] = (
                product[:, b * rows : (b + 1) * rows].astype(BF16).reshape(1, 1, wide, rows)
            )

    def send(which_x, b, to):
        pltpu.make_async_remote_copy(
            src_ref=parts.at[which_x, b, to],
            dst_ref=landed.at[x * 2 + core, y],
            send_sem=part_send,
            recv_sem=part_recv.at[x * 2 + core, y],
            device_id={"xh": which_x, "xl": lax.rem(to, 2), "core": b, "y": to // 2},
        ).start()

    def project(which_x, first, count):
        def step(k, carry):
            to = lax.rem(z // per_owner + owners + first + lax.rem(k + y, count), owners)
            compute(which_x, to)
            for b in range(2):
                stays = (which_x == xh) & (b == core) & (to == owner_me)

                @pl.when(jnp.logical_not(stays))
                def _():
                    send(which_x, b, to)

                @pl.when(stays)
                def _():
                    landed[pl.ds(x * 2 + core, 1), pl.ds(y, 1)] = parts[
                        pl.ds(which_x, 1), b, pl.ds(to, 1)
                    ].reshape(1, 1, wide, rows)

            return carry

        lax.fori_loop(0, count, step, 0)

    near = min(5, owners)
    for group in range(4):
        for copy in (share, share_down, share_up, share_across):
            copy[group].wait_recv()
    order(0)
    order(1)
    project(1 - xh, -(near // 2), near)
    project(xh, -(near // 2), near)
    ring(7)
    for step in range(8, right_steps + 1):
        ring(step)
    if near < owners:
        project(1 - xh, near - near // 2, owners - near)
        project(xh, near - near // 2, owners - near)

    def arrived(k, carry):
        index = lax.rem(my_index + k, everyone)
        which, owner = index // ys, lax.rem(index, ys)
        block = landed.at[which, owner]
        pltpu.make_async_copy(block, block, part_recv.at[which, owner]).wait()
        return carry

    lax.fori_loop(1, everyone, arrived, 0)
    sums = []
    for which in range(8):
        total = landed[which, 0].astype(F32)
        for source in range(1, ys):
            total = total + landed[which, source].astype(F32)
        sums.append(total)
    order = [a * 4 + c * 2 + b for a in range(2) for b in range(2) for c in range(2)]
    pieces = [
        sums[which][part * columns : (part + 1) * columns]
        for part in range(per_owner)
        for which in order
    ]
    out[...] = jnp.concatenate(pieces, axis=0).T.astype(out.dtype)

    h_copy.wait_send()
    x_copy.wait_send()

    @pl.when(core == 1)
    def _():
        halo_copy(0).wait_send()
        halo_copy(1).wait_send()

    swap.wait_send()
    for step in range(right_steps):
        right_copy(step).wait_send()
    for step in range(left_steps):
        left_copy(step).wait_send()
    wait_blocks(chips - 1, h_send, far_send.at[0])
    wait_blocks(chips - 1, u_send, far_send.at[1])
    wait_blocks(chips - 1, y_send, far_send.at[2])
    for group in (to_across, to_up, to_down, share, share_across, share_down, share_up):
        for copy in group:
            copy.wait_send()
    pltpu.make_async_copy(parts.at[1], parts.at[1], part_send).wait()
    pltpu.make_async_copy(parts.at[0, 1], parts.at[0, 1], part_send).wait()
    sent = parts.at[0, 0, pl.ds(1, owners - 1)]
    pltpu.make_async_copy(sent, sent, part_send).wait()


def body(qkv_in, short_taps, long_filter, skip_gain, out_weight):
    rows, _, channels = qkv_in.shape
    half = channels // 2
    zs = lax.axis_size("z")
    chips = zs * 2
    ys = lax.axis_size("y")
    blocks = 2 * chips
    columns = out_weight.shape[1] // 2
    wide = zs // (2 * ys) * columns
    lookup = tables(blocks, rows)
    exchange = (chips, 2 * CH, rows)
    dma = pltpu.SemaphoreType.DMA
    return pl.pallas_call(
        mixer_kernel,
        out_shape=jax.ShapeDtypeStruct((rows, channels), BF16),
        in_specs=[pl.BlockSpec(memory_space=pl.ANY)] * 9,
        out_specs=VMEM,
        scratch_shapes=[
            pltpu.VMEM(short_taps.shape, F32),
            pltpu.VMEM((rows, channels), F32),
            pltpu.VMEM((1, channels), F32),
            *[pltpu.VMEM(table.shape, table.dtype) for table in lookup],
            pltpu.VMEM((2 * blocks, 2 * blocks), BF16),
            pltpu.VMEM((6 * rows, 2 * rows), BF16),
            pltpu.VMEM((blocks, 6 * blocks), BF16),
            pltpu.VMEM((2, chips, CH, rows), F32),
            pltpu.VMEM(exchange, F32),
            pltpu.VMEM(exchange, BF16),
            pltpu.VMEM(exchange, BF16),
            pltpu.VMEM((3, 16 + 2 * rows, half), BF16),
            pltpu.VMEM(exchange, BF16),
            pltpu.VMEM(exchange, BF16),
            pltpu.VMEM(exchange, BF16),
            pltpu.VMEM(exchange, BF16),
            pltpu.VMEM((blocks * CH, rows), F32),
            pltpu.VMEM((zs, 2, columns, channels), BF16),
            pltpu.VMEM((half, 2 * rows), F32),
            pltpu.VMEM((half, 2 * rows), F32),
            pltpu.VMEM((2, 2, 2, zs, 2 * CH, 2 * rows), BF16),
            pltpu.VMEM((2, 2, channels, 2 * rows), BF16),
            pltpu.VMEM((2, 2, 2 * ys, wide, rows), BF16),
            pltpu.VMEM((8, ys, wide, rows), BF16),
            dma((9,)),
            dma((5,)),
            dma((4,)),
            dma((3,)),
            dma((3, 4)),
            dma((zs,)),
            dma((zs,)),
            dma((zs,)),
            dma((zs,)),
            dma((7, 4)),
            dma((7, 4)),
            dma,
            dma((8, ys)),
        ],
        compiler_params=pltpu.CompilerParams(
            collective_id=0, has_side_effects=True, vmem_limit_bytes=60 * 2**20
        ),
        name="mixer",
    )(
        qkv_in.transpose(1, 0, 2),
        short_taps,
        long_filter,
        skip_gain[None, :],
        out_weight.T,
        *lookup,
    )


def solution(mesh):
    sizes = dict(mesh.shape)
    split = Mesh(
        mesh.devices.reshape(sizes["ctx"] // 4, 2, 2, sizes["tp"] // 2, 2),
        ("z", "xh", "core", "y", "xl"),
    )
    ctx, tp = ("z", "xh", "core"), ("y", "xl")
    return jax.shard_map(
        body,
        mesh=split,
        in_specs=(P(ctx, None, tp), P(None, None, tp), P(ctx, tp), P(tp), P(tp, ctx)),
        out_specs=P(ctx, tp),
        check_vma=False,
    )
```

```python
import jax
import jax.numpy as jnp
import numpy as np
from jax import lax
from jax.experimental import pallas as pl
from jax.experimental.pallas import tpu as pltpu
from jax.sharding import Mesh, PartitionSpec as P

F32 = jnp.float32
BF16 = jnp.bfloat16
CH = 8
VMEM = pl.BlockSpec(memory_space=pltpu.VMEM)


def tables(blocks, width):
    length = blocks * width
    f1 = np.arange(blocks)[:, None]
    a = np.exp(-2j * np.pi * ((np.arange(blocks)[None, :] * (4 * f1 + 1)) % (4 * blocks)) / (4 * blocks))
    t = np.exp(-2j * np.pi * (np.arange(width)[None, :] * (4 * f1 + 1)) / (4 * length))
    i = np.arange(width)
    b = np.exp(-2j * np.pi * ((i[:, None] * i[None, :]) % width) / width)
    found = (
        np.concatenate([a.real, a.imag], 0),
        np.stack([t.real, t.imag]),
        np.block([[b.real, b.imag], [-b.imag, b.real]]),
        np.concatenate([a.real.T, a.imag.T], 1) / length,
    )
    return [jnp.asarray(table.astype(np.float32)) for table in found]


def dot(left, right):
    return jnp.dot(left, right, preferred_element_type=F32)


def high_low(value):
    high = value.astype(BF16)
    return high, (value - high.astype(F32)).astype(BF16)


def send_all(z, xh, source, target, send_sem, recv_sems, by_turn=False):
    zs = lax.axis_size("z")
    me = z * 2 + xh
    size = 2 * zs // recv_sems.shape[0]

    def step(k, carry):
        turn = k // 2
        ahead = zs // 2 + jnp.where(lax.rem(turn, 2) == 1, -((turn + 1) // 2), turn // 2)
        to_z = lax.rem(z + ahead, zs)
        to_x = jnp.where(lax.rem(k, 2) == 0, 1 - xh, xh)
        pltpu.make_async_remote_copy(
            src_ref=source.at[to_z * 2 + to_x],
            dst_ref=target.at[turn * 2 + xh if by_turn else me],
            send_sem=send_sem,
            recv_sem=recv_sems.at[k // size],
            device_id={"z": to_z, "xh": to_x},
        ).start()
        return carry

    lax.fori_loop(0, 2 * zs - 1, step, 0)
    slot = (zs - 1) * 2 + xh if by_turn else me
    target[pl.ds(slot, 1)] = source[pl.ds(me, 1)]


def wait_blocks(count, ref, sem):
    part = ref.at[pl.ds(0, count)]
    pltpu.make_async_copy(part, part, sem).wait()


def wait_group(ref, sems, group):
    size = ref.shape[0] // sems.shape[0]
    wait_blocks(size - (group == sems.shape[0] - 1), ref, sems.at[group])


def spectrum(received, scratch, a_fwd, t_re, t_im, b_dft):
    rows = scratch.shape[0]
    blocks = rows // CH
    scratch[...] = received[...].astype(F32).reshape(rows, -1)
    columns = [scratch[pl.ds(c, blocks, stride=CH), :].astype(BF16) for c in range(CH)]
    signal = jnp.concatenate(columns, axis=1)
    mixed = dot(a_fwd[...], jnp.concatenate([signal, signal], axis=0))
    width = t_re.shape[1]
    parts = []
    for c in range(CH):
        re = mixed[:blocks, c * width : (c + 1) * width]
        im = mixed[blocks:, c * width : (c + 1) * width]
        parts.append(
            jnp.concatenate(
                [re * t_re - im * t_im, re * t_im + im * t_re], axis=1
            )
        )
    high, low = high_low(jnp.concatenate(parts, axis=0))
    return dot(jnp.concatenate([high, low, high], axis=1), b_dft[...])


def inverse(product, scratch, t_re, t_im, b_dft, a_inv):
    blocks, width = t_re.shape
    high, low = high_low(product)
    back = dot(jnp.concatenate([high, low, high], axis=1), b_dft[...])
    parts = []
    for c in range(CH):
        im = back[c * blocks : (c + 1) * blocks, :width]
        re = back[c * blocks : (c + 1) * blocks, width:]
        parts.append(
            jnp.concatenate(
                [re * t_re + im * t_im, im * t_re - re * t_im], axis=0
            )
        )
    high, low = high_low(jnp.concatenate(parts, axis=1))
    result = dot(a_inv[...], jnp.concatenate([high, low, high], axis=0))
    for c in range(CH):
        scratch[pl.ds(c, blocks, stride=CH), :] = result[:, c * width : (c + 1) * width]


def local_copy(source, target, sem):
    copy = pltpu.make_async_copy(source, target, sem)
    copy.start()
    return copy


def mixer_kernel(
    qkv_hbm, taps_hbm, filt_hbm, skip_hbm, weight_hbm,
    a_fwd_hbm, t_hbm, b_dft_hbm, a_inv_hbm,
    out,
    taps, filt, skip, a_table, t_both, b_table, a_back, a_fwd, b_dft, a_inv,
    h_own, h_pair, h_send, h_recv, x_all, u_send, u_recv, y_send, y_recv, scratch,
    weight, query_t, skip_t, g_all, g_ordered, parts, landed,
    load_sem, near_send, near_recv, far_send, far_recv,
    right_send, right_recv, left_send, left_recv, g_send, g_recv, part_send, part_recv,
):
    z, xh, core = lax.axis_index("z"), lax.axis_index("xh"), lax.axis_index("core")
    y, xl = lax.axis_index("y"), lax.axis_index("xl")
    zs, ys = lax.axis_size("z"), lax.axis_size("y")
    chips = zs * 2
    per_owner = zs // (2 * ys)
    me = z * 2 + xh
    other = 1 - core
    rows = qkv_hbm.shape[1]
    half = chips * CH
    halo = 16
    mine = pl.ds(pl.multiple_of(core * half, half), half)
    theirs = pl.ds(pl.multiple_of(other * half, half), half)
    place = pl.ds(pl.multiple_of(halo + core * rows, 16), rows)
    x = xh * 2 + xl
    everyone = 8 * ys
    my_index = (x * 2 + core) * ys + y
    up, down = lax.rem(x + 1, 4), lax.rem(x + 3, 4)
    up_x = {"xh": up // 2, "xl": lax.rem(up, 2)}
    down_x = {"xh": down // 2, "xl": lax.rem(down, 2)}
    columns = weight.shape[2]

    filt_load = local_copy(filt_hbm, filt, load_sem.at[0])
    x_load = local_copy(qkv_hbm.at[:, :, mine], x_all.at[:, place, :], load_sem.at[1])
    weight_load = local_copy(
        weight_hbm.at[pl.ds(pl.multiple_of(xl * columns, columns), columns), :],
        weight.at[z, xl],
        load_sem.at[2],
    )
    small = [
        local_copy(source, target, load_sem.at[3 + k])
        for k, (source, target) in enumerate(
            [
                (taps_hbm, taps),
                (skip_hbm, skip),
                (a_fwd_hbm, a_table),
                (t_hbm, t_both),
                (b_dft_hbm, b_table),
                (a_inv_hbm, a_back),
            ]
        )
    ]

    barrier = pltpu.get_barrier_semaphore()
    step_to = lax.rem(me + jnp.where(core == 1, 1, chips - 1), chips)
    pl.semaphore_signal(
        barrier, inc=1, device_id={"z": step_to // 2, "xh": lax.rem(step_to, 2), "core": other}
    )


    def place_of(index):
        which = index // ys
        return {
            "xh": which // 4,
            "xl": lax.rem(which // 2, 2),
            "core": lax.rem(which, 2),
            "y": lax.rem(index, ys),
        }

    def greet_ctx(k, carry):
        peer = lax.rem(me + k, chips)
        pl.semaphore_signal(
            barrier, inc=1, device_id={"z": peer // 2, "xh": lax.rem(peer, 2)}
        )
        return carry

    def greet_plane(k, carry):
        pl.semaphore_signal(barrier, inc=1, device_id=place_of(lax.rem(my_index + k, everyone)))
        return carry

    lax.fori_loop(1, chips, greet_ctx, 0)
    lax.fori_loop(1, everyone, greet_plane, 0)

    filt_load.wait()
    h_own[...] = filt[...].T.reshape(2, chips, CH, rows)
    pl.semaphore_wait(barrier, 1 + chips - 1 + everyone - 1)

    my_rows = pl.ds(pl.multiple_of(core * CH, CH), CH)
    h_copy = pltpu.make_async_remote_copy(
        src_ref=h_own.at[other],
        dst_ref=h_pair.at[:, my_rows, :],
        send_sem=near_send.at[0],
        recv_sem=near_recv.at[0],
        device_id={"core": other},
    )
    h_copy.start()
    x_copy = pltpu.make_async_remote_copy(
        src_ref=qkv_hbm.at[:, :, theirs],
        dst_ref=x_all.at[:, place, :],
        send_sem=near_send.at[1],
        recv_sem=near_recv.at[1],
        device_id={"core": other},
    )
    x_copy.start()

    after = lax.rem(me + 1, chips)

    def halo_copy(target):
        return pltpu.make_async_remote_copy(
            src_ref=qkv_hbm.at[:, pl.ds(rows - halo, halo), pl.ds(target * half, half)],
            dst_ref=x_all.at[:, pl.ds(0, halo), :],
            send_sem=near_send.at[2 + target],
            recv_sem=near_recv.at[2],
            device_id={"z": after // 2, "xh": lax.rem(after, 2), "core": target},
        )

    @pl.when(core == 1)
    def _():
        halo_copy(0).start()
        halo_copy(1).start()

    swap = pltpu.make_async_remote_copy(
        src_ref=weight_hbm.at[pl.ds(pl.multiple_of((1 - xl) * columns, columns), columns), :],
        dst_ref=weight.at[z, xl],
        send_sem=near_send.at[4],
        recv_sem=near_recv.at[3],
        device_id={"xl": 1 - xl},
    )
    swap.start()
    right_steps = zs // 2
    left_steps = zs - 1 - right_steps

    def pass_on(block, lane, step, send_sem, recv_sem, ahead):
        half_block = weight.at[block, lax.rem(xl + lane, 2)]
        return pltpu.make_async_remote_copy(
            src_ref=half_block,
            dst_ref=half_block,
            send_sem=send_sem.at[lane, step],
            recv_sem=recv_sem.at[lane, step],
            device_id={"z": lax.rem(z + ahead, zs)},
        )

    def right_copy(lane, step):
        return pass_on(lax.rem(z + zs - step, zs), lane, step, right_send, right_recv, 1)

    def left_copy(lane, step):
        return pass_on(lax.rem(z + step, zs), lane, step, left_send, left_recv, zs - 1)

    def landing(lane, step, shift, sem):
        landed_at = weight.at[lax.rem(z + shift, zs), lax.rem(xl + lane, 2)]
        pltpu.make_async_copy(landed_at, landed_at, sem.at[lane, step]).wait()

    def ring(lane, step):
        if step > right_steps:
            return
        if step == 0 and lane == 0:
            weight_load.wait()
        if step == 0 and lane == 1:
            swap.wait_recv()
        if 0 < step <= right_steps:
            landing(lane, step - 1, zs - step, right_recv)
        if 0 < step <= left_steps:
            landing(lane, step - 1, step, left_recv)
        if step < right_steps:
            right_copy(lane, step).start()
        if step < left_steps:
            left_copy(lane, step).start()

    ring(0, 0)
    h_pair[:, my_rows, :] = h_own[pl.ds(core, 1)].reshape(chips, CH, rows)
    h_copy.wait_recv()
    h_send[...] = h_pair[...].astype(BF16)
    send_all(z, xh, h_send, h_recv, far_send.at[0], far_recv.at[0])

    x_load.wait()
    small[0].wait()
    small[1].wait()
    x_copy.wait_recv()
    halo_copy(0).wait_recv()
    features = []
    for s in range(3):
        raw = x_all[s].astype(F32)
        first = jnp.where(me == 0, 0.0, raw[:halo])
        raw = jnp.concatenate([first, raw[halo:]], axis=0)
        total = taps[s, 0:1, mine] * raw[halo:]
        for back in range(1, taps.shape[1]):
            total = total + taps[s, back : back + 1, mine] * raw[halo - back : halo - back + 2 * rows]
        features.append(total)
    query, mixed_in = features[0], features[1] * features[2]
    flipped = mixed_in.T.reshape(chips, CH, 2 * rows)
    u_send[...] = jnp.concatenate([flipped[:, :, :rows], flipped[:, :, rows:]], axis=1).astype(BF16)
    send_all(z, xh, u_send, u_recv, far_send.at[1], far_recv.at[1])
    ring(1, 0)
    ring(0, 1)
    query_t[...] = query.T
    skip_t[...] = (skip[:, mine] * mixed_in).T

    for load in small[2:]:
        load.wait()
    a_fwd[...] = jnp.concatenate(high_low(a_table[...]), axis=1)
    high, low = high_low(b_table[...])
    b_dft[...] = jnp.concatenate([high, high, low], axis=0)
    high, low = high_low(a_back[...])
    a_inv[...] = jnp.concatenate([high, high, low], axis=1)
    ring(1, 1)
    for group in range(4):
        wait_group(h_recv, far_recv.at[0], group)
        if group == 1:
            ring(0, 2)
    ring(1, 2)
    t_re, t_im = t_both[0], t_both[1]
    h_freq = spectrum(h_recv, scratch, a_fwd, t_re, t_im, b_dft)
    for group in range(4):
        wait_group(u_recv, far_recv.at[1], group)
        if group == 1:
            ring(0, 3)
            ring(1, 3)
    u_freq = spectrum(u_recv, scratch, a_fwd, t_re, t_im, b_dft)
    width = t_re.shape[1]
    h_re, h_im = h_freq[:, :width], h_freq[:, width:]
    u_re, u_im = u_freq[:, :width], u_freq[:, width:]
    product = jnp.concatenate([h_re * u_im + h_im * u_re, h_re * u_re - h_im * u_im], axis=1)
    inverse(product, scratch, t_re, t_im, b_dft, a_inv)
    y_send[...] = scratch[...].reshape(y_send.shape).astype(BF16)
    send_all(z, xh, y_send, y_recv, far_send.at[2], far_recv.at[2], by_turn=True)
    ring(0, 4)
    ring(1, 4)

    tokens = 2 * rows
    turns = zs // 4
    pairs = 2 * CH
    across = lax.rem(x + 2, 4)

    def g_copy(kind, group, which, device_id):
        part = g_all.at[which // 2, lax.rem(which, 2), core, pl.ds(group * turns, turns)]
        return pltpu.make_async_remote_copy(
            src_ref=part,
            dst_ref=part,
            send_sem=g_send.at[kind, group],
            recv_sem=g_recv.at[kind, group],
            device_id=device_id,
        )

    def g_copies(kind, which, device_id):
        return [g_copy(kind, group, which, device_id) for group in range(4)]

    to_across = g_copies(0, x, {"xh": 1 - xh})
    to_up = g_copies(1, x, up_x)
    to_down = g_copies(2, x, down_x)
    share = g_copies(3, x, {"core": other})
    share_across = g_copies(4, across, {"core": other})
    share_down = g_copies(5, down, {"core": other})
    share_up = g_copies(6, up, {"core": other})
    for group in range(4):
        wait_group(y_recv, far_recv.at[2], group)
        for turn in range(group * turns, (group + 1) * turns):
            ahead = zs // 2 + (-((turn + 1) // 2) if turn % 2 else turn // 2)
            source = pl.ds(pl.multiple_of(lax.rem(z + zs - ahead, zs) * pairs, pairs), pairs)
            back = y_recv[pl.ds(2 * turn, 2)].astype(F32)
            convolved = jnp.concatenate(
                [back[:, CH * b : CH * (b + 1), :].reshape(pairs, rows) for b in range(2)], axis=1
            )
            value = query_t[source, :] * (convolved + skip_t[source, :])
            g_all[pl.ds(xh, 1), pl.ds(xl, 1), pl.ds(core, 1), turn] = value.astype(BF16).reshape(
                1, 1, 1, pairs, tokens
            )
        to_across[group].start()
        to_up[group].start()
        to_down[group].start()
        share[group].start()
        if group % 2 == 0:
            ring(0, 5 + group // 2)
            ring(1, 5 + group // 2)
    for group in range(4):
        to_up[group].wait_recv()
        share_down[group].start()
        to_down[group].wait_recv()
        share_up[group].start()
    ring(0, 7)
    ring(1, 7)
    for group in range(4):
        to_across[group].wait_recv()
        share_across[group].start()

    owners = 2 * ys
    owner_me = y * 2 + xl
    wide = per_owner * columns

    def order(which_x):
        for part in range(2):
            for c in range(2):
                for block in range(zs):
                    shift = lax.rem(z + zs - block, zs) - zs // 2
                    turn = jnp.where(shift < 0, -2 * shift - 1, 2 * shift)
                    start = c * half + block * pairs
                    g_ordered[part, start : start + pairs, :] = g_all[
                        pl.ds(which_x, 1), part, c, pl.ds(turn, 1)
                    ].reshape(pairs, tokens)

    def send(which_x, b, to):
        pltpu.make_async_remote_copy(
            src_ref=parts.at[which_x, b, to],
            dst_ref=landed.at[x * 2 + core, y],
            send_sem=part_send,
            recv_sem=part_recv.at[x * 2 + core, y],
            device_id={"xh": which_x, "xl": lax.rem(to, 2), "core": b, "y": to // 2},
        ).start()

    def project(which_x, own, first, count):
        targets = [
            lax.rem(z // per_owner + owners + first + lax.rem(y + k, count), owners)
            for k in range(count)
        ]
        product = jnp.zeros((count * wide, tokens), F32)
        for part in range(2):
            left = [
                weight[pl.ds(to * per_owner, per_owner), part].reshape(wide, 2 * half)
                for to in targets
            ]
            product = product + dot(jnp.concatenate(left, axis=0), g_ordered[part])
        for k, to in enumerate(targets):
            for b in range(2):
                value = product[k * wide : (k + 1) * wide, b * rows : (b + 1) * rows]
                parts[pl.ds(which_x, 1), b, pl.ds(to, 1)] = value.astype(BF16).reshape(
                    1, 1, wide, rows
                )
                if not own:
                    send(which_x, b, to)
                    continue
                stays = (b == core) & (to == owner_me)

                @pl.when(jnp.logical_not(stays))
                def _():
                    send(which_x, b, to)

                @pl.when(stays)
                def _():
                    landed[pl.ds(x * 2 + core, 1), pl.ds(y, 1)] = parts[
                        pl.ds(which_x, 1), b, pl.ds(to, 1)
                    ].reshape(1, 1, wide, rows)

    near = min(5, owners)
    for group in range(4):
        share[group].wait_recv()

        @pl.when(xl == 0)
        def _():
            share_up[group].wait_recv()

        @pl.when(xl == 1)
        def _():
            share_down[group].wait_recv()

    order(xh)
    project(xh, True, -(near // 2), near)
    if near < owners:
        for step in range(8, right_steps + 1):
            ring(0, step)
            ring(1, step)
        project(xh, True, near - near // 2, owners - near)
    for group in range(4):
        share_across[group].wait_recv()

        @pl.when(xl == 1)
        def _():
            share_up[group].wait_recv()

        @pl.when(xl == 0)
        def _():
            share_down[group].wait_recv()

    order(1 - xh)
    project(1 - xh, False, -(owners // 2), owners)

    def arrived(k, carry):
        index = lax.rem(my_index + k, everyone)
        which, owner = index // ys, lax.rem(index, ys)
        block = landed.at[which, owner]
        pltpu.make_async_copy(block, block, part_recv.at[which, owner]).wait()
        return carry

    lax.fori_loop(1, everyone, arrived, 0)
    sums = []
    for which in range(8):
        total = landed[which, 0].astype(F32)
        for source in range(1, ys):
            total = total + landed[which, source].astype(F32)
        sums.append(total)
    order = [a * 4 + c * 2 + b for a in range(2) for b in range(2) for c in range(2)]
    pieces = [
        sums[which][part * columns : (part + 1) * columns]
        for part in range(per_owner)
        for which in order
    ]
    out[...] = jnp.concatenate(pieces, axis=0).T.astype(out.dtype)

    h_copy.wait_send()
    x_copy.wait_send()

    @pl.when(core == 1)
    def _():
        halo_copy(0).wait_send()
        halo_copy(1).wait_send()

    swap.wait_send()
    for step in range(right_steps):
        for lane in range(2):
            right_copy(lane, step).wait_send()
    for step in range(left_steps):
        for lane in range(2):
            left_copy(lane, step).wait_send()
    wait_blocks(chips - 1, h_send, far_send.at[0])
    wait_blocks(chips - 1, u_send, far_send.at[1])
    wait_blocks(chips - 1, y_send, far_send.at[2])
    for group in (to_across, to_up, to_down, share, share_across, share_down, share_up):
        for copy in group:
            copy.wait_send()
    pltpu.make_async_copy(parts.at[1], parts.at[1], part_send).wait()
    pltpu.make_async_copy(parts.at[0, 1], parts.at[0, 1], part_send).wait()
    sent = parts.at[0, 0, pl.ds(1, owners - 1)]
    pltpu.make_async_copy(sent, sent, part_send).wait()


def body(qkv_in, short_taps, long_filter, skip_gain, out_weight):
    rows, _, channels = qkv_in.shape
    half = channels // 2
    zs = lax.axis_size("z")
    chips = zs * 2
    ys = lax.axis_size("y")
    blocks = 2 * chips
    columns = out_weight.shape[1] // 2
    wide = zs // (2 * ys) * columns
    lookup = tables(blocks, rows)
    exchange = (chips, 2 * CH, rows)
    dma = pltpu.SemaphoreType.DMA
    return pl.pallas_call(
        mixer_kernel,
        out_shape=jax.ShapeDtypeStruct((rows, channels), BF16),
        in_specs=[pl.BlockSpec(memory_space=pl.ANY)] * 9,
        out_specs=VMEM,
        scratch_shapes=[
            pltpu.VMEM(short_taps.shape, F32),
            pltpu.VMEM((rows, channels), F32),
            pltpu.VMEM((1, channels), F32),
            *[pltpu.VMEM(table.shape, table.dtype) for table in lookup],
            pltpu.VMEM((2 * blocks, 2 * blocks), BF16),
            pltpu.VMEM((6 * rows, 2 * rows), BF16),
            pltpu.VMEM((blocks, 6 * blocks), BF16),
            pltpu.VMEM((2, chips, CH, rows), F32),
            pltpu.VMEM(exchange, F32),
            pltpu.VMEM(exchange, BF16),
            pltpu.VMEM(exchange, BF16),
            pltpu.VMEM((3, 16 + 2 * rows, half), BF16),
            pltpu.VMEM(exchange, BF16),
            pltpu.VMEM(exchange, BF16),
            pltpu.VMEM(exchange, BF16),
            pltpu.VMEM(exchange, BF16),
            pltpu.VMEM((blocks * CH, rows), F32),
            pltpu.VMEM((zs, 2, columns, channels), BF16),
            pltpu.VMEM((half, 2 * rows), F32),
            pltpu.VMEM((half, 2 * rows), F32),
            pltpu.VMEM((2, 2, 2, zs, 2 * CH, 2 * rows), BF16),
            pltpu.VMEM((2, channels, 2 * rows), BF16),
            pltpu.VMEM((2, 2, 2 * ys, wide, rows), BF16),
            pltpu.VMEM((8, ys, wide, rows), BF16),
            dma((9,)),
            dma((5,)),
            dma((4,)),
            dma((3,)),
            dma((3, 4)),
            dma((2, zs)),
            dma((2, zs)),
            dma((2, zs)),
            dma((2, zs)),
            dma((7, 4)),
            dma((7, 4)),
            dma,
            dma((8, ys)),
        ],
        compiler_params=pltpu.CompilerParams(
            collective_id=0, has_side_effects=True, vmem_limit_bytes=60 * 2**20
        ),
        name="mixer",
    )(
        qkv_in.transpose(1, 0, 2),
        short_taps,
        long_filter,
        skip_gain[None, :],
        out_weight.T,
        *lookup,
    )


def solution(mesh):
    sizes = dict(mesh.shape)
    split = Mesh(
        mesh.devices.reshape(sizes["ctx"] // 4, 2, 2, sizes["tp"] // 2, 2),
        ("z", "xh", "core", "y", "xl"),
    )
    ctx, tp = ("z", "xh", "core"), ("y", "xl")
    return jax.shard_map(
        body,
        mesh=split,
        in_specs=(P(ctx, None, tp), P(None, None, tp), P(ctx, tp), P(tp), P(tp, ctx)),
        out_specs=P(ctx, tp),
        check_vma=False,
    )
```

```python
import jax
import jax.numpy as jnp
import numpy as np
from jax import lax
from jax.experimental import pallas as pl
from jax.experimental.pallas import tpu as pltpu
from jax.sharding import Mesh, PartitionSpec as P

F32 = jnp.float32
BF16 = jnp.bfloat16
CH = 8
VMEM = pl.BlockSpec(memory_space=pltpu.VMEM)


def tables(blocks, width):
    length = blocks * width
    f1 = np.arange(blocks)[:, None]
    a = np.exp(-2j * np.pi * ((np.arange(blocks)[None, :] * (4 * f1 + 1)) % (4 * blocks)) / (4 * blocks))
    t = np.exp(-2j * np.pi * (np.arange(width)[None, :] * (4 * f1 + 1)) / (4 * length))
    i = np.arange(width)
    b = np.exp(-2j * np.pi * ((i[:, None] * i[None, :]) % width) / width)
    found = (
        np.concatenate([a.real, a.imag], 0),
        np.stack([t.real, t.imag]),
        np.block([[b.real, b.imag], [-b.imag, b.real]]),
        np.concatenate([a.real.T, a.imag.T], 1) / length,
    )
    return [jnp.asarray(table.astype(np.float32)) for table in found]


def dot(left, right):
    return jnp.dot(left, right, preferred_element_type=F32)


def high_low(value):
    high = value.astype(BF16)
    return high, (value - high.astype(F32)).astype(BF16)


def send_all(z, xh, source, target, send_sem, recv_sems, by_turn=False):
    zs = lax.axis_size("z")
    me = z * 2 + xh
    size = 2 * zs // recv_sems.shape[0]

    def step(k, carry):
        turn = k // 2
        ahead = zs // 2 + jnp.where(lax.rem(turn, 2) == 1, -((turn + 1) // 2), turn // 2)
        to_z = lax.rem(z + ahead, zs)
        to_x = jnp.where(lax.rem(k, 2) == 0, 1 - xh, xh)
        pltpu.make_async_remote_copy(
            src_ref=source.at[to_z * 2 + to_x],
            dst_ref=target.at[turn * 2 + xh if by_turn else me],
            send_sem=send_sem,
            recv_sem=recv_sems.at[k // size],
            device_id={"z": to_z, "xh": to_x},
        ).start()
        return carry

    lax.fori_loop(0, 2 * zs - 1, step, 0)
    slot = (zs - 1) * 2 + xh if by_turn else me
    target[pl.ds(slot, 1)] = source[pl.ds(me, 1)]


def wait_blocks(count, ref, sem):
    part = ref.at[pl.ds(0, count)]
    pltpu.make_async_copy(part, part, sem).wait()


def wait_group(ref, sems, group):
    size = ref.shape[0] // sems.shape[0]
    wait_blocks(size - (group == sems.shape[0] - 1), ref, sems.at[group])


def spectrum(received, scratch, a_fwd, t_re, t_im, b_dft):
    rows = scratch.shape[0]
    blocks = rows // CH
    scratch[...] = received[...].astype(F32).reshape(rows, -1)
    columns = [scratch[pl.ds(c, blocks, stride=CH), :].astype(BF16) for c in range(CH)]
    signal = jnp.concatenate(columns, axis=1)
    mixed = dot(a_fwd[...], jnp.concatenate([signal, signal], axis=0))
    width = t_re.shape[1]
    parts = []
    for c in range(CH):
        re = mixed[:blocks, c * width : (c + 1) * width]
        im = mixed[blocks:, c * width : (c + 1) * width]
        parts.append(
            jnp.concatenate(
                [re * t_re - im * t_im, re * t_im + im * t_re], axis=1
            )
        )
    high, low = high_low(jnp.concatenate(parts, axis=0))
    return dot(jnp.concatenate([high, low, high], axis=1), b_dft[...])


def inverse(product, scratch, t_re, t_im, b_dft, a_inv):
    blocks, width = t_re.shape
    high, low = high_low(product)
    back = dot(jnp.concatenate([high, low, high], axis=1), b_dft[...])
    parts = []
    for c in range(CH):
        im = back[c * blocks : (c + 1) * blocks, :width]
        re = back[c * blocks : (c + 1) * blocks, width:]
        parts.append(
            jnp.concatenate(
                [re * t_re + im * t_im, im * t_re - re * t_im], axis=0
            )
        )
    high, low = high_low(jnp.concatenate(parts, axis=1))
    result = dot(a_inv[...], jnp.concatenate([high, low, high], axis=0))
    for c in range(CH):
        scratch[pl.ds(c, blocks, stride=CH), :] = result[:, c * width : (c + 1) * width]


def local_copy(source, target, sem):
    copy = pltpu.make_async_copy(source, target, sem)
    copy.start()
    return copy


def mixer_kernel(
    qkv_hbm, taps_hbm, filt_hbm, skip_hbm, weight_hbm,
    a_fwd_hbm, t_hbm, b_dft_hbm, a_inv_hbm,
    out,
    taps, filt, skip, a_table, t_both, b_table, a_back, a_fwd, b_dft, a_inv,
    h_own, h_pair, h_send, h_recv, x_all, u_send, u_recv, y_send, y_recv, scratch,
    weight, query_t, skip_t, g_all, g_ordered, parts, landed,
    load_sem, near_send, near_recv, far_send, far_recv,
    right_send, right_recv, left_send, left_recv, g_send, g_recv, part_send, part_recv,
):
    z, xh, core = lax.axis_index("z"), lax.axis_index("xh"), lax.axis_index("core")
    y, xl = lax.axis_index("y"), lax.axis_index("xl")
    zs, ys = lax.axis_size("z"), lax.axis_size("y")
    chips = zs * 2
    per_owner = zs // (2 * ys)
    me = z * 2 + xh
    other = 1 - core
    rows = qkv_hbm.shape[1]
    half = chips * CH
    halo = 16
    mine = pl.ds(pl.multiple_of(core * half, half), half)
    theirs = pl.ds(pl.multiple_of(other * half, half), half)
    place = pl.ds(pl.multiple_of(halo + core * rows, 16), rows)
    x = xh * 2 + xl
    everyone = 8 * ys
    my_index = (x * 2 + core) * ys + y
    up, down = lax.rem(x + 1, 4), lax.rem(x + 3, 4)
    up_x = {"xh": up // 2, "xl": lax.rem(up, 2)}
    down_x = {"xh": down // 2, "xl": lax.rem(down, 2)}
    columns = weight.shape[2]

    filt_load = local_copy(filt_hbm, filt, load_sem.at[0])
    x_load = local_copy(qkv_hbm.at[:, :, mine], x_all.at[:, place, :], load_sem.at[1])
    weight_load = local_copy(
        weight_hbm.at[pl.ds(pl.multiple_of(xl * columns, columns), columns), :],
        weight.at[z, xl],
        load_sem.at[2],
    )
    small = [
        local_copy(source, target, load_sem.at[3 + k])
        for k, (source, target) in enumerate(
            [
                (taps_hbm, taps),
                (skip_hbm, skip),
                (a_fwd_hbm, a_table),
                (t_hbm, t_both),
                (b_dft_hbm, b_table),
                (a_inv_hbm, a_back),
            ]
        )
    ]

    barrier = pltpu.get_barrier_semaphore()
    step_to = lax.rem(me + jnp.where(core == 1, 1, chips - 1), chips)
    pl.semaphore_signal(
        barrier, inc=1, device_id={"z": step_to // 2, "xh": lax.rem(step_to, 2), "core": other}
    )


    def place_of(index):
        which = index // ys
        return {
            "xh": which // 4,
            "xl": lax.rem(which // 2, 2),
            "core": lax.rem(which, 2),
            "y": lax.rem(index, ys),
        }

    def greet_ctx(k, carry):
        peer = lax.rem(me + k, chips)
        pl.semaphore_signal(
            barrier, inc=1, device_id={"z": peer // 2, "xh": lax.rem(peer, 2)}
        )
        return carry

    def greet_plane(k, carry):
        pl.semaphore_signal(barrier, inc=1, device_id=place_of(lax.rem(my_index + k, everyone)))
        return carry

    lax.fori_loop(1, chips, greet_ctx, 0)
    lax.fori_loop(1, everyone, greet_plane, 0)

    filt_load.wait()
    h_own[...] = filt[...].T.reshape(2, chips, CH, rows)
    pl.semaphore_wait(barrier, 1 + chips - 1 + everyone - 1)

    my_rows = pl.ds(pl.multiple_of(core * CH, CH), CH)
    h_copy = pltpu.make_async_remote_copy(
        src_ref=h_own.at[other],
        dst_ref=h_pair.at[:, my_rows, :],
        send_sem=near_send.at[0],
        recv_sem=near_recv.at[0],
        device_id={"core": other},
    )
    h_copy.start()
    x_copy = pltpu.make_async_remote_copy(
        src_ref=qkv_hbm.at[:, :, theirs],
        dst_ref=x_all.at[:, place, :],
        send_sem=near_send.at[1],
        recv_sem=near_recv.at[1],
        device_id={"core": other},
    )
    x_copy.start()

    after = lax.rem(me + 1, chips)

    def halo_copy(target):
        return pltpu.make_async_remote_copy(
            src_ref=qkv_hbm.at[:, pl.ds(rows - halo, halo), pl.ds(target * half, half)],
            dst_ref=x_all.at[:, pl.ds(0, halo), :],
            send_sem=near_send.at[2 + target],
            recv_sem=near_recv.at[2],
            device_id={"z": after // 2, "xh": lax.rem(after, 2), "core": target},
        )

    @pl.when(core == 1)
    def _():
        halo_copy(0).start()
        halo_copy(1).start()

    swap = pltpu.make_async_remote_copy(
        src_ref=weight_hbm.at[pl.ds(pl.multiple_of((1 - xl) * columns, columns), columns), :],
        dst_ref=weight.at[z, xl],
        send_sem=near_send.at[4],
        recv_sem=near_recv.at[3],
        device_id={"xl": 1 - xl},
    )
    swap.start()
    right_steps = zs // 2
    left_steps = zs - 1 - right_steps

    def pass_on(block, lane, step, send_sem, recv_sem, ahead):
        half_block = weight.at[block, lax.rem(xl + lane, 2)]
        return pltpu.make_async_remote_copy(
            src_ref=half_block,
            dst_ref=half_block,
            send_sem=send_sem.at[lane, step],
            recv_sem=recv_sem.at[lane, step],
            device_id={"z": lax.rem(z + ahead, zs)},
        )

    def right_copy(lane, step):
        return pass_on(lax.rem(z + zs - step, zs), lane, step, right_send, right_recv, 1)

    def left_copy(lane, step):
        return pass_on(lax.rem(z + step, zs), lane, step, left_send, left_recv, zs - 1)

    def landing(lane, step, shift, sem):
        landed_at = weight.at[lax.rem(z + shift, zs), lax.rem(xl + lane, 2)]
        pltpu.make_async_copy(landed_at, landed_at, sem.at[lane, step]).wait()

    def ring(lane, step):
        if step > right_steps:
            return
        if step == 0 and lane == 0:
            weight_load.wait()
        if step == 0 and lane == 1:
            swap.wait_recv()
        if 0 < step <= right_steps:
            landing(lane, step - 1, zs - step, right_recv)
        if 0 < step <= left_steps:
            landing(lane, step - 1, step, left_recv)
        if step < right_steps:
            right_copy(lane, step).start()
        if step < left_steps:
            left_copy(lane, step).start()

    ring(0, 0)
    h_pair[:, my_rows, :] = h_own[pl.ds(core, 1)].reshape(chips, CH, rows)
    h_copy.wait_recv()
    h_send[...] = h_pair[...].astype(BF16)
    send_all(z, xh, h_send, h_recv, far_send.at[0], far_recv.at[0])
    ring(1, 0)

    x_load.wait()
    small[0].wait()
    small[1].wait()
    x_copy.wait_recv()
    halo_copy(0).wait_recv()
    features = []
    for s in range(3):
        raw = x_all[s].astype(F32)
        first = jnp.where(me == 0, 0.0, raw[:halo])
        raw = jnp.concatenate([first, raw[halo:]], axis=0)
        total = taps[s, 0:1, mine] * raw[halo:]
        for back in range(1, taps.shape[1]):
            total = total + taps[s, back : back + 1, mine] * raw[halo - back : halo - back + 2 * rows]
        features.append(total)
    query, mixed_in = features[0], features[1] * features[2]
    flipped = mixed_in.T.reshape(chips, CH, 2 * rows)
    u_send[...] = jnp.concatenate([flipped[:, :, :rows], flipped[:, :, rows:]], axis=1).astype(BF16)
    send_all(z, xh, u_send, u_recv, far_send.at[1], far_recv.at[1])
    ring(0, 1)
    query_t[...] = query.T
    skip_t[...] = (skip[:, mine] * mixed_in).T

    for load in small[2:]:
        load.wait()
    a_fwd[...] = jnp.concatenate(high_low(a_table[...]), axis=1)
    high, low = high_low(b_table[...])
    b_dft[...] = jnp.concatenate([high, high, low], axis=0)
    high, low = high_low(a_back[...])
    a_inv[...] = jnp.concatenate([high, high, low], axis=1)
    ring(1, 1)
    for group in range(4):
        wait_group(h_recv, far_recv.at[0], group)
    t_re, t_im = t_both[0], t_both[1]
    h_freq = spectrum(h_recv, scratch, a_fwd, t_re, t_im, b_dft)
    for group in range(4):
        wait_group(u_recv, far_recv.at[1], group)
        if group == 2:
            ring(0, 2)
            ring(1, 2)
    u_freq = spectrum(u_recv, scratch, a_fwd, t_re, t_im, b_dft)
    width = t_re.shape[1]
    h_re, h_im = h_freq[:, :width], h_freq[:, width:]
    u_re, u_im = u_freq[:, :width], u_freq[:, width:]
    product = jnp.concatenate([h_re * u_im + h_im * u_re, h_re * u_re - h_im * u_im], axis=1)
    inverse(product, scratch, t_re, t_im, b_dft, a_inv)
    y_send[...] = scratch[...].reshape(y_send.shape).astype(BF16)
    ring(0, 3)
    ring(1, 3)
    send_all(z, xh, y_send, y_recv, far_send.at[2], far_recv.at[2], by_turn=True)
    ring(0, 4)
    ring(1, 4)

    tokens = 2 * rows
    turns = zs // 4
    pairs = 2 * CH
    across = lax.rem(x + 2, 4)

    def g_copy(kind, group, which, device_id):
        part = g_all.at[which // 2, lax.rem(which, 2), core, pl.ds(group * turns, turns)]
        return pltpu.make_async_remote_copy(
            src_ref=part,
            dst_ref=part,
            send_sem=g_send.at[kind, group],
            recv_sem=g_recv.at[kind, group],
            device_id=device_id,
        )

    def g_copies(kind, which, device_id):
        return [g_copy(kind, group, which, device_id) for group in range(4)]

    to_across = g_copies(0, x, {"xh": 1 - xh})
    to_up = g_copies(1, x, up_x)
    to_down = g_copies(2, x, down_x)
    share = g_copies(3, x, {"core": other})
    share_across = g_copies(4, across, {"core": other})
    share_down = g_copies(5, down, {"core": other})
    share_up = g_copies(6, up, {"core": other})
    for group in range(4):
        wait_group(y_recv, far_recv.at[2], group)
        for turn in range(group * turns, (group + 1) * turns):
            ahead = zs // 2 + (-((turn + 1) // 2) if turn % 2 else turn // 2)
            source = pl.ds(pl.multiple_of(lax.rem(z + zs - ahead, zs) * pairs, pairs), pairs)
            back = y_recv[pl.ds(2 * turn, 2)].astype(F32)
            convolved = jnp.concatenate(
                [back[:, CH * b : CH * (b + 1), :].reshape(pairs, rows) for b in range(2)], axis=1
            )
            value = query_t[source, :] * (convolved + skip_t[source, :])
            g_all[pl.ds(xh, 1), pl.ds(xl, 1), pl.ds(core, 1), turn] = value.astype(BF16).reshape(
                1, 1, 1, pairs, tokens
            )
        to_across[group].start()
        to_up[group].start()
        to_down[group].start()
        share[group].start()
        if group in (0, 3):
            ring(0, 5 + group // 3)
            ring(1, 5 + group // 3)
    for group in range(4):
        to_up[group].wait_recv()
        share_down[group].start()
        to_down[group].wait_recv()
        share_up[group].start()
    ring(0, 7)
    ring(1, 7)
    for group in range(4):
        to_across[group].wait_recv()
        share_across[group].start()

    owners = 2 * ys
    owner_me = y * 2 + xl
    wide = per_owner * columns

    def order(far):
        which_x = 1 - xh if far else xh
        for part in range(2):
            for c in range(2):
                for block in range(zs):
                    shift = lax.rem(z + zs - block, zs) - zs // 2
                    turn = jnp.where(shift < 0, -2 * shift - 1, 2 * shift)
                    start = c * half + block * pairs
                    g_ordered[far, part, start : start + pairs, :] = g_all[
                        pl.ds(which_x, 1), part, c, pl.ds(turn, 1)
                    ].reshape(pairs, tokens)

    def send(which_x, b, to):
        pltpu.make_async_remote_copy(
            src_ref=parts.at[which_x, b, to],
            dst_ref=landed.at[x * 2 + core, y],
            send_sem=part_send,
            recv_sem=part_recv.at[x * 2 + core, y],
            device_id={"xh": which_x, "xl": lax.rem(to, 2), "core": b, "y": to // 2},
        ).start()

    def project(far, first, count):
        which_x = 1 - xh if far else xh
        targets = [
            lax.rem(z // per_owner + owners + first + lax.rem(y + k, count), owners)
            for k in range(count)
        ]
        product = jnp.zeros((count * wide, tokens), F32)
        for part in range(2):
            left = [
                weight[pl.ds(to * per_owner, per_owner), part].reshape(wide, 2 * half)
                for to in targets
            ]
            product = product + dot(jnp.concatenate(left, axis=0), g_ordered[far, part])
        for k, to in enumerate(targets):
            for b in range(2):
                value = product[k * wide : (k + 1) * wide, b * rows : (b + 1) * rows]
                parts[pl.ds(which_x, 1), b, pl.ds(to, 1)] = value.astype(BF16).reshape(
                    1, 1, wide, rows
                )
                if far:
                    send(which_x, b, to)
                    continue
                stays = (b == core) & (to == owner_me)

                @pl.when(jnp.logical_not(stays))
                def _():
                    send(which_x, b, to)

                @pl.when(stays)
                def _():
                    landed[pl.ds(x * 2 + core, 1), pl.ds(y, 1)] = parts[
                        pl.ds(which_x, 1), b, pl.ds(to, 1)
                    ].reshape(1, 1, wide, rows)

    near = min(5, owners)
    for group in range(4):
        share[group].wait_recv()

        @pl.when(xl == 0)
        def _():
            share_up[group].wait_recv()

        @pl.when(xl == 1)
        def _():
            share_down[group].wait_recv()

    order(0)
    project(0, -(near // 2), near)
    for group in range(4):
        share_across[group].wait_recv()

        @pl.when(xl == 1)
        def _():
            share_up[group].wait_recv()

        @pl.when(xl == 0)
        def _():
            share_down[group].wait_recv()

    order(1)
    project(1, -(near // 2), near)
    if near < owners:
        for step in range(8, right_steps + 1):
            ring(0, step)
            ring(1, step)
        project(1, near - near // 2, owners - near)
        project(0, near - near // 2, owners - near)

    def arrived(k, carry):
        index = lax.rem(my_index + k, everyone)
        which, owner = index // ys, lax.rem(index, ys)
        block = landed.at[which, owner]
        pltpu.make_async_copy(block, block, part_recv.at[which, owner]).wait()
        return carry

    lax.fori_loop(1, everyone, arrived, 0)
    sums = []
    for which in range(8):
        total = landed[which, 0].astype(F32)
        for source in range(1, ys):
            total = total + landed[which, source].astype(F32)
        sums.append(total)
    order = [a * 4 + c * 2 + b for a in range(2) for b in range(2) for c in range(2)]
    pieces = [
        sums[which][part * columns : (part + 1) * columns]
        for part in range(per_owner)
        for which in order
    ]
    out[...] = jnp.concatenate(pieces, axis=0).T.astype(out.dtype)

    h_copy.wait_send()
    x_copy.wait_send()

    @pl.when(core == 1)
    def _():
        halo_copy(0).wait_send()
        halo_copy(1).wait_send()

    swap.wait_send()
    for step in range(right_steps):
        for lane in range(2):
            right_copy(lane, step).wait_send()
    for step in range(left_steps):
        for lane in range(2):
            left_copy(lane, step).wait_send()
    wait_blocks(chips - 1, h_send, far_send.at[0])
    wait_blocks(chips - 1, u_send, far_send.at[1])
    wait_blocks(chips - 1, y_send, far_send.at[2])
    for group in (to_across, to_up, to_down, share, share_across, share_down, share_up):
        for copy in group:
            copy.wait_send()
    pltpu.make_async_copy(parts.at[1], parts.at[1], part_send).wait()
    pltpu.make_async_copy(parts.at[0, 1], parts.at[0, 1], part_send).wait()
    sent = parts.at[0, 0, pl.ds(1, owners - 1)]
    pltpu.make_async_copy(sent, sent, part_send).wait()


def body(qkv_in, short_taps, long_filter, skip_gain, out_weight):
    rows, _, channels = qkv_in.shape
    half = channels // 2
    zs = lax.axis_size("z")
    chips = zs * 2
    ys = lax.axis_size("y")
    blocks = 2 * chips
    columns = out_weight.shape[1] // 2
    wide = zs // (2 * ys) * columns
    lookup = tables(blocks, rows)
    exchange = (chips, 2 * CH, rows)
    dma = pltpu.SemaphoreType.DMA
    return pl.pallas_call(
        mixer_kernel,
        out_shape=jax.ShapeDtypeStruct((rows, channels), BF16),
        in_specs=[pl.BlockSpec(memory_space=pl.ANY)] * 9,
        out_specs=VMEM,
        scratch_shapes=[
            pltpu.VMEM(short_taps.shape, F32),
            pltpu.VMEM((rows, channels), F32),
            pltpu.VMEM((1, channels), F32),
            *[pltpu.VMEM(table.shape, table.dtype) for table in lookup],
            pltpu.VMEM((2 * blocks, 2 * blocks), BF16),
            pltpu.VMEM((6 * rows, 2 * rows), BF16),
            pltpu.VMEM((blocks, 6 * blocks), BF16),
            pltpu.VMEM((2, chips, CH, rows), F32),
            pltpu.VMEM(exchange, F32),
            pltpu.VMEM(exchange, BF16),
            pltpu.VMEM(exchange, BF16),
            pltpu.VMEM((3, 16 + 2 * rows, half), BF16),
            pltpu.VMEM(exchange, BF16),
            pltpu.VMEM(exchange, BF16),
            pltpu.VMEM(exchange, BF16),
            pltpu.VMEM(exchange, BF16),
            pltpu.VMEM((blocks * CH, rows), F32),
            pltpu.VMEM((zs, 2, columns, channels), BF16),
            pltpu.VMEM((half, 2 * rows), F32),
            pltpu.VMEM((half, 2 * rows), F32),
            pltpu.VMEM((2, 2, 2, zs, 2 * CH, 2 * rows), BF16),
            pltpu.VMEM((2, 2, channels, 2 * rows), BF16),
            pltpu.VMEM((2, 2, 2 * ys, wide, rows), BF16),
            pltpu.VMEM((8, ys, wide, rows), BF16),
            dma((9,)),
            dma((5,)),
            dma((4,)),
            dma((3,)),
            dma((3, 4)),
            dma((2, zs)),
            dma((2, zs)),
            dma((2, zs)),
            dma((2, zs)),
            dma((7, 4)),
            dma((7, 4)),
            dma,
            dma((8, ys)),
        ],
        compiler_params=pltpu.CompilerParams(
            collective_id=0, has_side_effects=True, vmem_limit_bytes=60 * 2**20
        ),
        name="mixer",
    )(
        qkv_in.transpose(1, 0, 2),
        short_taps,
        long_filter,
        skip_gain[None, :],
        out_weight.T,
        *lookup,
    )


def solution(mesh):
    sizes = dict(mesh.shape)
    split = Mesh(
        mesh.devices.reshape(sizes["ctx"] // 4, 2, 2, sizes["tp"] // 2, 2),
        ("z", "xh", "core", "y", "xl"),
    )
    ctx, tp = ("z", "xh", "core"), ("y", "xl")
    return jax.shard_map(
        body,
        mesh=split,
        in_specs=(P(ctx, None, tp), P(None, None, tp), P(ctx, tp), P(tp), P(tp, ctx)),
        out_specs=P(ctx, tp),
        check_vma=False,
    )
```

```python
import jax
import jax.numpy as jnp
import numpy as np
from jax import lax
from jax.experimental import pallas as pl
from jax.experimental.pallas import tpu as pltpu
from jax.sharding import Mesh, PartitionSpec as P

F32 = jnp.float32
BF16 = jnp.bfloat16
CH = 8
VMEM = pl.BlockSpec(memory_space=pltpu.VMEM)


def tables(blocks, width):
    length = blocks * width
    f1 = np.arange(blocks)[:, None]
    a = np.exp(-2j * np.pi * ((np.arange(blocks)[None, :] * (4 * f1 + 1)) % (4 * blocks)) / (4 * blocks))
    t = np.exp(-2j * np.pi * (np.arange(width)[None, :] * (4 * f1 + 1)) / (4 * length))
    i = np.arange(width)
    b = np.exp(-2j * np.pi * ((i[:, None] * i[None, :]) % width) / width)
    found = (
        np.concatenate([a.real, a.imag], 0),
        np.stack([t.real, t.imag]),
        np.block([[b.real, b.imag], [-b.imag, b.real]]),
        np.concatenate([a.real.T, a.imag.T], 1) / length,
    )
    return [jnp.asarray(table.astype(np.float32)) for table in found]


def dot(left, right):
    return jnp.dot(left, right, preferred_element_type=F32)


def high_low(value):
    high = value.astype(BF16)
    return high, (value - high.astype(F32)).astype(BF16)


def hops(turn):
    if isinstance(turn, int):
        return -((turn + 1) // 2) if turn % 2 else turn // 2
    return jnp.where(lax.rem(turn, 2) == 1, -((turn + 1) // 2), turn // 2)


def send_all(z, xh, source, target, send_sem, recv_sems, near_first=False):
    zs = lax.axis_size("z")
    me = z * 2 + xh
    size = 2 * zs // recv_sems.shape[0]

    def step(k, carry):
        turn = k // 2
        ahead = hops(turn) + (zs if near_first else zs // 2)
        to_z = lax.rem(z + ahead, zs)
        to_x = jnp.where(lax.rem(k, 2) == 0, 1 - xh, xh)
        pltpu.make_async_remote_copy(
            src_ref=source.at[to_z * 2 + to_x],
            dst_ref=target.at[turn * 2 + xh if near_first else me],
            send_sem=send_sem,
            recv_sem=recv_sems.at[k // size],
            device_id={"z": to_z, "xh": to_x},
        ).start()
        return carry

    if near_first:
        step(0, 0)
        lax.fori_loop(2, 2 * zs, step, 0)
    else:
        lax.fori_loop(0, 2 * zs - 1, step, 0)
    slot = xh if near_first else me
    target[pl.ds(slot, 1)] = source[pl.ds(me, 1)]


def wait_blocks(count, ref, sem):
    part = ref.at[pl.ds(0, count)]
    pltpu.make_async_copy(part, part, sem).wait()


def wait_group(ref, sems, group, short):
    size = ref.shape[0] // sems.shape[0]
    wait_blocks(size - (group == short), ref, sems.at[group])


def spectrum(received, scratch, a_fwd, t_re, t_im, b_dft):
    rows = scratch.shape[0]
    blocks = rows // CH
    scratch[...] = received[...].astype(F32).reshape(rows, -1)
    columns = [scratch[pl.ds(c, blocks, stride=CH), :].astype(BF16) for c in range(CH)]
    signal = jnp.concatenate(columns, axis=1)
    mixed = dot(a_fwd[...], jnp.concatenate([signal, signal], axis=0))
    width = t_re.shape[1]
    parts = []
    for c in range(CH):
        re = mixed[:blocks, c * width : (c + 1) * width]
        im = mixed[blocks:, c * width : (c + 1) * width]
        parts.append(
            jnp.concatenate(
                [re * t_re - im * t_im, re * t_im + im * t_re], axis=1
            )
        )
    high, low = high_low(jnp.concatenate(parts, axis=0))
    return dot(jnp.concatenate([high, low, high], axis=1), b_dft[...])


def inverse(product, scratch, t_re, t_im, b_dft, a_inv):
    blocks, width = t_re.shape
    high, low = high_low(product)
    back = dot(jnp.concatenate([high, low, high], axis=1), b_dft[...])
    parts = []
    for c in range(CH):
        im = back[c * blocks : (c + 1) * blocks, :width]
        re = back[c * blocks : (c + 1) * blocks, width:]
        parts.append(
            jnp.concatenate(
                [re * t_re + im * t_im, im * t_re - re * t_im], axis=0
            )
        )
    high, low = high_low(jnp.concatenate(parts, axis=1))
    result = dot(a_inv[...], jnp.concatenate([high, low, high], axis=0))
    for c in range(CH):
        scratch[pl.ds(c, blocks, stride=CH), :] = result[:, c * width : (c + 1) * width]


def local_copy(source, target, sem):
    copy = pltpu.make_async_copy(source, target, sem)
    copy.start()
    return copy


def mixer_kernel(
    qkv_hbm, taps_hbm, filt_hbm, skip_hbm, weight_hbm,
    a_fwd_hbm, t_hbm, b_dft_hbm, a_inv_hbm,
    out,
    taps, filt, skip, a_table, t_both, b_table, a_back, a_fwd, b_dft, a_inv,
    h_own, h_pair, h_send, h_recv, x_all, u_send, u_recv, y_send, y_recv, scratch,
    weight, query_t, skip_t, g_all, g_ordered, parts, landed,
    load_sem, near_send, near_recv, far_send, far_recv,
    right_send, right_recv, left_send, left_recv, g_send, g_recv, part_send, part_recv,
):
    z, xh, core = lax.axis_index("z"), lax.axis_index("xh"), lax.axis_index("core")
    y, xl = lax.axis_index("y"), lax.axis_index("xl")
    zs, ys = lax.axis_size("z"), lax.axis_size("y")
    chips = zs * 2
    per_owner = zs // (2 * ys)
    me = z * 2 + xh
    other = 1 - core
    rows = qkv_hbm.shape[1]
    half = chips * CH
    halo = 16
    mine = pl.ds(pl.multiple_of(core * half, half), half)
    theirs = pl.ds(pl.multiple_of(other * half, half), half)
    place = pl.ds(pl.multiple_of(halo + core * rows, 16), rows)
    x = xh * 2 + xl
    everyone = 8 * ys
    my_index = (x * 2 + core) * ys + y
    up, down = lax.rem(x + 1, 4), lax.rem(x + 3, 4)
    up_x = {"xh": up // 2, "xl": lax.rem(up, 2)}
    down_x = {"xh": down // 2, "xl": lax.rem(down, 2)}
    columns = weight.shape[2]

    barrier = pltpu.get_barrier_semaphore()
    step_to = lax.rem(me + jnp.where(core == 1, 1, chips - 1), chips)
    pl.semaphore_signal(
        barrier, inc=1, device_id={"z": step_to // 2, "xh": lax.rem(step_to, 2), "core": other}
    )


    def place_of(index):
        which = index // ys
        return {
            "xh": which // 4,
            "xl": lax.rem(which // 2, 2),
            "core": lax.rem(which, 2),
            "y": lax.rem(index, ys),
        }

    def greet_ctx(k, carry):
        peer = lax.rem(me + k, chips)
        pl.semaphore_signal(
            barrier, inc=1, device_id={"z": peer // 2, "xh": lax.rem(peer, 2)}
        )
        return carry

    def greet_plane(k, carry):
        pl.semaphore_signal(barrier, inc=1, device_id=place_of(lax.rem(my_index + k, everyone)))
        return carry

    lax.fori_loop(1, chips, greet_ctx, 0)
    lax.fori_loop(1, everyone, greet_plane, 0)

    filt_load = local_copy(filt_hbm, filt, load_sem.at[0])
    x_load = local_copy(qkv_hbm.at[:, :, mine], x_all.at[:, place, :], load_sem.at[1])
    weight_load = local_copy(
        weight_hbm.at[pl.ds(pl.multiple_of(xl * columns, columns), columns), :],
        weight.at[z, xl],
        load_sem.at[2],
    )
    small = [
        local_copy(source, target, load_sem.at[3 + k])
        for k, (source, target) in enumerate(
            [
                (taps_hbm, taps),
                (skip_hbm, skip),
                (a_fwd_hbm, a_table),
                (t_hbm, t_both),
                (b_dft_hbm, b_table),
                (a_inv_hbm, a_back),
            ]
        )
    ]

    filt_load.wait()
    h_own[...] = filt[...].T.reshape(2, chips, CH, rows)
    pl.semaphore_wait(barrier, 1 + chips - 1 + everyone - 1)

    my_rows = pl.ds(pl.multiple_of(core * CH, CH), CH)
    h_copy = pltpu.make_async_remote_copy(
        src_ref=h_own.at[other],
        dst_ref=h_pair.at[:, my_rows, :],
        send_sem=near_send.at[0],
        recv_sem=near_recv.at[0],
        device_id={"core": other},
    )
    h_copy.start()
    x_copy = pltpu.make_async_remote_copy(
        src_ref=qkv_hbm.at[:, :, theirs],
        dst_ref=x_all.at[:, place, :],
        send_sem=near_send.at[1],
        recv_sem=near_recv.at[1],
        device_id={"core": other},
    )
    x_copy.start()

    after = lax.rem(me + 1, chips)

    def halo_copy(target):
        return pltpu.make_async_remote_copy(
            src_ref=qkv_hbm.at[:, pl.ds(rows - halo, halo), pl.ds(target * half, half)],
            dst_ref=x_all.at[:, pl.ds(0, halo), :],
            send_sem=near_send.at[2 + target],
            recv_sem=near_recv.at[2],
            device_id={"z": after // 2, "xh": lax.rem(after, 2), "core": target},
        )

    @pl.when(core == 1)
    def _():
        halo_copy(0).start()
        halo_copy(1).start()

    swap = pltpu.make_async_remote_copy(
        src_ref=weight_hbm.at[pl.ds(pl.multiple_of((1 - xl) * columns, columns), columns), :],
        dst_ref=weight.at[z, xl],
        send_sem=near_send.at[4],
        recv_sem=near_recv.at[3],
        device_id={"xl": 1 - xl},
    )
    swap.start()
    right_steps = zs // 2
    left_steps = zs - 1 - right_steps

    def pass_on(block, lane, step, send_sem, recv_sem, ahead):
        half_block = weight.at[block, lax.rem(xl + lane, 2)]
        return pltpu.make_async_remote_copy(
            src_ref=half_block,
            dst_ref=half_block,
            send_sem=send_sem.at[lane, step],
            recv_sem=recv_sem.at[lane, step],
            device_id={"z": lax.rem(z + ahead, zs)},
        )

    def right_copy(lane, step):
        return pass_on(lax.rem(z + zs - step, zs), lane, step, right_send, right_recv, 1)

    def left_copy(lane, step):
        return pass_on(lax.rem(z + step, zs), lane, step, left_send, left_recv, zs - 1)

    def landing(lane, step, shift, sem):
        landed_at = weight.at[lax.rem(z + shift, zs), lax.rem(xl + lane, 2)]
        pltpu.make_async_copy(landed_at, landed_at, sem.at[lane, step]).wait()

    def ring(lane, step):
        if step > right_steps:
            return
        if step == 0 and lane == 0:
            weight_load.wait()
        if step == 0 and lane == 1:
            swap.wait_recv()
        if 0 < step <= right_steps:
            landing(lane, step - 1, zs - step, right_recv)
        if 0 < step <= left_steps:
            landing(lane, step - 1, step, left_recv)
        if step < right_steps:
            right_copy(lane, step).start()
        if step < left_steps:
            left_copy(lane, step).start()

    ring(0, 0)
    h_pair[:, my_rows, :] = h_own[pl.ds(core, 1)].reshape(chips, CH, rows)
    h_copy.wait_recv()
    h_send[...] = h_pair[...].astype(BF16)
    send_all(z, xh, h_send, h_recv, far_send.at[0], far_recv.at[0])
    ring(1, 0)

    x_load.wait()
    small[0].wait()
    small[1].wait()
    x_copy.wait_recv()
    halo_copy(0).wait_recv()
    features = []
    for s in range(3):
        raw = x_all[s].astype(F32)
        first = jnp.where(me == 0, 0.0, raw[:halo])
        raw = jnp.concatenate([first, raw[halo:]], axis=0)
        total = taps[s, 0:1, mine] * raw[halo:]
        for back in range(1, taps.shape[1]):
            total = total + taps[s, back : back + 1, mine] * raw[halo - back : halo - back + 2 * rows]
        features.append(total)
    query, mixed_in = features[0], features[1] * features[2]
    flipped = mixed_in.T.reshape(chips, CH, 2 * rows)
    u_send[...] = jnp.concatenate([flipped[:, :, :rows], flipped[:, :, rows:]], axis=1).astype(BF16)
    send_all(z, xh, u_send, u_recv, far_send.at[1], far_recv.at[1])
    ring(0, 1)
    query_t[...] = query.T
    skip_t[...] = (skip[:, mine] * mixed_in).T

    for load in small[2:]:
        load.wait()
    a_fwd[...] = jnp.concatenate(high_low(a_table[...]), axis=1)
    high, low = high_low(b_table[...])
    b_dft[...] = jnp.concatenate([high, high, low], axis=0)
    high, low = high_low(a_back[...])
    a_inv[...] = jnp.concatenate([high, high, low], axis=1)
    ring(1, 1)
    for group in range(4):
        wait_group(h_recv, far_recv.at[0], group, 3)
    t_re, t_im = t_both[0], t_both[1]
    h_freq = spectrum(h_recv, scratch, a_fwd, t_re, t_im, b_dft)
    for group in range(4):
        wait_group(u_recv, far_recv.at[1], group, 3)
        if group == 0:
            ring(0, 2)
            ring(1, 2)
    u_freq = spectrum(u_recv, scratch, a_fwd, t_re, t_im, b_dft)
    width = t_re.shape[1]
    h_re, h_im = h_freq[:, :width], h_freq[:, width:]
    u_re, u_im = u_freq[:, :width], u_freq[:, width:]
    product = jnp.concatenate([h_re * u_im + h_im * u_re, h_re * u_re - h_im * u_im], axis=1)
    inverse(product, scratch, t_re, t_im, b_dft, a_inv)
    y_send[...] = scratch[...].reshape(y_send.shape).astype(BF16)
    send_all(z, xh, y_send, y_recv, far_send.at[2], far_recv.at[2], near_first=True)
    ring(0, 3)
    ring(1, 3)
    ring(0, 4)
    ring(1, 4)

    tokens = 2 * rows
    turns = zs // 4
    pairs = 2 * CH
    across = lax.rem(x + 2, 4)

    def g_copy(kind, group, which, device_id):
        part = g_all.at[which // 2, lax.rem(which, 2), core, pl.ds(group * turns, turns)]
        return pltpu.make_async_remote_copy(
            src_ref=part,
            dst_ref=part,
            send_sem=g_send.at[kind, group],
            recv_sem=g_recv.at[kind, group],
            device_id=device_id,
        )

    def g_copies(kind, which, device_id):
        return [g_copy(kind, group, which, device_id) for group in range(4)]

    to_across = g_copies(0, x, {"xh": 1 - xh})
    to_up = g_copies(1, x, up_x)
    to_down = g_copies(2, x, down_x)
    share = g_copies(3, x, {"core": other})
    share_across = g_copies(4, across, {"core": other})
    share_down = g_copies(5, down, {"core": other})
    share_up = g_copies(6, up, {"core": other})
    for group in range(4):
        wait_group(y_recv, far_recv.at[2], group, 0)
        for turn in range(group * turns, (group + 1) * turns):
            origin = lax.rem(z + zs - hops(turn), zs)
            source = pl.ds(pl.multiple_of(origin * pairs, pairs), pairs)
            back = y_recv[pl.ds(2 * turn, 2)].astype(F32)
            convolved = jnp.concatenate(
                [back[:, CH * b : CH * (b + 1), :].reshape(pairs, rows) for b in range(2)], axis=1
            )
            value = query_t[source, :] * (convolved + skip_t[source, :])
            g_all[pl.ds(xh, 1), pl.ds(xl, 1), pl.ds(core, 1), turn] = value.astype(BF16).reshape(
                1, 1, 1, pairs, tokens
            )
        to_across[group].start()
        to_up[group].start()
        to_down[group].start()
        share[group].start()
        if group in (1, 3):
            ring(0, 5 + group // 3)
            ring(1, 5 + group // 3)
    for group in range(4):
        to_up[group].wait_recv()
        share_down[group].start()
        to_down[group].wait_recv()
        share_up[group].start()
    ring(0, 7)
    ring(1, 7)
    for group in range(4):
        to_across[group].wait_recv()
        share_across[group].start()

    owners = 2 * ys
    owner_me = y * 2 + xl
    wide = per_owner * columns

    def order(far):
        which_x = 1 - xh if far else xh
        for part in range(2):
            for c in range(2):
                for block in range(zs):
                    shift = lax.rem(z + zs - block, zs)
                    shift = jnp.where(shift < zs // 2, shift, shift - zs)
                    turn = jnp.where(shift < 0, -2 * shift - 1, 2 * shift)
                    start = c * half + block * pairs
                    g_ordered[far, part, start : start + pairs, :] = g_all[
                        pl.ds(which_x, 1), part, c, pl.ds(turn, 1)
                    ].reshape(pairs, tokens)

    def send(which_x, b, to):
        pltpu.make_async_remote_copy(
            src_ref=parts.at[which_x, b, to],
            dst_ref=landed.at[x * 2 + core, y],
            send_sem=part_send,
            recv_sem=part_recv.at[x * 2 + core, y],
            device_id={"xh": which_x, "xl": lax.rem(to, 2), "core": b, "y": to // 2},
        ).start()

    def project(far, first, count):
        which_x = 1 - xh if far else xh
        targets = [
            lax.rem(z // per_owner + owners + first + lax.rem(y + k, count), owners)
            for k in range(count)
        ]
        product = jnp.zeros((count * wide, tokens), F32)
        for part in range(2):
            left = [
                weight[pl.ds(to * per_owner, per_owner), part].reshape(wide, 2 * half)
                for to in targets
            ]
            product = product + dot(jnp.concatenate(left, axis=0), g_ordered[far, part])
        for k, to in enumerate(targets):
            for b in range(2):
                value = product[k * wide : (k + 1) * wide, b * rows : (b + 1) * rows]
                parts[pl.ds(which_x, 1), b, pl.ds(to, 1)] = value.astype(BF16).reshape(
                    1, 1, wide, rows
                )
                if far:
                    send(which_x, b, to)
                    continue
                stays = (b == core) & (to == owner_me)

                @pl.when(jnp.logical_not(stays))
                def _():
                    send(which_x, b, to)

                @pl.when(stays)
                def _():
                    landed[pl.ds(x * 2 + core, 1), pl.ds(y, 1)] = parts[
                        pl.ds(which_x, 1), b, pl.ds(to, 1)
                    ].reshape(1, 1, wide, rows)

    near = min(7, owners)
    for group in range(4):
        share[group].wait_recv()

        @pl.when(xl == 0)
        def _():
            share_up[group].wait_recv()

        @pl.when(xl == 1)
        def _():
            share_down[group].wait_recv()

    order(0)
    project(0, -(near // 2), near)
    for group in range(4):
        share_across[group].wait_recv()

        @pl.when(xl == 1)
        def _():
            share_up[group].wait_recv()

        @pl.when(xl == 0)
        def _():
            share_down[group].wait_recv()

    order(1)
    project(1, -(near // 2), near)
    if near < owners:
        for step in range(8, right_steps + 1):
            ring(0, step)
            ring(1, step)
        project(1, near - near // 2, owners - near)
        project(0, near - near // 2, owners - near)

    def arrived(k, carry):
        index = lax.rem(my_index + k, everyone)
        which, owner = index // ys, lax.rem(index, ys)
        block = landed.at[which, owner]
        pltpu.make_async_copy(block, block, part_recv.at[which, owner]).wait()
        return carry

    lax.fori_loop(1, everyone, arrived, 0)
    sums = []
    for which in range(8):
        total = landed[which, 0].astype(F32)
        for source in range(1, ys):
            total = total + landed[which, source].astype(F32)
        sums.append(total)
    order = [a * 4 + c * 2 + b for a in range(2) for b in range(2) for c in range(2)]
    pieces = [
        sums[which][part * columns : (part + 1) * columns]
        for part in range(per_owner)
        for which in order
    ]
    out[...] = jnp.concatenate(pieces, axis=0).T.astype(out.dtype)

    h_copy.wait_send()
    x_copy.wait_send()

    @pl.when(core == 1)
    def _():
        halo_copy(0).wait_send()
        halo_copy(1).wait_send()

    swap.wait_send()
    for step in range(right_steps):
        for lane in range(2):
            right_copy(lane, step).wait_send()
    for step in range(left_steps):
        for lane in range(2):
            left_copy(lane, step).wait_send()
    wait_blocks(chips - 1, h_send, far_send.at[0])
    wait_blocks(chips - 1, u_send, far_send.at[1])
    wait_blocks(chips - 1, y_send, far_send.at[2])
    for group in (to_across, to_up, to_down, share, share_across, share_down, share_up):
        for copy in group:
            copy.wait_send()
    pltpu.make_async_copy(parts.at[1], parts.at[1], part_send).wait()
    pltpu.make_async_copy(parts.at[0, 1], parts.at[0, 1], part_send).wait()
    sent = parts.at[0, 0, pl.ds(1, owners - 1)]
    pltpu.make_async_copy(sent, sent, part_send).wait()


def body(qkv_in, short_taps, long_filter, skip_gain, out_weight):
    rows, _, channels = qkv_in.shape
    half = channels // 2
    zs = lax.axis_size("z")
    chips = zs * 2
    ys = lax.axis_size("y")
    blocks = 2 * chips
    columns = out_weight.shape[1] // 2
    wide = zs // (2 * ys) * columns
    lookup = tables(blocks, rows)
    exchange = (chips, 2 * CH, rows)
    dma = pltpu.SemaphoreType.DMA
    return pl.pallas_call(
        mixer_kernel,
        out_shape=jax.ShapeDtypeStruct((rows, channels), BF16),
        in_specs=[pl.BlockSpec(memory_space=pl.ANY)] * 9,
        out_specs=VMEM,
        scratch_shapes=[
            pltpu.VMEM(short_taps.shape, F32),
            pltpu.VMEM((rows, channels), F32),
            pltpu.VMEM((1, channels), F32),
            *[pltpu.VMEM(table.shape, table.dtype) for table in lookup],
            pltpu.VMEM((2 * blocks, 2 * blocks), BF16),
            pltpu.VMEM((6 * rows, 2 * rows), BF16),
            pltpu.VMEM((blocks, 6 * blocks), BF16),
            pltpu.VMEM((2, chips, CH, rows), F32),
            pltpu.VMEM(exchange, F32),
            pltpu.VMEM(exchange, BF16),
            pltpu.VMEM(exchange, BF16),
            pltpu.VMEM((3, 16 + 2 * rows, half), BF16),
            pltpu.VMEM(exchange, BF16),
            pltpu.VMEM(exchange, BF16),
            pltpu.VMEM(exchange, BF16),
            pltpu.VMEM(exchange, BF16),
            pltpu.VMEM((blocks * CH, rows), F32),
            pltpu.VMEM((zs, 2, columns, channels), BF16),
            pltpu.VMEM((half, 2 * rows), F32),
            pltpu.VMEM((half, 2 * rows), F32),
            pltpu.VMEM((2, 2, 2, zs, 2 * CH, 2 * rows), BF16),
            pltpu.VMEM((2, 2, channels, 2 * rows), BF16),
            pltpu.VMEM((2, 2, 2 * ys, wide, rows), BF16),
            pltpu.VMEM((8, ys, wide, rows), BF16),
            dma((9,)),
            dma((5,)),
            dma((4,)),
            dma((3,)),
            dma((3, 4)),
            dma((2, zs)),
            dma((2, zs)),
            dma((2, zs)),
            dma((2, zs)),
            dma((7, 4)),
            dma((7, 4)),
            dma,
            dma((8, ys)),
        ],
        compiler_params=pltpu.CompilerParams(
            collective_id=0, has_side_effects=True, vmem_limit_bytes=60 * 2**20
        ),
        name="mixer",
    )(
        qkv_in.transpose(1, 0, 2),
        short_taps,
        long_filter,
        skip_gain[None, :],
        out_weight.T,
        *lookup,
    )


def solution(mesh):
    sizes = dict(mesh.shape)
    split = Mesh(
        mesh.devices.reshape(sizes["ctx"] // 4, 2, 2, sizes["tp"] // 2, 2),
        ("z", "xh", "core", "y", "xl"),
    )
    ctx, tp = ("z", "xh", "core"), ("y", "xl")
    return jax.shard_map(
        body,
        mesh=split,
        in_specs=(P(ctx, None, tp), P(None, None, tp), P(ctx, tp), P(tp), P(tp, ctx)),
        out_specs=P(ctx, tp),
        check_vma=False,
    )
```

```python
import jax
import jax.numpy as jnp
import numpy as np
from jax import lax
from jax.experimental import pallas as pl
from jax.experimental.pallas import tpu as pltpu
from jax.sharding import Mesh, PartitionSpec as P

F32 = jnp.float32
BF16 = jnp.bfloat16
CH = 8
VMEM = pl.BlockSpec(memory_space=pltpu.VMEM)


def tables(blocks, width):
    length = blocks * width
    f1 = np.arange(blocks)[:, None]
    a = np.exp(-2j * np.pi * ((np.arange(blocks)[None, :] * (4 * f1 + 1)) % (4 * blocks)) / (4 * blocks))
    t = np.exp(-2j * np.pi * (np.arange(width)[None, :] * (4 * f1 + 1)) / (4 * length))
    i = np.arange(width)
    b = np.exp(-2j * np.pi * ((i[:, None] * i[None, :]) % width) / width)
    found = (
        np.concatenate([a.real, a.imag], 0),
        np.stack([t.real, t.imag]),
        np.block([[b.real, b.imag], [-b.imag, b.real]]),
        np.concatenate([a.real.T, a.imag.T], 1) / length,
    )
    return [jnp.asarray(table.astype(np.float32)) for table in found]


def dot(left, right):
    return jnp.dot(left, right, preferred_element_type=F32)


def high_low(value):
    high = value.astype(BF16)
    return high, (value - high.astype(F32)).astype(BF16)


def hops(turn):
    if isinstance(turn, int):
        return -((turn + 1) // 2) if turn % 2 else turn // 2
    return jnp.where(lax.rem(turn, 2) == 1, -((turn + 1) // 2), turn // 2)


def send_all(z, xh, source, target, send_sem, recv_sems, near_first=False):
    zs = lax.axis_size("z")
    me = z * 2 + xh
    size = 2 * zs // recv_sems.shape[0]

    def step(k, carry):
        turn = k // 2
        ahead = hops(turn) + (zs if near_first else zs // 2)
        to_z = lax.rem(z + ahead, zs)
        to_x = jnp.where(lax.rem(k, 2) == 0, 1 - xh, xh)
        pltpu.make_async_remote_copy(
            src_ref=source.at[to_z * 2 + to_x],
            dst_ref=target.at[turn * 2 + xh if near_first else me],
            send_sem=send_sem,
            recv_sem=recv_sems.at[k // size],
            device_id={"z": to_z, "xh": to_x},
        ).start()
        return carry

    if near_first:
        lax.fori_loop(2 * zs - size, 2 * zs, step, 0)
        step(0, 0)
        lax.fori_loop(2, 2 * zs - size, step, 0)
    else:
        lax.fori_loop(0, 2 * zs - 1, step, 0)
    slot = xh if near_first else me
    target[pl.ds(slot, 1)] = source[pl.ds(me, 1)]


def wait_blocks(count, ref, sem):
    part = ref.at[pl.ds(0, count)]
    pltpu.make_async_copy(part, part, sem).wait()


def wait_group(ref, sems, group, short):
    size = ref.shape[0] // sems.shape[0]
    wait_blocks(size - (group == short), ref, sems.at[group])


def spectrum(received, scratch, a_fwd, t_re, t_im, b_dft):
    rows = scratch.shape[0]
    blocks = rows // CH
    scratch[...] = received[...].astype(F32).reshape(rows, -1)
    columns = [scratch[pl.ds(c, blocks, stride=CH), :].astype(BF16) for c in range(CH)]
    signal = jnp.concatenate(columns, axis=1)
    mixed = dot(a_fwd[...], jnp.concatenate([signal, signal], axis=0))
    width = t_re.shape[1]
    parts = []
    for c in range(CH):
        re = mixed[:blocks, c * width : (c + 1) * width]
        im = mixed[blocks:, c * width : (c + 1) * width]
        parts.append(
            jnp.concatenate(
                [re * t_re - im * t_im, re * t_im + im * t_re], axis=1
            )
        )
    high, low = high_low(jnp.concatenate(parts, axis=0))
    return dot(jnp.concatenate([high, low, high], axis=1), b_dft[...])


def inverse(product, scratch, t_re, t_im, b_dft, a_inv):
    blocks, width = t_re.shape
    high, low = high_low(product)
    back = dot(jnp.concatenate([high, low, high], axis=1), b_dft[...])
    parts = []
    for c in range(CH):
        im = back[c * blocks : (c + 1) * blocks, :width]
        re = back[c * blocks : (c + 1) * blocks, width:]
        parts.append(
            jnp.concatenate(
                [re * t_re + im * t_im, im * t_re - re * t_im], axis=0
            )
        )
    high, low = high_low(jnp.concatenate(parts, axis=1))
    result = dot(a_inv[...], jnp.concatenate([high, low, high], axis=0))
    for c in range(CH):
        scratch[pl.ds(c, blocks, stride=CH), :] = result[:, c * width : (c + 1) * width]


def local_copy(source, target, sem):
    copy = pltpu.make_async_copy(source, target, sem)
    copy.start()
    return copy


def mixer_kernel(
    qkv_hbm, taps_hbm, filt_hbm, skip_hbm, weight_hbm,
    a_fwd_hbm, t_hbm, b_dft_hbm, a_inv_hbm,
    out,
    taps, filt, skip, a_table, t_both, b_table, a_back, a_fwd, b_dft, a_inv,
    h_own, h_pair, h_send, h_recv, x_all, u_send, u_recv, y_send, y_recv, scratch,
    weight, query_t, skip_t, g_all, g_ordered, parts, landed,
    load_sem, near_send, near_recv, far_send, far_recv,
    right_send, right_recv, left_send, left_recv, g_send, g_recv, part_send, part_recv,
):
    z, xh, core = lax.axis_index("z"), lax.axis_index("xh"), lax.axis_index("core")
    y, xl = lax.axis_index("y"), lax.axis_index("xl")
    zs, ys = lax.axis_size("z"), lax.axis_size("y")
    chips = zs * 2
    per_owner = zs // (2 * ys)
    me = z * 2 + xh
    other = 1 - core
    rows = qkv_hbm.shape[1]
    half = chips * CH
    halo = 16
    mine = pl.ds(pl.multiple_of(core * half, half), half)
    theirs = pl.ds(pl.multiple_of(other * half, half), half)
    place = pl.ds(pl.multiple_of(halo + core * rows, 16), rows)
    x = xh * 2 + xl
    everyone = 8 * ys
    my_index = (x * 2 + core) * ys + y
    up, down = lax.rem(x + 1, 4), lax.rem(x + 3, 4)
    up_x = {"xh": up // 2, "xl": lax.rem(up, 2)}
    down_x = {"xh": down // 2, "xl": lax.rem(down, 2)}
    columns = weight.shape[2]

    barrier = pltpu.get_barrier_semaphore()
    step_to = lax.rem(me + jnp.where(core == 1, 1, chips - 1), chips)
    pl.semaphore_signal(
        barrier, inc=1, device_id={"z": step_to // 2, "xh": lax.rem(step_to, 2), "core": other}
    )


    def place_of(index):
        which = index // ys
        return {
            "xh": which // 4,
            "xl": lax.rem(which // 2, 2),
            "core": lax.rem(which, 2),
            "y": lax.rem(index, ys),
        }

    def greet_ctx(k, carry):
        peer = lax.rem(me + k, chips)
        pl.semaphore_signal(
            barrier, inc=1, device_id={"z": peer // 2, "xh": lax.rem(peer, 2)}
        )
        return carry

    def greet_plane(k, carry):
        pl.semaphore_signal(barrier, inc=1, device_id=place_of(lax.rem(my_index + k, everyone)))
        return carry

    lax.fori_loop(1, chips, greet_ctx, 0)
    lax.fori_loop(1, everyone, greet_plane, 0)

    filt_load = local_copy(filt_hbm, filt, load_sem.at[0])
    x_load = local_copy(qkv_hbm.at[:, :, mine], x_all.at[:, place, :], load_sem.at[1])
    weight_load = local_copy(
        weight_hbm.at[pl.ds(pl.multiple_of(xl * columns, columns), columns), :],
        weight.at[z, xl],
        load_sem.at[2],
    )
    small = [
        local_copy(source, target, load_sem.at[3 + k])
        for k, (source, target) in enumerate(
            [
                (taps_hbm, taps),
                (skip_hbm, skip),
                (a_fwd_hbm, a_table),
                (t_hbm, t_both),
                (b_dft_hbm, b_table),
                (a_inv_hbm, a_back),
            ]
        )
    ]

    filt_load.wait()
    turned = filt[...].T.reshape(2, chips, CH, rows)
    h_send[...] = jnp.concatenate([turned[0], turned[1]], axis=1).astype(BF16)
    pl.semaphore_wait(barrier, 1 + chips - 1 + everyone - 1)

    x_copy = pltpu.make_async_remote_copy(
        src_ref=qkv_hbm.at[:, :, theirs],
        dst_ref=x_all.at[:, place, :],
        send_sem=near_send.at[1],
        recv_sem=near_recv.at[1],
        device_id={"core": other},
    )
    x_copy.start()

    after = lax.rem(me + 1, chips)

    def halo_copy(target):
        return pltpu.make_async_remote_copy(
            src_ref=qkv_hbm.at[:, pl.ds(rows - halo, halo), pl.ds(target * half, half)],
            dst_ref=x_all.at[:, pl.ds(0, halo), :],
            send_sem=near_send.at[2 + target],
            recv_sem=near_recv.at[2],
            device_id={"z": after // 2, "xh": lax.rem(after, 2), "core": target},
        )

    @pl.when(core == 1)
    def _():
        halo_copy(0).start()
        halo_copy(1).start()

    send_all(z, xh, h_send, h_recv, far_send.at[0], far_recv.at[0])

    swap = pltpu.make_async_remote_copy(
        src_ref=weight_hbm.at[pl.ds(pl.multiple_of((1 - xl) * columns, columns), columns), :],
        dst_ref=weight.at[z, xl],
        send_sem=near_send.at[4],
        recv_sem=near_recv.at[3],
        device_id={"xl": 1 - xl},
    )
    swap.start()
    right_steps = zs // 2
    left_steps = zs - 1 - right_steps

    def pass_on(block, lane, step, send_sem, recv_sem, ahead):
        half_block = weight.at[block, lax.rem(xl + lane, 2)]
        return pltpu.make_async_remote_copy(
            src_ref=half_block,
            dst_ref=half_block,
            send_sem=send_sem.at[lane, step],
            recv_sem=recv_sem.at[lane, step],
            device_id={"z": lax.rem(z + ahead, zs)},
        )

    def right_copy(lane, step):
        return pass_on(lax.rem(z + zs - step, zs), lane, step, right_send, right_recv, 1)

    def left_copy(lane, step):
        return pass_on(lax.rem(z + step, zs), lane, step, left_send, left_recv, zs - 1)

    def landing(lane, step, shift, sem):
        landed_at = weight.at[lax.rem(z + shift, zs), lax.rem(xl + lane, 2)]
        pltpu.make_async_copy(landed_at, landed_at, sem.at[lane, step]).wait()

    def ring(lane, step):
        if step > right_steps:
            return
        if step == 0 and lane == 0:
            weight_load.wait()
        if step == 0 and lane == 1:
            swap.wait_recv()
        if 0 < step <= right_steps:
            landing(lane, step - 1, zs - step, right_recv)
        if 0 < step <= left_steps:
            landing(lane, step - 1, step, left_recv)
        if step < right_steps:
            right_copy(lane, step).start()
        if step < left_steps:
            left_copy(lane, step).start()

    ring(0, 0)
    ring(1, 0)

    x_load.wait()
    small[0].wait()
    small[1].wait()
    x_copy.wait_recv()
    halo_copy(0).wait_recv()

    def feature(kind):
        raw = x_all[kind].astype(F32)
        first = jnp.where(me == 0, 0.0, raw[:halo])
        raw = jnp.concatenate([first, raw[halo:]], axis=0)
        total = taps[kind, 0:1, mine] * raw[halo:]
        for back in range(1, taps.shape[1]):
            shifted = raw[halo - back : halo - back + 2 * rows]
            total = total + taps[kind, back : back + 1, mine] * shifted
        return total

    mixed_in = feature(1) * feature(2)
    flipped = mixed_in.T.reshape(chips, CH, 2 * rows)
    u_send[...] = jnp.concatenate([flipped[:, :, :rows], flipped[:, :, rows:]], axis=1).astype(BF16)
    send_all(z, xh, u_send, u_recv, far_send.at[1], far_recv.at[1])
    ring(0, 1)
    query_t[...] = feature(0).T
    skip_t[...] = (skip[:, mine] * mixed_in).T

    for load in small[2:]:
        load.wait()
    a_fwd[...] = jnp.concatenate(high_low(a_table[...]), axis=1)
    high, low = high_low(b_table[...])
    b_dft[...] = jnp.concatenate([high, high, low], axis=0)
    high, low = high_low(a_back[...])
    a_inv[...] = jnp.concatenate([high, high, low], axis=1)
    ring(1, 1)
    for group in range(4):
        wait_group(h_recv, far_recv.at[0], group, 3)
    my_rows = pl.ds(pl.multiple_of(core * CH, CH), CH)
    their_rows = pl.ds(pl.multiple_of(other * CH, CH), CH)
    h_own[...] = h_recv[...].astype(F32)
    h_copy = pltpu.make_async_remote_copy(
        src_ref=h_own.at[:, their_rows, :],
        dst_ref=h_pair.at[:, my_rows, :],
        send_sem=near_send.at[0],
        recv_sem=near_recv.at[0],
        device_id={"core": other},
    )
    h_copy.start()
    h_pair[:, my_rows, :] = h_own[:, my_rows, :]
    h_copy.wait_recv()
    t_re, t_im = t_both[0], t_both[1]
    h_freq = spectrum(h_pair, scratch, a_fwd, t_re, t_im, b_dft)
    for group in range(4):
        wait_group(u_recv, far_recv.at[1], group, 3)
        if group == 0:
            ring(0, 2)
            ring(1, 2)
    u_freq = spectrum(u_recv, scratch, a_fwd, t_re, t_im, b_dft)
    width = t_re.shape[1]
    h_re, h_im = h_freq[:, :width], h_freq[:, width:]
    u_re, u_im = u_freq[:, :width], u_freq[:, width:]
    product = jnp.concatenate([h_re * u_im + h_im * u_re, h_re * u_re - h_im * u_im], axis=1)
    inverse(product, scratch, t_re, t_im, b_dft, a_inv)
    y_send[...] = scratch[...].reshape(y_send.shape).astype(BF16)
    send_all(z, xh, y_send, y_recv, far_send.at[2], far_recv.at[2], near_first=True)
    ring(0, 3)
    ring(1, 3)
    ring(0, 4)
    ring(1, 4)

    tokens = 2 * rows
    turns = zs // 4
    pairs = 2 * CH
    across = lax.rem(x + 2, 4)

    def g_copy(kind, group, which, device_id):
        part = g_all.at[which // 2, lax.rem(which, 2), core, pl.ds(group * turns, turns)]
        return pltpu.make_async_remote_copy(
            src_ref=part,
            dst_ref=part,
            send_sem=g_send.at[kind, group],
            recv_sem=g_recv.at[kind, group],
            device_id=device_id,
        )

    def g_copies(kind, which, device_id):
        return [g_copy(kind, group, which, device_id) for group in range(4)]

    to_across = g_copies(0, x, {"xh": 1 - xh})
    to_up = g_copies(1, x, up_x)
    to_down = g_copies(2, x, down_x)
    share = g_copies(3, x, {"core": other})
    share_across = g_copies(4, across, {"core": other})
    share_down = g_copies(5, down, {"core": other})
    share_up = g_copies(6, up, {"core": other})
    for group in range(4):
        wait_group(y_recv, far_recv.at[2], group, 0)
        for turn in range(group * turns, (group + 1) * turns):
            origin = lax.rem(z + zs - hops(turn), zs)
            source = pl.ds(pl.multiple_of(origin * pairs, pairs), pairs)
            back = y_recv[pl.ds(2 * turn, 2)].astype(F32)
            convolved = jnp.concatenate(
                [back[:, CH * b : CH * (b + 1), :].reshape(pairs, rows) for b in range(2)], axis=1
            )
            value = query_t[source, :] * (convolved + skip_t[source, :])
            g_all[pl.ds(xh, 1), pl.ds(xl, 1), pl.ds(core, 1), turn] = value.astype(BF16).reshape(
                1, 1, 1, pairs, tokens
            )
        to_across[group].start()
        to_up[group].start()
        to_down[group].start()
        share[group].start()
        if group == 3:
            ring(0, 5)
            ring(1, 5)
    for group in range(4):
        to_up[group].wait_recv()
        share_down[group].start()
        to_down[group].wait_recv()
        share_up[group].start()
    ring(0, 6)
    ring(1, 6)
    for group in range(4):
        to_across[group].wait_recv()
        share_across[group].start()

    owners = 2 * ys
    owner_me = y * 2 + xl
    wide = per_owner * columns

    def order(far):
        which_x = 1 - xh if far else xh
        for part in range(2):
            for c in range(2):
                for block in range(zs):
                    shift = lax.rem(z + zs - block, zs)
                    shift = jnp.where(shift < zs // 2, shift, shift - zs)
                    turn = jnp.where(shift < 0, -2 * shift - 1, 2 * shift)
                    start = c * half + block * pairs
                    g_ordered[far, part, start : start + pairs, :] = g_all[
                        pl.ds(which_x, 1), part, c, pl.ds(turn, 1)
                    ].reshape(pairs, tokens)

    def send(which_x, b, to):
        pltpu.make_async_remote_copy(
            src_ref=parts.at[which_x, b, to],
            dst_ref=landed.at[x * 2 + core, y],
            send_sem=part_send,
            recv_sem=part_recv.at[x * 2 + core, y],
            device_id={"xh": which_x, "xl": lax.rem(to, 2), "core": b, "y": to // 2},
        ).start()

    def project(far, first, count):
        which_x = 1 - xh if far else xh
        targets = [
            lax.rem(z // per_owner + owners + first + lax.rem(y + k, count), owners)
            for k in range(count)
        ]
        product = jnp.zeros((count * wide, tokens), F32)
        for part in range(2):
            left = [
                weight[pl.ds(to * per_owner, per_owner), part].reshape(wide, 2 * half)
                for to in targets
            ]
            product = product + dot(jnp.concatenate(left, axis=0), g_ordered[far, part])
        for k, to in enumerate(targets):
            for b in range(2):
                value = product[k * wide : (k + 1) * wide, b * rows : (b + 1) * rows]
                parts[pl.ds(which_x, 1), b, pl.ds(to, 1)] = value.astype(BF16).reshape(
                    1, 1, wide, rows
                )
                if far:
                    send(which_x, b, to)
                    continue
                stays = (b == core) & (to == owner_me)

                @pl.when(jnp.logical_not(stays))
                def _():
                    send(which_x, b, to)

                @pl.when(stays)
                def _():
                    landed[pl.ds(x * 2 + core, 1), pl.ds(y, 1)] = parts[
                        pl.ds(which_x, 1), b, pl.ds(to, 1)
                    ].reshape(1, 1, wide, rows)

    near, nearer = min(7, owners), min(5, owners)
    for group in range(4):
        share[group].wait_recv()

        @pl.when(xl == 0)
        def _():
            share_up[group].wait_recv()

        @pl.when(xl == 1)
        def _():
            share_down[group].wait_recv()

    order(0)
    project(0, -(nearer // 2), nearer)
    ring(0, 7)
    ring(1, 7)
    for group in range(4):
        share_across[group].wait_recv()

        @pl.when(xl == 1)
        def _():
            share_up[group].wait_recv()

        @pl.when(xl == 0)
        def _():
            share_down[group].wait_recv()

    order(1)
    project(1, -(near // 2), near)
    for step in range(8, right_steps + 1):
        ring(0, step)
        ring(1, step)
    if near < owners:
        project(1, near - near // 2, owners - near)
    if nearer < owners:
        project(0, nearer - nearer // 2, owners - nearer)

    def arrived(k, carry):
        index = lax.rem(my_index + k, everyone)
        which, owner = index // ys, lax.rem(index, ys)
        block = landed.at[which, owner]
        pltpu.make_async_copy(block, block, part_recv.at[which, owner]).wait()
        return carry

    lax.fori_loop(1, everyone, arrived, 0)
    sums = []
    for which in range(8):
        total = landed[which, 0].astype(F32)
        for source in range(1, ys):
            total = total + landed[which, source].astype(F32)
        sums.append(total)
    order = [a * 4 + c * 2 + b for a in range(2) for b in range(2) for c in range(2)]
    pieces = [
        sums[which][part * columns : (part + 1) * columns]
        for part in range(per_owner)
        for which in order
    ]
    out[...] = jnp.concatenate(pieces, axis=0).T.astype(out.dtype)

    h_copy.wait_send()
    x_copy.wait_send()

    @pl.when(core == 1)
    def _():
        halo_copy(0).wait_send()
        halo_copy(1).wait_send()

    swap.wait_send()
    for step in range(right_steps):
        for lane in range(2):
            right_copy(lane, step).wait_send()
    for step in range(left_steps):
        for lane in range(2):
            left_copy(lane, step).wait_send()
    wait_blocks(chips - 1, h_send, far_send.at[0])
    wait_blocks(chips - 1, u_send, far_send.at[1])
    wait_blocks(chips - 1, y_send, far_send.at[2])
    for group in (to_across, to_up, to_down, share, share_across, share_down, share_up):
        for copy in group:
            copy.wait_send()
    pltpu.make_async_copy(parts.at[1], parts.at[1], part_send).wait()
    pltpu.make_async_copy(parts.at[0, 1], parts.at[0, 1], part_send).wait()
    sent = parts.at[0, 0, pl.ds(1, owners - 1)]
    pltpu.make_async_copy(sent, sent, part_send).wait()


def body(qkv_in, short_taps, long_filter, skip_gain, out_weight):
    rows, _, channels = qkv_in.shape
    half = channels // 2
    zs = lax.axis_size("z")
    chips = zs * 2
    ys = lax.axis_size("y")
    blocks = 2 * chips
    columns = out_weight.shape[1] // 2
    wide = zs // (2 * ys) * columns
    lookup = tables(blocks, rows)
    exchange = (chips, 2 * CH, rows)
    dma = pltpu.SemaphoreType.DMA
    return pl.pallas_call(
        mixer_kernel,
        out_shape=jax.ShapeDtypeStruct((rows, channels), BF16),
        in_specs=[pl.BlockSpec(memory_space=pl.ANY)] * 9,
        out_specs=VMEM,
        scratch_shapes=[
            pltpu.VMEM(short_taps.shape, F32),
            pltpu.VMEM((rows, channels), F32),
            pltpu.VMEM((1, channels), F32),
            *[pltpu.VMEM(table.shape, table.dtype) for table in lookup],
            pltpu.VMEM((2 * blocks, 2 * blocks), BF16),
            pltpu.VMEM((6 * rows, 2 * rows), BF16),
            pltpu.VMEM((blocks, 6 * blocks), BF16),
            pltpu.VMEM(exchange, F32),
            pltpu.VMEM(exchange, F32),
            pltpu.VMEM(exchange, BF16),
            pltpu.VMEM(exchange, BF16),
            pltpu.VMEM((3, 16 + 2 * rows, half), BF16),
            pltpu.VMEM(exchange, BF16),
            pltpu.VMEM(exchange, BF16),
            pltpu.VMEM(exchange, BF16),
            pltpu.VMEM(exchange, BF16),
            pltpu.VMEM((blocks * CH, rows), F32),
            pltpu.VMEM((zs, 2, columns, channels), BF16),
            pltpu.VMEM((half, 2 * rows), F32),
            pltpu.VMEM((half, 2 * rows), F32),
            pltpu.VMEM((2, 2, 2, zs, 2 * CH, 2 * rows), BF16),
            pltpu.VMEM((2, 2, channels, 2 * rows), BF16),
            pltpu.VMEM((2, 2, 2 * ys, wide, rows), BF16),
            pltpu.VMEM((8, ys, wide, rows), BF16),
            dma((9,)),
            dma((5,)),
            dma((4,)),
            dma((3,)),
            dma((3, 4)),
            dma((2, zs)),
            dma((2, zs)),
            dma((2, zs)),
            dma((2, zs)),
            dma((7, 4)),
            dma((7, 4)),
            dma,
            dma((8, ys)),
        ],
        compiler_params=pltpu.CompilerParams(
            collective_id=0, has_side_effects=True, vmem_limit_bytes=60 * 2**20
        ),
        name="mixer",
    )(
        qkv_in.transpose(1, 0, 2),
        short_taps,
        long_filter,
        skip_gain[None, :],
        out_weight.T,
        *lookup,
    )


def solution(mesh):
    sizes = dict(mesh.shape)
    split = Mesh(
        mesh.devices.reshape(sizes["ctx"] // 4, 2, 2, sizes["tp"] // 2, 2),
        ("z", "xh", "core", "y", "xl"),
    )
    ctx, tp = ("z", "xh", "core"), ("y", "xl")
    return jax.shard_map(
        body,
        mesh=split,
        in_specs=(P(ctx, None, tp), P(None, None, tp), P(ctx, tp), P(tp), P(tp, ctx)),
        out_specs=P(ctx, tp),
        check_vma=False,
    )
```

```python
import jax
import jax.numpy as jnp
import numpy as np
from jax import lax
from jax.experimental import pallas as pl
from jax.experimental.pallas import tpu as pltpu
from jax.sharding import Mesh, PartitionSpec as P

F32 = jnp.float32
BF16 = jnp.bfloat16
CH = 8
VMEM = pl.BlockSpec(memory_space=pltpu.VMEM)


def tables(blocks, width):
    length = blocks * width
    f1 = np.arange(blocks)[:, None]
    a = np.exp(-2j * np.pi * ((np.arange(blocks)[None, :] * (4 * f1 + 1)) % (4 * blocks)) / (4 * blocks))
    t = np.exp(-2j * np.pi * (np.arange(width)[None, :] * (4 * f1 + 1)) / (4 * length))
    i = np.arange(width)
    b = np.exp(-2j * np.pi * ((i[:, None] * i[None, :]) % width) / width)
    found = (
        np.concatenate([a.real, a.imag], 0),
        np.stack([t.real, t.imag]),
        np.block([[b.real, b.imag], [-b.imag, b.real]]),
        np.concatenate([a.real.T, a.imag.T], 1) / length,
    )
    return [jnp.asarray(table.astype(np.float32)) for table in found]


def dot(left, right):
    return jnp.dot(left, right, preferred_element_type=F32)


def high_low(value):
    high = value.astype(BF16)
    return high, (value - high.astype(F32)).astype(BF16)


def hops(turn):
    if isinstance(turn, int):
        return -((turn + 1) // 2) if turn % 2 else turn // 2
    return jnp.where(lax.rem(turn, 2) == 1, -((turn + 1) // 2), turn // 2)


def send_all(z, xh, source, target, send_sem, recv_sems, near_first=False):
    zs = lax.axis_size("z")
    me = z * 2 + xh
    size = 2 * zs // recv_sems.shape[0]

    def step(k, carry):
        turn = k // 2
        ahead = hops(turn) + (zs if near_first else zs // 2)
        to_z = lax.rem(z + ahead, zs)
        to_x = jnp.where(lax.rem(k, 2) == 0, 1 - xh, xh)
        pltpu.make_async_remote_copy(
            src_ref=source.at[to_z * 2 + to_x],
            dst_ref=target.at[turn * 2 + xh if near_first else me],
            send_sem=send_sem,
            recv_sem=recv_sems.at[k // size],
            device_id={"z": to_z, "xh": to_x},
        ).start()
        return carry

    if near_first:
        lax.fori_loop(2 * zs - size, 2 * zs, step, 0)
        step(0, 0)
        lax.fori_loop(2, 2 * zs - size, step, 0)
    else:
        lax.fori_loop(0, 2 * zs - 1, step, 0)
    slot = xh if near_first else me
    target[pl.ds(slot, 1)] = source[pl.ds(me, 1)]


def wait_blocks(count, ref, sem):
    part = ref.at[pl.ds(0, count)]
    pltpu.make_async_copy(part, part, sem).wait()


def wait_group(ref, sems, group, short):
    size = ref.shape[0] // sems.shape[0]
    wait_blocks(size - (group == short), ref, sems.at[group])


def spectrum(received, scratch, a_fwd, t_re, t_im, b_dft):
    rows = scratch.shape[0]
    blocks = rows // CH
    scratch[...] = received[...].astype(F32).reshape(rows, -1)
    columns = [scratch[pl.ds(c, blocks, stride=CH), :].astype(BF16) for c in range(CH)]
    signal = jnp.concatenate(columns, axis=1)
    mixed = dot(a_fwd[...], jnp.concatenate([signal, signal], axis=0))
    width = t_re.shape[1]
    parts = []
    for c in range(CH):
        re = mixed[:blocks, c * width : (c + 1) * width]
        im = mixed[blocks:, c * width : (c + 1) * width]
        parts.append(
            jnp.concatenate(
                [re * t_re - im * t_im, re * t_im + im * t_re], axis=1
            )
        )
    high, low = high_low(jnp.concatenate(parts, axis=0))
    return dot(jnp.concatenate([high, low, high], axis=1), b_dft[...])


def inverse(product, scratch, t_re, t_im, b_dft, a_inv):
    blocks, width = t_re.shape
    high, low = high_low(product)
    back = dot(jnp.concatenate([high, low, high], axis=1), b_dft[...])
    parts = []
    for c in range(CH):
        im = back[c * blocks : (c + 1) * blocks, :width]
        re = back[c * blocks : (c + 1) * blocks, width:]
        parts.append(
            jnp.concatenate(
                [re * t_re + im * t_im, im * t_re - re * t_im], axis=0
            )
        )
    high, low = high_low(jnp.concatenate(parts, axis=1))
    result = dot(a_inv[...], jnp.concatenate([high, low, high], axis=0))
    for c in range(CH):
        scratch[pl.ds(c, blocks, stride=CH), :] = result[:, c * width : (c + 1) * width]


def local_copy(source, target, sem):
    copy = pltpu.make_async_copy(source, target, sem)
    copy.start()
    return copy


def mixer_kernel(
    qkv_hbm, taps_hbm, filt_hbm, skip_hbm, weight_hbm,
    a_fwd_hbm, t_hbm, b_dft_hbm, a_inv_hbm,
    out,
    taps, filt, skip, a_table, t_both, b_table, a_back, a_fwd, b_dft, a_inv,
    h_own, h_pair, h_send, h_recv, x_all, u_send, u_recv, y_send, y_recv, scratch,
    weight, query_t, skip_t, g_all, g_ordered, parts, landed,
    load_sem, near_send, near_recv, far_send, far_recv,
    right_send, right_recv, left_send, left_recv, g_send, g_recv, part_send, part_recv,
):
    z, xh, core = lax.axis_index("z"), lax.axis_index("xh"), lax.axis_index("core")
    y, xl = lax.axis_index("y"), lax.axis_index("xl")
    zs, ys = lax.axis_size("z"), lax.axis_size("y")
    chips = zs * 2
    per_owner = zs // (2 * ys)
    me = z * 2 + xh
    other = 1 - core
    rows = qkv_hbm.shape[1]
    half = chips * CH
    halo = 16
    mine = pl.ds(pl.multiple_of(core * half, half), half)
    theirs = pl.ds(pl.multiple_of(other * half, half), half)
    place = pl.ds(pl.multiple_of(halo + core * rows, 16), rows)
    x = xh * 2 + xl
    everyone = 8 * ys
    my_index = (x * 2 + core) * ys + y
    up, down = lax.rem(x + 1, 4), lax.rem(x + 3, 4)
    up_x = {"xh": up // 2, "xl": lax.rem(up, 2)}
    down_x = {"xh": down // 2, "xl": lax.rem(down, 2)}
    columns = weight.shape[2]

    barrier = pltpu.get_barrier_semaphore()
    step_to = lax.rem(me + jnp.where(core == 1, 1, chips - 1), chips)
    pl.semaphore_signal(
        barrier, inc=1, device_id={"z": step_to // 2, "xh": lax.rem(step_to, 2), "core": other}
    )


    def place_of(index):
        which = index // ys
        return {
            "xh": which // 4,
            "xl": lax.rem(which // 2, 2),
            "core": lax.rem(which, 2),
            "y": lax.rem(index, ys),
        }

    def greet_ctx(k, carry):
        peer = lax.rem(me + k, chips)
        pl.semaphore_signal(
            barrier, inc=1, device_id={"z": peer // 2, "xh": lax.rem(peer, 2)}
        )
        return carry

    def greet_plane(k, carry):
        pl.semaphore_signal(barrier, inc=1, device_id=place_of(lax.rem(my_index + k, everyone)))
        return carry

    lax.fori_loop(1, chips, greet_ctx, 0)
    lax.fori_loop(1, everyone, greet_plane, 0)

    filt_load = local_copy(filt_hbm, filt, load_sem.at[0])
    x_load = local_copy(qkv_hbm.at[:, :, mine], x_all.at[:, place, :], load_sem.at[1])
    weight_load = local_copy(
        weight_hbm.at[pl.ds(pl.multiple_of(xl * columns, columns), columns), :],
        weight.at[z, xl],
        load_sem.at[2],
    )
    small = [
        local_copy(source, target, load_sem.at[3 + k])
        for k, (source, target) in enumerate(
            [
                (taps_hbm, taps),
                (skip_hbm, skip),
                (a_fwd_hbm, a_table),
                (t_hbm, t_both),
                (b_dft_hbm, b_table),
                (a_inv_hbm, a_back),
            ]
        )
    ]

    filt_load.wait()
    turned = filt[...].T.reshape(2, chips, CH, rows)
    h_send[...] = jnp.concatenate([turned[0], turned[1]], axis=1).astype(BF16)
    pl.semaphore_wait(barrier, 1 + chips - 1 + everyone - 1)

    x_copy = pltpu.make_async_remote_copy(
        src_ref=qkv_hbm.at[:, :, theirs],
        dst_ref=x_all.at[:, place, :],
        send_sem=near_send.at[1],
        recv_sem=near_recv.at[1],
        device_id={"core": other},
    )
    x_copy.start()

    after = lax.rem(me + 1, chips)

    def halo_copy(target):
        return pltpu.make_async_remote_copy(
            src_ref=qkv_hbm.at[:, pl.ds(rows - halo, halo), pl.ds(target * half, half)],
            dst_ref=x_all.at[:, pl.ds(0, halo), :],
            send_sem=near_send.at[2 + target],
            recv_sem=near_recv.at[2],
            device_id={"z": after // 2, "xh": lax.rem(after, 2), "core": target},
        )

    @pl.when(core == 1)
    def _():
        halo_copy(0).start()
        halo_copy(1).start()

    send_all(z, xh, h_send, h_recv, far_send.at[0], far_recv.at[0])

    swap = pltpu.make_async_remote_copy(
        src_ref=weight_hbm.at[pl.ds(pl.multiple_of((1 - xl) * columns, columns), columns), :],
        dst_ref=weight.at[z, xl],
        send_sem=near_send.at[4],
        recv_sem=near_recv.at[3],
        device_id={"xl": 1 - xl},
    )
    swap.start()
    right_steps = zs // 2
    left_steps = zs - 1 - right_steps

    def pass_on(block, lane, step, send_sem, recv_sem, ahead):
        half_block = weight.at[block, lax.rem(xl + lane, 2)]
        return pltpu.make_async_remote_copy(
            src_ref=half_block,
            dst_ref=half_block,
            send_sem=send_sem.at[lane, step],
            recv_sem=recv_sem.at[lane, step],
            device_id={"z": lax.rem(z + ahead, zs)},
        )

    def right_copy(lane, step):
        return pass_on(lax.rem(z + zs - step, zs), lane, step, right_send, right_recv, 1)

    def left_copy(lane, step):
        return pass_on(lax.rem(z + step, zs), lane, step, left_send, left_recv, zs - 1)

    def landing(lane, step, shift, sem):
        landed_at = weight.at[lax.rem(z + shift, zs), lax.rem(xl + lane, 2)]
        pltpu.make_async_copy(landed_at, landed_at, sem.at[lane, step]).wait()

    def ring(lane, step):
        if step > right_steps:
            return
        if step == 0 and lane == 0:
            weight_load.wait()
        if step == 0 and lane == 1:
            swap.wait_recv()
        if 0 < step <= right_steps:
            landing(lane, step - 1, zs - step, right_recv)
        if 0 < step <= left_steps:
            landing(lane, step - 1, step, left_recv)
        if step < right_steps:
            right_copy(lane, step).start()
        if step < left_steps:
            left_copy(lane, step).start()

    ring(0, 0)
    ring(1, 0)

    x_load.wait()
    small[0].wait()
    small[1].wait()
    x_copy.wait_recv()
    halo_copy(0).wait_recv()

    def feature(kind):
        raw = x_all[kind].astype(F32)
        first = jnp.where(me == 0, 0.0, raw[:halo])
        raw = jnp.concatenate([first, raw[halo:]], axis=0)
        total = taps[kind, 0:1, mine] * raw[halo:]
        for back in range(1, taps.shape[1]):
            shifted = raw[halo - back : halo - back + 2 * rows]
            total = total + taps[kind, back : back + 1, mine] * shifted
        return total

    mixed_in = feature(1) * feature(2)
    flipped = mixed_in.T.reshape(chips, CH, 2 * rows)
    u_send[...] = jnp.concatenate([flipped[:, :, :rows], flipped[:, :, rows:]], axis=1).astype(BF16)
    send_all(z, xh, u_send, u_recv, far_send.at[1], far_recv.at[1])
    ring(0, 1)
    query_t[...] = feature(0).T
    skip_t[...] = (skip[:, mine] * mixed_in).T

    for load in small[2:]:
        load.wait()
    a_fwd[...] = jnp.concatenate(high_low(a_table[...]), axis=1)
    high, low = high_low(b_table[...])
    b_dft[...] = jnp.concatenate([high, high, low], axis=0)
    high, low = high_low(a_back[...])
    a_inv[...] = jnp.concatenate([high, high, low], axis=1)
    ring(1, 1)
    for group in range(4):
        wait_group(h_recv, far_recv.at[0], group, 3)
    my_rows = pl.ds(pl.multiple_of(core * CH, CH), CH)
    their_rows = pl.ds(pl.multiple_of(other * CH, CH), CH)
    h_own[...] = h_recv[...].astype(F32)
    h_copy = pltpu.make_async_remote_copy(
        src_ref=h_own.at[:, their_rows, :],
        dst_ref=h_pair.at[:, my_rows, :],
        send_sem=near_send.at[0],
        recv_sem=near_recv.at[0],
        device_id={"core": other},
    )
    h_copy.start()
    h_pair[:, my_rows, :] = h_own[:, my_rows, :]
    h_copy.wait_recv()
    t_re, t_im = t_both[0], t_both[1]
    h_freq = spectrum(h_pair, scratch, a_fwd, t_re, t_im, b_dft)
    for group in range(4):
        wait_group(u_recv, far_recv.at[1], group, 3)
        if group == 0:
            ring(0, 2)
            ring(1, 2)
    u_freq = spectrum(u_recv, scratch, a_fwd, t_re, t_im, b_dft)
    width = t_re.shape[1]
    h_re, h_im = h_freq[:, :width], h_freq[:, width:]
    u_re, u_im = u_freq[:, :width], u_freq[:, width:]
    product = jnp.concatenate([h_re * u_im + h_im * u_re, h_re * u_re - h_im * u_im], axis=1)
    inverse(product, scratch, t_re, t_im, b_dft, a_inv)
    y_send[...] = scratch[...].reshape(y_send.shape).astype(BF16)
    send_all(z, xh, y_send, y_recv, far_send.at[2], far_recv.at[2], near_first=True)
    ring(0, 3)
    ring(1, 3)

    tokens = 2 * rows
    turns = zs // 4
    pairs = 2 * CH
    across = lax.rem(x + 2, 4)

    def g_copy(kind, group, which, device_id):
        part = g_all.at[which // 2, lax.rem(which, 2), core, pl.ds(group * turns, turns)]
        return pltpu.make_async_remote_copy(
            src_ref=part,
            dst_ref=part,
            send_sem=g_send.at[kind, group],
            recv_sem=g_recv.at[kind, group],
            device_id=device_id,
        )

    def g_copies(kind, which, device_id):
        return [g_copy(kind, group, which, device_id) for group in range(4)]

    to_across = g_copies(0, x, {"xh": 1 - xh})
    to_up = g_copies(1, x, up_x)
    to_down = g_copies(2, x, down_x)
    share = g_copies(3, x, {"core": other})
    share_across = g_copies(4, across, {"core": other})
    share_down = g_copies(5, down, {"core": other})
    share_up = g_copies(6, up, {"core": other})
    for group in range(4):
        wait_group(y_recv, far_recv.at[2], group, 0)
        for turn in range(group * turns, (group + 1) * turns):
            origin = lax.rem(z + zs - hops(turn), zs)
            source = pl.ds(pl.multiple_of(origin * pairs, pairs), pairs)
            back = y_recv[pl.ds(2 * turn, 2)].astype(F32)
            convolved = jnp.concatenate(
                [back[:, CH * b : CH * (b + 1), :].reshape(pairs, rows) for b in range(2)], axis=1
            )
            value = query_t[source, :] * (convolved + skip_t[source, :])
            g_all[pl.ds(xh, 1), pl.ds(xl, 1), pl.ds(core, 1), turn] = value.astype(BF16).reshape(
                1, 1, 1, pairs, tokens
            )
        to_across[group].start()
        to_up[group].start()
        to_down[group].start()
        share[group].start()
        if group in (0, 3):
            ring(0, 4 + group // 3)
            ring(1, 4 + group // 3)
    for group in range(4):
        to_up[group].wait_recv()
        share_down[group].start()
        to_down[group].wait_recv()
        share_up[group].start()
    ring(0, 6)
    ring(1, 6)
    for group in range(4):
        to_across[group].wait_recv()
        share_across[group].start()

    owners = 2 * ys
    owner_me = y * 2 + xl
    wide = per_owner * columns

    def order(far):
        which_x = 1 - xh if far else xh
        for part in range(2):
            for c in range(2):
                for block in range(zs):
                    shift = lax.rem(z + zs - block, zs)
                    shift = jnp.where(shift < zs // 2, shift, shift - zs)
                    turn = jnp.where(shift < 0, -2 * shift - 1, 2 * shift)
                    start = c * half + block * pairs
                    g_ordered[far, part, start : start + pairs, :] = g_all[
                        pl.ds(which_x, 1), part, c, pl.ds(turn, 1)
                    ].reshape(pairs, tokens)

    def send(which_x, b, to):
        pltpu.make_async_remote_copy(
            src_ref=parts.at[which_x, b, to],
            dst_ref=landed.at[x * 2 + core, y],
            send_sem=part_send,
            recv_sem=part_recv.at[x * 2 + core, y],
            device_id={"xh": which_x, "xl": lax.rem(to, 2), "core": b, "y": to // 2},
        ).start()

    def project(far, first, count):
        which_x = 1 - xh if far else xh
        targets = [
            lax.rem(z // per_owner + owners + first + lax.rem(y + k, count), owners)
            for k in range(count)
        ]
        product = jnp.zeros((count * wide, tokens), F32)
        for part in range(2):
            left = [
                weight[pl.ds(to * per_owner, per_owner), part].reshape(wide, 2 * half)
                for to in targets
            ]
            product = product + dot(jnp.concatenate(left, axis=0), g_ordered[far, part])
        for k, to in enumerate(targets):
            for b in range(2):
                value = product[k * wide : (k + 1) * wide, b * rows : (b + 1) * rows]
                parts[pl.ds(which_x, 1), b, pl.ds(to, 1)] = value.astype(BF16).reshape(
                    1, 1, wide, rows
                )
                if far:
                    send(which_x, b, to)
                    continue
                stays = (b == core) & (to == owner_me)

                @pl.when(jnp.logical_not(stays))
                def _():
                    send(which_x, b, to)

                @pl.when(stays)
                def _():
                    landed[pl.ds(x * 2 + core, 1), pl.ds(y, 1)] = parts[
                        pl.ds(which_x, 1), b, pl.ds(to, 1)
                    ].reshape(1, 1, wide, rows)

    near, nearer = min(7, owners), min(5, owners)
    for group in range(4):
        share[group].wait_recv()

        @pl.when(xl == 0)
        def _():
            share_up[group].wait_recv()

        @pl.when(xl == 1)
        def _():
            share_down[group].wait_recv()

    order(0)
    project(0, -(nearer // 2), nearer)
    ring(0, 7)
    ring(1, 7)
    for group in range(4):
        share_across[group].wait_recv()

        @pl.when(xl == 1)
        def _():
            share_up[group].wait_recv()

        @pl.when(xl == 0)
        def _():
            share_down[group].wait_recv()

    order(1)
    project(1, -(near // 2), near)
    for step in range(8, right_steps + 1):
        ring(0, step)
        ring(1, step)
    if near < owners:
        project(1, near - near // 2, owners - near)
    if nearer < owners:
        project(0, nearer - nearer // 2, owners - nearer)

    def arrived(k, carry):
        index = lax.rem(my_index + k, everyone)
        which, owner = index // ys, lax.rem(index, ys)
        block = landed.at[which, owner]
        pltpu.make_async_copy(block, block, part_recv.at[which, owner]).wait()
        return carry

    lax.fori_loop(1, everyone, arrived, 0)
    sums = []
    for which in range(8):
        total = landed[which, 0].astype(F32)
        for source in range(1, ys):
            total = total + landed[which, source].astype(F32)
        sums.append(total)
    order = [a * 4 + c * 2 + b for a in range(2) for b in range(2) for c in range(2)]
    pieces = [
        sums[which][part * columns : (part + 1) * columns]
        for part in range(per_owner)
        for which in order
    ]
    out[...] = jnp.concatenate(pieces, axis=0).T.astype(out.dtype)

    h_copy.wait_send()
    x_copy.wait_send()

    @pl.when(core == 1)
    def _():
        halo_copy(0).wait_send()
        halo_copy(1).wait_send()

    swap.wait_send()
    for step in range(right_steps):
        for lane in range(2):
            right_copy(lane, step).wait_send()
    for step in range(left_steps):
        for lane in range(2):
            left_copy(lane, step).wait_send()
    wait_blocks(chips - 1, h_send, far_send.at[0])
    wait_blocks(chips - 1, u_send, far_send.at[1])
    wait_blocks(chips - 1, y_send, far_send.at[2])
    for group in (to_across, to_up, to_down, share, share_across, share_down, share_up):
        for copy in group:
            copy.wait_send()
    pltpu.make_async_copy(parts.at[1], parts.at[1], part_send).wait()
    pltpu.make_async_copy(parts.at[0, 1], parts.at[0, 1], part_send).wait()
    sent = parts.at[0, 0, pl.ds(1, owners - 1)]
    pltpu.make_async_copy(sent, sent, part_send).wait()


def body(qkv_in, short_taps, long_filter, skip_gain, out_weight):
    rows, _, channels = qkv_in.shape
    half = channels // 2
    zs = lax.axis_size("z")
    chips = zs * 2
    ys = lax.axis_size("y")
    blocks = 2 * chips
    columns = out_weight.shape[1] // 2
    wide = zs // (2 * ys) * columns
    lookup = tables(blocks, rows)
    exchange = (chips, 2 * CH, rows)
    dma = pltpu.SemaphoreType.DMA
    return pl.pallas_call(
        mixer_kernel,
        out_shape=jax.ShapeDtypeStruct((rows, channels), BF16),
        in_specs=[pl.BlockSpec(memory_space=pl.ANY)] * 9,
        out_specs=VMEM,
        scratch_shapes=[
            pltpu.VMEM(short_taps.shape, F32),
            pltpu.VMEM((rows, channels), F32),
            pltpu.VMEM((1, channels), F32),
            *[pltpu.VMEM(table.shape, table.dtype) for table in lookup],
            pltpu.VMEM((2 * blocks, 2 * blocks), BF16),
            pltpu.VMEM((6 * rows, 2 * rows), BF16),
            pltpu.VMEM((blocks, 6 * blocks), BF16),
            pltpu.VMEM(exchange, F32),
            pltpu.VMEM(exchange, F32),
            pltpu.VMEM(exchange, BF16),
            pltpu.VMEM(exchange, BF16),
            pltpu.VMEM((3, 16 + 2 * rows, half), BF16),
            pltpu.VMEM(exchange, BF16),
            pltpu.VMEM(exchange, BF16),
            pltpu.VMEM(exchange, BF16),
            pltpu.VMEM(exchange, BF16),
            pltpu.VMEM((blocks * CH, rows), F32),
            pltpu.VMEM((zs, 2, columns, channels), BF16),
            pltpu.VMEM((half, 2 * rows), F32),
            pltpu.VMEM((half, 2 * rows), F32),
            pltpu.VMEM((2, 2, 2, zs, 2 * CH, 2 * rows), BF16),
            pltpu.VMEM((2, 2, channels, 2 * rows), BF16),
            pltpu.VMEM((2, 2, 2 * ys, wide, rows), BF16),
            pltpu.VMEM((8, ys, wide, rows), BF16),
            dma((9,)),
            dma((5,)),
            dma((4,)),
            dma((3,)),
            dma((3, 4)),
            dma((2, zs)),
            dma((2, zs)),
            dma((2, zs)),
            dma((2, zs)),
            dma((7, 4)),
            dma((7, 4)),
            dma,
            dma((8, ys)),
        ],
        compiler_params=pltpu.CompilerParams(
            collective_id=0, has_side_effects=True, vmem_limit_bytes=60 * 2**20
        ),
        name="mixer",
    )(
        qkv_in.transpose(1, 0, 2),
        short_taps,
        long_filter,
        skip_gain[None, :],
        out_weight.T,
        *lookup,
    )


def solution(mesh):
    sizes = dict(mesh.shape)
    split = Mesh(
        mesh.devices.reshape(sizes["ctx"] // 4, 2, 2, sizes["tp"] // 2, 2),
        ("z", "xh", "core", "y", "xl"),
    )
    ctx, tp = ("z", "xh", "core"), ("y", "xl")
    return jax.shard_map(
        body,
        mesh=split,
        in_specs=(P(ctx, None, tp), P(None, None, tp), P(ctx, tp), P(tp), P(tp, ctx)),
        out_specs=P(ctx, tp),
        check_vma=False,
    )
```

```python
import jax
import jax.numpy as jnp
import numpy as np
from jax import lax
from jax.experimental import pallas as pl
from jax.experimental.pallas import tpu as pltpu
from jax.sharding import Mesh, PartitionSpec as P

F32 = jnp.float32
BF16 = jnp.bfloat16
CH = 8
VMEM = pl.BlockSpec(memory_space=pltpu.VMEM)


def tables(blocks, width):
    length = blocks * width
    f1 = np.arange(blocks)[:, None]
    a = np.exp(-2j * np.pi * ((np.arange(blocks)[None, :] * (4 * f1 + 1)) % (4 * blocks)) / (4 * blocks))
    t = np.exp(-2j * np.pi * (np.arange(width)[None, :] * (4 * f1 + 1)) / (4 * length))
    i = np.arange(width)
    b = np.exp(-2j * np.pi * ((i[:, None] * i[None, :]) % width) / width)
    found = (
        np.concatenate([a.real, a.imag], 0),
        np.stack([t.real, t.imag]),
        np.block([[b.real, b.imag], [-b.imag, b.real]]),
        np.concatenate([a.real.T, a.imag.T], 1) / length,
    )
    return [jnp.asarray(table.astype(np.float32)) for table in found]


def dot(left, right):
    return jnp.dot(left, right, preferred_element_type=F32)


def high_low(value):
    high = value.astype(BF16)
    return high, (value - high.astype(F32)).astype(BF16)


def hops(turn):
    if isinstance(turn, int):
        return -((turn + 1) // 2) if turn % 2 else turn // 2
    return jnp.where(lax.rem(turn, 2) == 1, -((turn + 1) // 2), turn // 2)


def send_all(z, xh, source, target, send_sem, recv_sems, near_first=False):
    zs = lax.axis_size("z")
    me = z * 2 + xh
    size = 2 * zs // recv_sems.shape[0]

    def step(k, carry):
        turn = k // 2
        ahead = hops(turn) + (zs if near_first else zs // 2)
        to_z = lax.rem(z + ahead, zs)
        to_x = jnp.where(lax.rem(k, 2) == 0, 1 - xh, xh)
        pltpu.make_async_remote_copy(
            src_ref=source.at[to_z * 2 + to_x],
            dst_ref=target.at[turn * 2 + xh if near_first else me],
            send_sem=send_sem,
            recv_sem=recv_sems.at[k // size],
            device_id={"z": to_z, "xh": to_x},
        ).start()
        return carry

    if near_first:
        lax.fori_loop(2 * zs - size, 2 * zs, step, 0)
        step(0, 0)
        lax.fori_loop(2, 2 * zs - size, step, 0)
    else:
        lax.fori_loop(0, 2 * zs - 1, step, 0)
    slot = xh if near_first else me
    target[pl.ds(slot, 1)] = source[pl.ds(me, 1)]


def wait_blocks(count, ref, sem):
    part = ref.at[pl.ds(0, count)]
    pltpu.make_async_copy(part, part, sem).wait()


def wait_group(ref, sems, group, short):
    size = ref.shape[0] // sems.shape[0]
    wait_blocks(size - (group == short), ref, sems.at[group])


def spectrum(received, scratch, a_fwd, t_re, t_im, b_dft):
    rows = scratch.shape[0]
    blocks = rows // CH
    scratch[...] = received[...].astype(F32).reshape(rows, -1)
    columns = [scratch[pl.ds(c, blocks, stride=CH), :].astype(BF16) for c in range(CH)]
    signal = jnp.concatenate(columns, axis=1)
    mixed = dot(a_fwd[...], jnp.concatenate([signal, signal], axis=0))
    width = t_re.shape[1]
    parts = []
    for c in range(CH):
        re = mixed[:blocks, c * width : (c + 1) * width]
        im = mixed[blocks:, c * width : (c + 1) * width]
        parts.append(
            jnp.concatenate(
                [re * t_re - im * t_im, re * t_im + im * t_re], axis=1
            )
        )
    high, low = high_low(jnp.concatenate(parts, axis=0))
    return dot(jnp.concatenate([high, low, high], axis=1), b_dft[...])


def inverse(product, scratch, t_re, t_im, b_dft, a_inv):
    blocks, width = t_re.shape
    high, low = high_low(product)
    back = dot(jnp.concatenate([high, low, high], axis=1), b_dft[...])
    parts = []
    for c in range(CH):
        im = back[c * blocks : (c + 1) * blocks, :width]
        re = back[c * blocks : (c + 1) * blocks, width:]
        parts.append(
            jnp.concatenate(
                [re * t_re + im * t_im, im * t_re - re * t_im], axis=0
            )
        )
    high, low = high_low(jnp.concatenate(parts, axis=1))
    result = dot(a_inv[...], jnp.concatenate([high, low, high], axis=0))
    for c in range(CH):
        scratch[pl.ds(c, blocks, stride=CH), :] = result[:, c * width : (c + 1) * width]


def local_copy(source, target, sem):
    copy = pltpu.make_async_copy(source, target, sem)
    copy.start()
    return copy


def mixer_kernel(
    qkv_hbm, taps_hbm, filt_hbm, skip_hbm, weight_hbm,
    a_fwd_hbm, t_hbm, b_dft_hbm, a_inv_hbm,
    out,
    taps, filt, skip, a_table, t_both, b_table, a_back, a_fwd, b_dft, a_inv,
    h_own, h_pair, h_send, h_recv, x_all, u_send, u_recv, y_send, y_recv, scratch,
    weight, query_t, skip_t, g_all, g_ordered, parts, landed,
    load_sem, near_send, near_recv, far_send, far_recv,
    right_send, right_recv, left_send, left_recv, g_send, g_recv, part_send, part_recv,
):
    z, xh, core = lax.axis_index("z"), lax.axis_index("xh"), lax.axis_index("core")
    y, xl = lax.axis_index("y"), lax.axis_index("xl")
    zs, ys = lax.axis_size("z"), lax.axis_size("y")
    chips = zs * 2
    per_owner = zs // (2 * ys)
    me = z * 2 + xh
    other = 1 - core
    rows = qkv_hbm.shape[1]
    half = chips * CH
    halo = 16
    mine = pl.ds(pl.multiple_of(core * half, half), half)
    theirs = pl.ds(pl.multiple_of(other * half, half), half)
    place = pl.ds(pl.multiple_of(halo + core * rows, 16), rows)
    x = xh * 2 + xl
    everyone = 8 * ys
    my_index = (x * 2 + core) * ys + y
    up, down = lax.rem(x + 1, 4), lax.rem(x + 3, 4)
    up_x = {"xh": up // 2, "xl": lax.rem(up, 2)}
    down_x = {"xh": down // 2, "xl": lax.rem(down, 2)}
    columns = weight.shape[2]

    barrier = pltpu.get_barrier_semaphore()
    step_to = lax.rem(me + jnp.where(core == 1, 1, chips - 1), chips)
    pl.semaphore_signal(
        barrier, inc=1, device_id={"z": step_to // 2, "xh": lax.rem(step_to, 2), "core": other}
    )


    def place_of(index):
        which = index // ys
        return {
            "xh": which // 4,
            "xl": lax.rem(which // 2, 2),
            "core": lax.rem(which, 2),
            "y": lax.rem(index, ys),
        }

    def greet_ctx(k, carry):
        peer = lax.rem(me + k, chips)
        pl.semaphore_signal(
            barrier, inc=1, device_id={"z": peer // 2, "xh": lax.rem(peer, 2)}
        )
        return carry

    def greet_plane(k, carry):
        pl.semaphore_signal(barrier, inc=1, device_id=place_of(lax.rem(my_index + k, everyone)))
        return carry

    lax.fori_loop(1, chips, greet_ctx, 0)
    lax.fori_loop(1, everyone, greet_plane, 0)

    filt_load = local_copy(filt_hbm, filt, load_sem.at[0])
    x_load = local_copy(qkv_hbm.at[:, :, mine], x_all.at[:, place, :], load_sem.at[1])
    weight_load = local_copy(
        weight_hbm.at[pl.ds(pl.multiple_of(xl * columns, columns), columns), :],
        weight.at[z, xl],
        load_sem.at[2],
    )
    small = [
        local_copy(source, target, load_sem.at[3 + k])
        for k, (source, target) in enumerate(
            [
                (taps_hbm, taps),
                (skip_hbm, skip),
                (a_fwd_hbm, a_table),
                (t_hbm, t_both),
                (b_dft_hbm, b_table),
                (a_inv_hbm, a_back),
            ]
        )
    ]

    filt_load.wait()
    turned = filt[...].T.reshape(2, chips, CH, rows)
    h_send[...] = jnp.concatenate([turned[0], turned[1]], axis=1).astype(BF16)
    pl.semaphore_wait(barrier, 1 + chips - 1 + everyone - 1)

    x_copy = pltpu.make_async_remote_copy(
        src_ref=qkv_hbm.at[:, :, theirs],
        dst_ref=x_all.at[:, place, :],
        send_sem=near_send.at[1],
        recv_sem=near_recv.at[1],
        device_id={"core": other},
    )
    x_copy.start()

    after = lax.rem(me + 1, chips)

    def halo_copy(target):
        return pltpu.make_async_remote_copy(
            src_ref=qkv_hbm.at[:, pl.ds(rows - halo, halo), pl.ds(target * half, half)],
            dst_ref=x_all.at[:, pl.ds(0, halo), :],
            send_sem=near_send.at[2 + target],
            recv_sem=near_recv.at[2],
            device_id={"z": after // 2, "xh": lax.rem(after, 2), "core": target},
        )

    @pl.when(core == 1)
    def _():
        halo_copy(0).start()
        halo_copy(1).start()

    send_all(z, xh, h_send, h_recv, far_send.at[0], far_recv.at[0])

    swap = pltpu.make_async_remote_copy(
        src_ref=weight_hbm.at[pl.ds(pl.multiple_of((1 - xl) * columns, columns), columns), :],
        dst_ref=weight.at[z, xl],
        send_sem=near_send.at[4],
        recv_sem=near_recv.at[3],
        device_id={"xl": 1 - xl},
    )
    swap.start()
    right_steps = zs // 2
    left_steps = zs - 1 - right_steps

    def pass_on(block, lane, step, send_sem, recv_sem, ahead):
        half_block = weight.at[block, lax.rem(xl + lane, 2)]
        return pltpu.make_async_remote_copy(
            src_ref=half_block,
            dst_ref=half_block,
            send_sem=send_sem.at[lane, step],
            recv_sem=recv_sem.at[lane, step],
            device_id={"z": lax.rem(z + ahead, zs)},
        )

    def right_copy(lane, step):
        return pass_on(lax.rem(z + zs - step, zs), lane, step, right_send, right_recv, 1)

    def left_copy(lane, step):
        return pass_on(lax.rem(z + step, zs), lane, step, left_send, left_recv, zs - 1)

    def landing(lane, step, shift, sem):
        landed_at = weight.at[lax.rem(z + shift, zs), lax.rem(xl + lane, 2)]
        pltpu.make_async_copy(landed_at, landed_at, sem.at[lane, step]).wait()

    def ring(lane, step):
        if step > right_steps:
            return
        if step == 0 and lane == 0:
            weight_load.wait()
        if step == 0 and lane == 1:
            swap.wait_recv()
        if 0 < step <= right_steps:
            landing(lane, step - 1, zs - step, right_recv)
        if 0 < step <= left_steps:
            landing(lane, step - 1, step, left_recv)
        if step < right_steps:
            right_copy(lane, step).start()
        if step < left_steps:
            left_copy(lane, step).start()

    ring(0, 0)
    ring(1, 0)

    x_load.wait()
    small[0].wait()
    small[1].wait()
    x_copy.wait_recv()
    halo_copy(0).wait_recv()

    def feature(kind):
        raw = x_all[kind].astype(F32)
        first = jnp.where(me == 0, 0.0, raw[:halo])
        raw = jnp.concatenate([first, raw[halo:]], axis=0)
        total = taps[kind, 0:1, mine] * raw[halo:]
        for back in range(1, taps.shape[1]):
            shifted = raw[halo - back : halo - back + 2 * rows]
            total = total + taps[kind, back : back + 1, mine] * shifted
        return total

    mixed_in = feature(1) * feature(2)
    flipped = mixed_in.T.reshape(chips, CH, 2 * rows)
    u_send[...] = jnp.concatenate([flipped[:, :, :rows], flipped[:, :, rows:]], axis=1).astype(BF16)
    send_all(z, xh, u_send, u_recv, far_send.at[1], far_recv.at[1])
    ring(0, 1)
    query_t[...] = feature(0).T
    skip_t[...] = (skip[:, mine] * mixed_in).T

    for load in small[2:]:
        load.wait()
    a_fwd[...] = jnp.concatenate(high_low(a_table[...]), axis=1)
    high, low = high_low(b_table[...])
    b_dft[...] = jnp.concatenate([high, high, low], axis=0)
    high, low = high_low(a_back[...])
    a_inv[...] = jnp.concatenate([high, high, low], axis=1)
    ring(1, 1)
    for group in range(4):
        wait_group(h_recv, far_recv.at[0], group, 3)
    my_rows = pl.ds(pl.multiple_of(core * CH, CH), CH)
    their_rows = pl.ds(pl.multiple_of(other * CH, CH), CH)
    h_own[...] = h_recv[...].astype(F32)
    h_copy = pltpu.make_async_remote_copy(
        src_ref=h_own.at[:, their_rows, :],
        dst_ref=h_pair.at[:, my_rows, :],
        send_sem=near_send.at[0],
        recv_sem=near_recv.at[0],
        device_id={"core": other},
    )
    h_copy.start()
    h_pair[:, my_rows, :] = h_own[:, my_rows, :]
    h_copy.wait_recv()
    t_re, t_im = t_both[0], t_both[1]
    h_freq = spectrum(h_pair, scratch, a_fwd, t_re, t_im, b_dft)
    for group in range(4):
        wait_group(u_recv, far_recv.at[1], group, 3)
        if group == 0:
            ring(0, 2)
            ring(1, 2)
    u_freq = spectrum(u_recv, scratch, a_fwd, t_re, t_im, b_dft)
    width = t_re.shape[1]
    h_re, h_im = h_freq[:, :width], h_freq[:, width:]
    u_re, u_im = u_freq[:, :width], u_freq[:, width:]
    product = jnp.concatenate([h_re * u_im + h_im * u_re, h_re * u_re - h_im * u_im], axis=1)
    inverse(product, scratch, t_re, t_im, b_dft, a_inv)
    y_send[...] = scratch[...].reshape(y_send.shape).astype(BF16)
    send_all(z, xh, y_send, y_recv, far_send.at[2], far_recv.at[2], near_first=True)
    ring(0, 3)
    ring(1, 3)

    tokens = 2 * rows
    turns = zs // 4
    pairs = 2 * CH
    across = lax.rem(x + 2, 4)

    def g_copy(kind, group, which, device_id):
        part = g_all.at[which // 2, lax.rem(which, 2), core, pl.ds(group * turns, turns)]
        return pltpu.make_async_remote_copy(
            src_ref=part,
            dst_ref=part,
            send_sem=g_send.at[kind, group],
            recv_sem=g_recv.at[kind, group],
            device_id=device_id,
        )

    def g_copies(kind, which, device_id):
        return [g_copy(kind, group, which, device_id) for group in range(4)]

    to_across = g_copies(0, x, {"xh": 1 - xh})
    to_up = g_copies(1, x, up_x)
    to_down = g_copies(2, x, down_x)
    share = g_copies(3, x, {"core": other})
    share_across = g_copies(4, across, {"core": other})
    share_down = g_copies(5, down, {"core": other})
    share_up = g_copies(6, up, {"core": other})
    for group in range(4):
        wait_group(y_recv, far_recv.at[2], group, 0)
        for turn in range(group * turns, (group + 1) * turns):
            origin = lax.rem(z + zs - hops(turn), zs)
            source = pl.ds(pl.multiple_of(origin * pairs, pairs), pairs)
            back = y_recv[pl.ds(2 * turn, 2)].astype(F32)
            convolved = jnp.concatenate(
                [back[:, CH * b : CH * (b + 1), :].reshape(pairs, rows) for b in range(2)], axis=1
            )
            value = query_t[source, :] * (convolved + skip_t[source, :])
            g_all[pl.ds(xh, 1), pl.ds(xl, 1), pl.ds(core, 1), turn] = value.astype(BF16).reshape(
                1, 1, 1, pairs, tokens
            )
        to_across[group].start()
        to_up[group].start()
        to_down[group].start()
        share[group].start()
        if group in (0, 3):
            ring(0, 4 + group // 3)
            ring(1, 4 + group // 3)
    for group in range(4):
        to_up[group].wait_recv()
        share_down[group].start()
        to_down[group].wait_recv()
        share_up[group].start()
    ring(0, 6)
    ring(1, 6)
    for group in range(4):
        to_across[group].wait_recv()
        share_across[group].start()

    owners = 2 * ys
    owner_me = y * 2 + xl
    wide = per_owner * columns

    def order(far, part):
        which_x = 1 - xh if far else xh
        for c in range(2):
            for block in range(zs):
                shift = lax.rem(z + zs - block, zs)
                shift = jnp.where(shift < zs // 2, shift, shift - zs)
                turn = jnp.where(shift < 0, -2 * shift - 1, 2 * shift)
                start = c * half + block * pairs
                g_ordered[far, pl.ds(part, 1), start : start + pairs, :] = g_all[
                    pl.ds(which_x, 1), pl.ds(part, 1), c, pl.ds(turn, 1)
                ].reshape(1, pairs, tokens)

    def send(which_x, b, to):
        pltpu.make_async_remote_copy(
            src_ref=parts.at[which_x, b, to],
            dst_ref=landed.at[x * 2 + core, y],
            send_sem=part_send,
            recv_sem=part_recv.at[x * 2 + core, y],
            device_id={"xh": which_x, "xl": lax.rem(to, 2), "core": b, "y": to // 2},
        ).start()

    def project(far, first, count):
        which_x = 1 - xh if far else xh
        targets = [
            lax.rem(z // per_owner + owners + first + lax.rem(y + k, count), owners)
            for k in range(count)
        ]
        product = jnp.zeros((count * wide, tokens), F32)
        for part in range(2):
            left = [
                weight[pl.ds(to * per_owner, per_owner), part].reshape(wide, 2 * half)
                for to in targets
            ]
            product = product + dot(jnp.concatenate(left, axis=0), g_ordered[far, part])
        for k, to in enumerate(targets):
            for b in range(2):
                value = product[k * wide : (k + 1) * wide, b * rows : (b + 1) * rows]
                parts[pl.ds(which_x, 1), b, pl.ds(to, 1)] = value.astype(BF16).reshape(
                    1, 1, wide, rows
                )
                if far:
                    send(which_x, b, to)
                    continue
                stays = (b == core) & (to == owner_me)

                @pl.when(jnp.logical_not(stays))
                def _():
                    send(which_x, b, to)

                @pl.when(stays)
                def _():
                    landed[pl.ds(x * 2 + core, 1), pl.ds(y, 1)] = parts[
                        pl.ds(which_x, 1), b, pl.ds(to, 1)
                    ].reshape(1, 1, wide, rows)

    near, nearer = min(7, owners), min(5, owners)
    for group in range(4):
        share[group].wait_recv()
    order(0, xl)
    for group in range(4):

        @pl.when(xl == 0)
        def _():
            share_up[group].wait_recv()

        @pl.when(xl == 1)
        def _():
            share_down[group].wait_recv()

    order(0, 1 - xl)
    project(0, -(nearer // 2), nearer)
    ring(0, 7)
    ring(1, 7)
    for group in range(4):
        @pl.when(xl == 1)
        def _():
            share_up[group].wait_recv()

        @pl.when(xl == 0)
        def _():
            share_down[group].wait_recv()

    order(1, 1 - xl)
    for group in range(4):
        share_across[group].wait_recv()
    order(1, xl)
    project(1, -(near // 2), near)
    for step in range(8, right_steps + 1):
        ring(0, step)
        ring(1, step)
    if near < owners:
        project(1, near - near // 2, owners - near)
    if nearer < owners:
        project(0, nearer - nearer // 2, owners - nearer)

    def arrived(k, carry):
        index = lax.rem(my_index + k, everyone)
        which, owner = index // ys, lax.rem(index, ys)
        block = landed.at[which, owner]
        pltpu.make_async_copy(block, block, part_recv.at[which, owner]).wait()
        return carry

    lax.fori_loop(1, everyone, arrived, 0)
    sums = []
    for which in range(8):
        total = landed[which, 0].astype(F32)
        for source in range(1, ys):
            total = total + landed[which, source].astype(F32)
        sums.append(total)
    order = [a * 4 + c * 2 + b for a in range(2) for b in range(2) for c in range(2)]
    pieces = [
        sums[which][part * columns : (part + 1) * columns]
        for part in range(per_owner)
        for which in order
    ]
    out[...] = jnp.concatenate(pieces, axis=0).T.astype(out.dtype)

    h_copy.wait_send()
    x_copy.wait_send()

    @pl.when(core == 1)
    def _():
        halo_copy(0).wait_send()
        halo_copy(1).wait_send()

    swap.wait_send()
    for step in range(right_steps):
        for lane in range(2):
            right_copy(lane, step).wait_send()
    for step in range(left_steps):
        for lane in range(2):
            left_copy(lane, step).wait_send()
    wait_blocks(chips - 1, h_send, far_send.at[0])
    wait_blocks(chips - 1, u_send, far_send.at[1])
    wait_blocks(chips - 1, y_send, far_send.at[2])
    for group in (to_across, to_up, to_down, share, share_across, share_down, share_up):
        for copy in group:
            copy.wait_send()
    pltpu.make_async_copy(parts.at[1], parts.at[1], part_send).wait()
    pltpu.make_async_copy(parts.at[0, 1], parts.at[0, 1], part_send).wait()
    sent = parts.at[0, 0, pl.ds(1, owners - 1)]
    pltpu.make_async_copy(sent, sent, part_send).wait()


def body(qkv_in, short_taps, long_filter, skip_gain, out_weight):
    rows, _, channels = qkv_in.shape
    half = channels // 2
    zs = lax.axis_size("z")
    chips = zs * 2
    ys = lax.axis_size("y")
    blocks = 2 * chips
    columns = out_weight.shape[1] // 2
    wide = zs // (2 * ys) * columns
    lookup = tables(blocks, rows)
    exchange = (chips, 2 * CH, rows)
    dma = pltpu.SemaphoreType.DMA
    return pl.pallas_call(
        mixer_kernel,
        out_shape=jax.ShapeDtypeStruct((rows, channels), BF16),
        in_specs=[pl.BlockSpec(memory_space=pl.ANY)] * 9,
        out_specs=VMEM,
        scratch_shapes=[
            pltpu.VMEM(short_taps.shape, F32),
            pltpu.VMEM((rows, channels), F32),
            pltpu.VMEM((1, channels), F32),
            *[pltpu.VMEM(table.shape, table.dtype) for table in lookup],
            pltpu.VMEM((2 * blocks, 2 * blocks), BF16),
            pltpu.VMEM((6 * rows, 2 * rows), BF16),
            pltpu.VMEM((blocks, 6 * blocks), BF16),
            pltpu.VMEM(exchange, F32),
            pltpu.VMEM(exchange, F32),
            pltpu.VMEM(exchange, BF16),
            pltpu.VMEM(exchange, BF16),
            pltpu.VMEM((3, 16 + 2 * rows, half), BF16),
            pltpu.VMEM(exchange, BF16),
            pltpu.VMEM(exchange, BF16),
            pltpu.VMEM(exchange, BF16),
            pltpu.VMEM(exchange, BF16),
            pltpu.VMEM((blocks * CH, rows), F32),
            pltpu.VMEM((zs, 2, columns, channels), BF16),
            pltpu.VMEM((half, 2 * rows), F32),
            pltpu.VMEM((half, 2 * rows), F32),
            pltpu.VMEM((2, 2, 2, zs, 2 * CH, 2 * rows), BF16),
            pltpu.VMEM((2, 2, channels, 2 * rows), BF16),
            pltpu.VMEM((2, 2, 2 * ys, wide, rows), BF16),
            pltpu.VMEM((8, ys, wide, rows), BF16),
            dma((9,)),
            dma((5,)),
            dma((4,)),
            dma((3,)),
            dma((3, 4)),
            dma((2, zs)),
            dma((2, zs)),
            dma((2, zs)),
            dma((2, zs)),
            dma((7, 4)),
            dma((7, 4)),
            dma,
            dma((8, ys)),
        ],
        compiler_params=pltpu.CompilerParams(
            collective_id=0, has_side_effects=True, vmem_limit_bytes=60 * 2**20
        ),
        name="mixer",
    )(
        qkv_in.transpose(1, 0, 2),
        short_taps,
        long_filter,
        skip_gain[None, :],
        out_weight.T,
        *lookup,
    )


def solution(mesh):
    sizes = dict(mesh.shape)
    split = Mesh(
        mesh.devices.reshape(sizes["ctx"] // 4, 2, 2, sizes["tp"] // 2, 2),
        ("z", "xh", "core", "y", "xl"),
    )
    ctx, tp = ("z", "xh", "core"), ("y", "xl")
    return jax.shard_map(
        body,
        mesh=split,
        in_specs=(P(ctx, None, tp), P(None, None, tp), P(ctx, tp), P(tp), P(tp, ctx)),
        out_specs=P(ctx, tp),
        check_vma=False,
    )
```
